32 devices in a mesh: groups: 2 (over x), dp: 8 (over z, y), ep: 2 (over core).
Axes of the slice: x: 2, y: 2, z: 4, core: 2. Of those that a mesh axis runs over, the one named last changes fastest.
Arguments:
- queries: bfloat16 [2048, 8192], P(('groups', 'dp'), 'ep'), parts along dimension 0, may hold values from -6 to 6
- key_weight: bfloat16 [64, 128, 512], P('ep'), may hold values from -0.25 to 0.25
- value_weight: bfloat16 [64, 512, 128], P('ep'), may hold values from -3 to 3
- prefix_latent: bfloat16 [16384, 512], P(('groups', 'dp')), parts along dimension 0
- fresh_latent: bfloat16 [2048, 512], P(('groups', 'dp')), parts along dimension 0
- span_counts: int32 [16], P(('groups', 'dp')), parts along dimension 0, may hold values from 1 to 2, as said below
- prefix_lengths: int32 [16], P(('groups', 'dp')), parts along dimension 0, may hold values from 0 to 1024, as said below
- routes: int32 [2048, 2], P(('groups', 'dp')), parts along dimension 0, may hold values from 0 to 15, all different within a row; in each aligned block of 128 rows (0 to 127, 128 to 255, ...) at most 16 rows name the same one
Outputs:
- expert_inputs: bfloat16 [32, 8, 16, 8192], P(('groups', 'dp', 'ep')), parts along dimension 0
The draws below stay inside these ranges and needn't reach their ends.
There are 2 independent parts, one for each index of `groups`. The reference program is written for one: setup_inputs(seed, part) draws one part's arguments, and reference() takes and returns one part's arrays. A program takes and returns all parts, laid end to end along the dimension named above; an argument that names none is the same for every part. Nothing has to cross between parts.
Inputs may be any that keep to these rules, and one draw needn't show every extreme that they name: `span_counts`: some prompt has 2 spans. `prefix_lengths`: some prompt has 1024 cached rows. `routes`: among each prompt's 128 slots every expert is named exactly 16 times; a slot names 2 different experts.
All inputs are finite; a program needn't handle non-finite values.
Results may differ from the reference program's by a relative error of at most 0.012.
Values may be sent and summed in bfloat16 or wider, within the bound.
No kernel may reach another device: no remote copies, remote signals or barrier semaphores. Data moves between devices by JAX's collectives and lax.ppermute only.
A program may use at most 64 MiB of HBM per device.

```python
import math
import jax
import jax.numpy as jnp
import numpy as np
from jax import lax

HEADS = 64
HEAD_DIM = 128
LATENT = 512
SPAN = 64
MAXC = 2
PMAX = 1024
TOPK = 2
TOK = 128
RANKS = 8
EXPERTS = 16
MOST = 16


def latent_rows(key, rows):
    first = jax.random.fold_in(key, 0)
    shape = (RANKS * rows, LATENT)
    values = jnp.clip(jax.random.normal(first, shape, jnp.float32), -6.0, 6.0)
    return values.astype(jnp.bfloat16)


def draw_prefix_latent(key, part):
    key = jax.random.fold_in(key, 11)
    return latent_rows(key, PMAX)


def draw_fresh_latent(key, part):
    key = jax.random.fold_in(key, 12)
    return latent_rows(key, TOK)


def draw_span_counts(key, part):
    key = jax.random.fold_in(key, 21)
    first, second = jax.random.split(key)
    values = jax.random.randint(first, (RANKS,), 1, MAXC + 1, dtype=jnp.int32)
    chosen = jax.random.randint(second, (), 0, RANKS, dtype=jnp.int32)
    return jnp.where(jnp.arange(RANKS, dtype=jnp.int32) == chosen, jnp.int32(MAXC), values)


def draw_prefix_lengths(key, part):
    key = jax.random.fold_in(key, 22)
    first, second, third = jax.random.split(key, 3)
    left = jax.random.randint(first, (RANKS,), 0, PMAX + 1, dtype=jnp.int32)
    right = jax.random.randint(second, (RANKS,), 0, PMAX + 1, dtype=jnp.int32)
    values = left * right // PMAX
    chosen = jax.random.randint(third, (), 0, RANKS, dtype=jnp.int32)
    return jnp.where(jnp.arange(RANKS, dtype=jnp.int32) == chosen, jnp.int32(PMAX), values)


def block_scale(own_key, extent, shards, smallest, largest):
    def one(position, parts):
        heights = jax.random.uniform(jax.random.fold_in(jax.random.fold_in(own_key, 6), position), (parts,), jnp.float32, smallest / len(shards), largest / len(shards))
        return jnp.repeat(jnp.exp(heights), extent[position] // parts).reshape((-1,) + (1,) * (len(extent) - position - 1))

    loudness = one(*shards[0])
    for cut in shards[1:]:
        loudness = loudness * one(*cut)
    return loudness


def assign_block(rng, own, number, rows, amount, top, limit, skew):
    sequence = jax.random.permutation(rng, amount)
    crowded, common = load_shares(amount, rows * top, limit, skew, True), load_shares(amount, rows * top, limit, skew, False)
    places = jnp.arange(amount)

    def named(lengths, turn):
        used = int((lengths > 0).sum())
        fixed = max(1, used // 4)
        shifted = fixed + (places - fixed + turn * (used - fixed)) % max(1, amount - fixed)
        return jnp.zeros((amount,), jnp.int32).at[sequence[jnp.where(places < fixed, places, shifted)]].set(jnp.asarray(lengths, jnp.int32))

    lengths = jnp.where(number % 4 == 0, named(crowded, number // 4), named(common, number - number // 4 - 1))
    mixed = jax.random.permutation(jax.random.fold_in(own, 3), amount)
    giver, taker = mixed[0:amount // 2 * 2:2], mixed[1:amount // 2 * 2:2]
    room = jnp.minimum(lengths[giver] - 1, limit - lengths[taker]) // 2
    room = jnp.where((giver == sequence[0]) | (taker == sequence[0]) | (lengths[taker] == 0), 0, jnp.maximum(room, 0))
    shifted = jax.random.randint(jax.random.fold_in(own, 4), (amount // 2,), 0, 1 << 20) % (room + 1)
    lengths = lengths.at[giver].add(-shifted).at[taker].add(shifted)
    labels = jnp.searchsorted(jnp.cumsum(lengths), jnp.arange(rows * top), side="right").astype(jnp.int32)
    table = labels.reshape(top, rows).T
    table = table[jax.random.permutation(jax.random.fold_in(own, 1), rows)]
    turn = jax.random.randint(jax.random.fold_in(own, 2), (rows, 1), 0, top)
    return jnp.take_along_axis(table, (jnp.arange(top)[None, :] + turn) % top, axis=1)


def load_shares(amount, total, most, lean, full):
    loads = [(1 << 20) // math.isqrt(grade ** lean) + 1 for grade in range(1, amount + 1)]
    largest = most if full else min(most, max(-(-total // amount), total * loads[0] // sum(loads)))
    least = 1 if total - largest >= amount - 1 else 0
    holding, spare = [largest] + [least] * (amount - 1), total - largest - least * (amount - 1)
    while spare > 0:
        free = [i for i in range(1, amount) if holding[i] < largest] or [i for i in range(1, amount) if holding[i] < most]
        pool, remaining = sum([loads[i] for i in free]), spare
        for i in free:
            more = min(most - holding[i], max(1, remaining * loads[i] // pool), spare)
            holding[i] = holding[i] + more
            spare = spare - more
    return np.array(holding)


def bell_draw(own_key, extent, width, most, shards=(), kind=jnp.bfloat16):
    loudness = block_scale(own_key, extent, shards, -0.22, 0.18) if shards else 1.0
    drawn = jax.random.normal(own_key, extent, jnp.float32) * width * loudness
    return jnp.minimum(jnp.maximum(drawn, -most), most).astype(kind)


def setup_inputs(seed: int = 0, part: int = 0) -> dict:
    arg_keys = jax.random.split(jax.random.key(seed), 9)
    own_keys = jax.random.split(jax.random.fold_in(arg_keys[8], part), 9)
    queries = bell_draw(own_keys[0], (RANKS * TOK, HEADS * HEAD_DIM), 1.0, 6.0, ((0, 8), (1, 2)))
    key_weight = bell_draw(arg_keys[1], (HEADS, HEAD_DIM, LATENT), (4 * HEAD_DIM) ** -0.5, 0.25, ((0, 2),))
    value_weight = bell_draw(arg_keys[2], (HEADS, LATENT, HEAD_DIM), 4 ** -0.5, 3.0, ((0, 2),))
    prefix_latent = draw_prefix_latent(jax.random.fold_in(jax.random.fold_in(arg_keys[8], part), 71), part)
    fresh_latent = draw_fresh_latent(jax.random.fold_in(jax.random.fold_in(arg_keys[8], part), 71), part)
    span_counts = draw_span_counts(jax.random.fold_in(jax.random.fold_in(arg_keys[8], part), 71), part)
    prefix_lengths = draw_prefix_lengths(jax.random.fold_in(jax.random.fold_in(arg_keys[8], part), 71), part)
    routes_keys = jax.random.split(jax.random.fold_in(own_keys[7], 1), (RANKS * TOK) // TOK)
    routes_turns = jax.random.permutation(jax.random.fold_in(own_keys[7], 3), (RANKS * TOK) // TOK)
    routes = jax.vmap(lambda own, number: assign_block(jax.random.fold_in(own_keys[7], 2), own, number, TOK, EXPERTS, TOPK, MOST, 0))(routes_keys, routes_turns).reshape((RANKS * TOK, TOPK))
    return {"queries": queries, "key_weight": key_weight, "value_weight": value_weight, "prefix_latent": prefix_latent, "fresh_latent": fresh_latent, "span_counts": span_counts, "prefix_lengths": prefix_lengths, "routes": routes}


def rank_attention(queries_rank, prefix_rank, fresh_rank, count_rank, prefix_size, key_weight, value_weight):
    slots = queries_rank.shape[0]
    split = queries_rank.reshape(slots, HEADS, HEAD_DIM).astype(jnp.float32)
    lifted = jnp.einsum('thd,hdc->htc', split, key_weight.astype(jnp.float32)).astype(jnp.bfloat16)
    lifted = lax.optimization_barrier(lifted).astype(jnp.float32)
    keys = jnp.concatenate([prefix_rank, fresh_rank], 0).astype(jnp.float32)
    scores = jnp.einsum('htc,kc->htk', lifted, keys) / jnp.sqrt(jnp.float32(HEAD_DIM))
    positions = jnp.arange(PMAX + TOK, dtype=jnp.int32)
    query_pos = jnp.arange(TOK, dtype=jnp.int32)
    fresh_pos = positions - PMAX
    allowed = jnp.where(positions[None, :] < PMAX, positions[None, :] < prefix_size, (fresh_pos[None, :] <= query_pos[:, None]) & (fresh_pos[None, :] < count_rank * SPAN))
    scores = jnp.where(allowed[None], scores, jnp.float32(-1e+30))
    highest = lax.optimization_barrier(jnp.max(scores, axis=-1, keepdims=True))
    weights = jnp.where(allowed[None], jnp.exp(scores - highest), jnp.float32(0.0))
    total = lax.optimization_barrier(jnp.sum(weights, axis=-1))
    rounded = lax.optimization_barrier(weights.astype(jnp.bfloat16)).astype(jnp.float32)
    mixed = jnp.einsum('htk,kc->htc', rounded, keys) / total[..., None]
    projected = jnp.einsum('htc,hce->the', mixed, value_weight.astype(jnp.float32), precision=lax.Precision.HIGHEST)
    return projected.reshape(slots, HEADS * HEAD_DIM).astype(jnp.bfloat16)

def rank_dispatch(attended_rank, routes_rank, count_rank):
    valid = jnp.arange(TOK, dtype=jnp.int32) < count_rank * SPAN
    hits = ((routes_rank[:, :, None] == jnp.arange(EXPERTS, dtype=jnp.int32)[None, None, :]) & valid[:, None, None]).astype(jnp.int32)
    per_token = lax.optimization_barrier(jnp.sum(hits, axis=1))
    before = jnp.cumsum(per_token, axis=0) - per_token
    place = lax.optimization_barrier(jnp.sum(hits * before[:, None, :], axis=-1))
    target = routes_rank * MOST + place
    table = (target[:, :, None] == jnp.arange(EXPERTS * MOST, dtype=jnp.int32)[None, None, :]) & valid[:, None, None]
    table = jnp.any(table, axis=1).astype(jnp.float32)
    grouped = jnp.einsum('tp,tf->pf', table, attended_rank.astype(jnp.float32))
    return grouped.astype(jnp.bfloat16).reshape(EXPERTS, MOST, HEADS * HEAD_DIM)

def reference(queries, key_weight, value_weight, prefix_latent, fresh_latent, span_counts, prefix_lengths, routes):
    query_ranks = queries.reshape(RANKS, TOK, HEADS * HEAD_DIM)
    prefix_ranks = prefix_latent.reshape(RANKS, PMAX, LATENT)
    fresh_ranks = fresh_latent.reshape(RANKS, TOK, LATENT)
    route_ranks = routes.reshape(RANKS, TOK, TOPK)

    def one_rank(pieces):
        query_rank, prefix_rank, fresh_rank, count_rank, prefix_size, route_rank = pieces
        attended = rank_attention(query_rank, prefix_rank, fresh_rank, count_rank, prefix_size, key_weight, value_weight)
        return rank_dispatch(attended, route_rank, count_rank)
    grouped = lax.map(one_rank, (query_ranks, prefix_ranks, fresh_ranks, span_counts, prefix_lengths, route_ranks))
    return jnp.transpose(grouped, (1, 0, 2, 3))
```

```python
import functools
import math

import jax
import jax.numpy as jnp
from jax import lax
from jax.experimental import pallas as pl
from jax.experimental.pallas import tpu as pltpu
from jax.sharding import PartitionSpec as P

SPAN = 64
GROUP = 4
UNROLL = 2
MASKED = -1e30
OPEN = 3e38
NT = (((1,), (1,)), ((), ()))


def dot(left, right):
    return jnp.dot(left, right, preferred_element_type=jnp.float32)


def build_table(count, routes_ref, table_ref, capacity):
    slots = routes_ref.shape[1]
    rows = table_ref.shape[0]
    place = lax.broadcasted_iota(jnp.int32, (rows, slots), 0)
    token = lax.broadcasted_iota(jnp.int32, (rows, slots), 1)
    expert = place // capacity
    hit = ((routes_ref[0:1, :] == expert) | (routes_ref[1:2, :] == expert)) & (
        token < count * SPAN
    )
    hit = jnp.where(hit, jnp.float32(1.0), jnp.float32(0.0))
    first = lax.broadcasted_iota(jnp.int32, (slots, slots), 0)
    second = lax.broadcasted_iota(jnp.int32, (slots, slots), 1)
    earlier = jnp.where(first < second, jnp.float32(1.0), jnp.float32(0.0))
    before = dot(hit.astype(jnp.bfloat16), earlier.astype(jnp.bfloat16))
    wanted = (place - expert * capacity).astype(jnp.float32)
    table_ref[...] = jnp.where(before == wanted, hit, jnp.float32(0.0)).astype(jnp.bfloat16)


def attend_kernel(
    capacity,
    count_ref,
    size_ref,
    routes_ref,
    queries_ref,
    key_weight_ref,
    value_weight_ref,
    prefix_ref,
    fresh_ref,
    out_ref,
    keys_ref,
    cap_ref,
    table_ref,
):
    slots = queries_ref.shape[0]
    past = prefix_ref.shape[0]
    dim = key_weight_ref.shape[1]

    @pl.when(pl.program_id(0) == 0)
    def _():
        count, size = count_ref[0], size_ref[0]
        keys_ref[:past] = prefix_ref[...]
        keys_ref[past:] = fresh_ref[...]
        lane = lax.broadcasted_iota(jnp.int32, (slots, past), 1)
        cap_ref[:, :past] = jnp.where(lane < size, jnp.float32(OPEN), jnp.float32(MASKED))
        row = lax.broadcasted_iota(jnp.int32, (slots, slots), 0)
        col = lax.broadcasted_iota(jnp.int32, (slots, slots), 1)
        cap_ref[:, past:] = jnp.where(
            (col <= row) & (col < count * SPAN), jnp.float32(OPEN), jnp.float32(MASKED)
        )
        build_table(count, routes_ref, table_ref, capacity)

    scale = math.log2(math.e) / math.sqrt(dim)
    keys = keys_ref[...]
    scores = []
    for stack in range(UNROLL):
        lifted = []
        for h in range(stack * GROUP, (stack + 1) * GROUP):
            one = dot(queries_ref[:, h * dim : (h + 1) * dim], key_weight_ref[h])
            lifted.append(one.astype(jnp.bfloat16))
        lifted = jnp.concatenate(lifted, axis=0)
        score = lax.dot_general(lifted, keys, NT, preferred_element_type=jnp.float32)
        scores.append(score)
    for stack in range(UNROLL):
        score = scores[stack].reshape(GROUP, slots, keys.shape[0])
        score = jnp.minimum(score, cap_ref[...][None])
        highest = jnp.max(score, axis=-1, keepdims=True) * scale
        weights = jnp.exp2(score * scale - highest)
        total = jnp.sum(weights, axis=-1, keepdims=True)
        weights = weights.astype(jnp.bfloat16).reshape(GROUP * slots, keys.shape[0])
        mixed = dot(weights, keys).astype(jnp.bfloat16)
        for g in range(GROUP):
            h = stack * GROUP + g
            projected = dot(mixed[g * slots : (g + 1) * slots], value_weight_ref[h])
            attended = (projected / total[g]).astype(jnp.bfloat16)
            out_ref[:, h * dim : (h + 1) * dim] = dot(table_ref[...], attended).astype(
                jnp.bfloat16
            )


def attend(queries, key_weight, value_weight, prefix, fresh, count, size, routes, experts):
    slots = queries.shape[0]
    heads, dim, latent = key_weight.shape
    step = GROUP * UNROLL
    places = slots * routes.shape[1]
    keys = prefix.shape[0] + slots
    whole = lambda shape: pl.BlockSpec(shape, lambda i: (0,) * len(shape))
    smem = pl.BlockSpec(memory_space=pltpu.SMEM)
    return pl.pallas_call(
        functools.partial(attend_kernel, places // experts),
        grid=(heads // step,),
        in_specs=[
            smem,
            smem,
            whole((routes.shape[1], slots)),
            pl.BlockSpec((slots, step * dim), lambda i: (0, i)),
            pl.BlockSpec((step, dim, latent), lambda i: (i, 0, 0)),
            pl.BlockSpec((step, latent, dim), lambda i: (i, 0, 0)),
            whole(prefix.shape),
            whole(fresh.shape),
        ],
        out_specs=pl.BlockSpec((places, step * dim), lambda i: (0, i)),
        out_shape=jax.ShapeDtypeStruct((places, heads * dim), jnp.bfloat16),
        scratch_shapes=[
            pltpu.VMEM((keys, latent), jnp.bfloat16),
            pltpu.VMEM((slots, keys), jnp.float32),
            pltpu.VMEM((places, slots), jnp.bfloat16),
        ],
        compiler_params=pltpu.CompilerParams(vmem_limit_bytes=48 * 1024 * 1024),
    )(count, size, routes.T, queries, key_weight, value_weight, prefix, fresh)


def place_kernel(arrived_ref, out_ref, sem):
    sources, _, features = arrived_ref.shape
    ranks = out_ref.shape[1]
    cores = sources // ranks
    copies = [
        pltpu.make_async_copy(
            arrived_ref.at[s],
            out_ref.at[0, s // cores, :, pl.ds(s % cores * features, features)],
            sem.at[s],
        )
        for s in range(sources)
    ]
    for copy in copies:
        copy.start()
    for copy in copies:
        copy.wait()


def assemble(arrived, ranks, cores):
    sources, capacity, features = arrived.shape
    if capacity % 16:
        arrived = arrived.reshape(ranks, cores, capacity, features).transpose(0, 2, 1, 3)
        return arrived.reshape(1, ranks, capacity, cores * features)
    return pl.pallas_call(
        place_kernel,
        in_specs=[pl.BlockSpec(memory_space=pl.ANY)],
        out_specs=pl.BlockSpec(memory_space=pl.ANY),
        out_shape=jax.ShapeDtypeStruct((1, ranks, capacity, cores * features), arrived.dtype),
        scratch_shapes=[pltpu.SemaphoreType.DMA((sources,))],
    )(arrived)


def local(
    queries,
    key_weight,
    value_weight,
    prefix_latent,
    fresh_latent,
    span_counts,
    prefix_lengths,
    routes,
):
    ranks, cores = lax.axis_size("dp"), lax.axis_size("ep")
    experts = ranks * cores
    outgoing = attend(
        queries,
        key_weight,
        value_weight,
        prefix_latent,
        fresh_latent,
        span_counts,
        prefix_lengths,
        routes,
        experts,
    )
    arrived = lax.all_to_all(
        outgoing.reshape(experts, -1, outgoing.shape[1]),
        ("dp", "ep"),
        split_axis=0,
        concat_axis=0,
        tiled=True,
    )
    return assemble(arrived, ranks, cores)


def solution(mesh):
    in_specs = (
        P(("groups", "dp"), "ep"),
        P("ep", None, None),
        P("ep", None, None),
        P(("groups", "dp"), None),
        P(("groups", "dp"), None),
        P(("groups", "dp")),
        P(("groups", "dp")),
        P(("groups", "dp"), None),
    )
    out_specs = P(("groups", "dp", "ep"), None, None, None)
    return jax.shard_map(local, mesh=mesh, in_specs=in_specs, out_specs=out_specs, check_vma=False)
```

```python
import functools
import math

import jax
import jax.numpy as jnp
from jax import lax
from jax.experimental import pallas as pl
from jax.experimental.pallas import tpu as pltpu
from jax.sharding import PartitionSpec as P

SPAN = 64
GROUP = 4
CHUNKS = 4
DIRECT = 32
MASKED = -1e30
OPEN = 3e38
NT = (((1,), (1,)), ((), ()))


def dot(left, right):
    return jnp.dot(left, right, preferred_element_type=jnp.float32)


def build_table(me, count, routes_ref, table_ref, capacity):
    slots = routes_ref.shape[1]
    rows = table_ref.shape[0]
    place = lax.broadcasted_iota(jnp.int32, (rows, slots), 0)
    token = lax.broadcasted_iota(jnp.int32, (rows, slots), 1)
    block = place // capacity
    expert = block ^ me
    hit = ((routes_ref[0:1, :] == expert) | (routes_ref[1:2, :] == expert)) & (
        token < count * SPAN
    )
    hit = jnp.where(hit, jnp.float32(1.0), jnp.float32(0.0))
    first = lax.broadcasted_iota(jnp.int32, (slots, slots), 0)
    second = lax.broadcasted_iota(jnp.int32, (slots, slots), 1)
    earlier = jnp.where(first < second, jnp.float32(1.0), jnp.float32(0.0))
    before = dot(hit.astype(jnp.bfloat16), earlier.astype(jnp.bfloat16))
    wanted = (place - block * capacity).astype(jnp.float32)
    table_ref[...] = jnp.where(before == wanted, hit, jnp.float32(0.0)).astype(jnp.bfloat16)


def attend_kernel(
    capacity,
    me_ref,
    count_ref,
    size_ref,
    routes_ref,
    queries_ref,
    key_weight_ref,
    value_weight_ref,
    prefix_ref,
    fresh_ref,
    *rest,
):
    *out_refs, keys_ref, cap_ref, table_ref, attended_ref = rest
    slots = queries_ref.shape[0]
    past = prefix_ref.shape[0]
    dim = key_weight_ref.shape[1]
    count, size = count_ref[0], size_ref[0]
    keys_ref[:past] = prefix_ref[...]
    keys_ref[past:] = fresh_ref[...]
    lane = lax.broadcasted_iota(jnp.int32, (slots, past), 1)
    cap_ref[:, :past] = jnp.where(lane < size, jnp.float32(OPEN), jnp.float32(MASKED))
    row = lax.broadcasted_iota(jnp.int32, (slots, slots), 0)
    col = lax.broadcasted_iota(jnp.int32, (slots, slots), 1)
    cap_ref[:, past:] = jnp.where(
        (col <= row) & (col < count * SPAN), jnp.float32(OPEN), jnp.float32(MASKED)
    )
    build_table(me_ref[0], count, routes_ref, table_ref, capacity)

    scale = math.log2(math.e) / math.sqrt(dim)
    keys = keys_ref[...]
    stacks = key_weight_ref.shape[0] // GROUP
    scores = []
    for stack in range(stacks):
        lifted = []
        for h in range(stack * GROUP, (stack + 1) * GROUP):
            one = dot(queries_ref[:, h * dim : (h + 1) * dim], key_weight_ref[h])
            lifted.append(one.astype(jnp.bfloat16))
        lifted = jnp.concatenate(lifted, axis=0)
        score = lax.dot_general(lifted, keys, NT, preferred_element_type=jnp.float32)
        scores.append(score)
    for stack in range(stacks):
        score = scores[stack].reshape(GROUP, slots, keys.shape[0])
        score = jnp.minimum(score, cap_ref[...][None])
        highest = jnp.max(score, axis=-1, keepdims=True) * scale
        weights = jnp.exp2(score * scale - highest)
        total = jnp.sum(weights, axis=-1, keepdims=True)
        weights = weights.astype(jnp.bfloat16).reshape(GROUP * slots, keys.shape[0])
        mixed = dot(weights, keys).astype(jnp.bfloat16)
        for g in range(GROUP):
            h = stack * GROUP + g
            projected = dot(mixed[g * slots : (g + 1) * slots], value_weight_ref[h])
            attended_ref[:, h * dim : (h + 1) * dim] = (projected / total[g]).astype(jnp.bfloat16)
    grouped = dot(table_ref[...], attended_ref[...]).astype(jnp.bfloat16)
    rows = out_refs[0].shape[0]
    for k, out_ref in enumerate(out_refs):
        out_ref[...] = grouped[k * rows : (k + 1) * rows]


def attend(
    chunk, heads, me, queries, key_weight, value_weight, prefix, fresh, count, size, routes, experts, pieces
):
    slots = queries.shape[0]
    _, dim, latent = key_weight.shape
    places = slots * routes.shape[1]
    keys = prefix.shape[0] + slots
    whole = lambda shape: pl.BlockSpec(shape, lambda i: (0,) * len(shape))
    smem = pl.BlockSpec(memory_space=pltpu.SMEM)
    piece = (places // pieces, heads * dim)
    flops = 4 * slots * heads * keys * latent
    return pl.pallas_call(
        functools.partial(attend_kernel, places // experts),
        grid=(1,),
        in_specs=[
            smem,
            smem,
            smem,
            whole((routes.shape[1], slots)),
            pl.BlockSpec((slots, heads * dim), lambda i: (0, chunk)),
            pl.BlockSpec((heads, dim, latent), lambda i: (chunk, 0, 0)),
            pl.BlockSpec((heads, latent, dim), lambda i: (chunk, 0, 0)),
            whole(prefix.shape),
            whole(fresh.shape),
        ],
        out_specs=[whole(piece)] * pieces,
        out_shape=[jax.ShapeDtypeStruct(piece, jnp.bfloat16)] * pieces,
        scratch_shapes=[
            pltpu.VMEM((keys, latent), jnp.bfloat16),
            pltpu.VMEM((slots, keys), jnp.float32),
            pltpu.VMEM((places, slots), jnp.bfloat16),
            pltpu.VMEM((slots, heads * dim), jnp.bfloat16),
        ],
        compiler_params=pltpu.CompilerParams(vmem_limit_bytes=40 * 1024 * 1024),
        cost_estimate=pl.CostEstimate(
            flops=flops, bytes_accessed=4 * heads * dim * latent, transcendentals=heads * slots * keys
        ),
    )(me, count, size, routes.T, queries, key_weight, value_weight, prefix, fresh)


def place_kernel(chunks, cores, me_ref, *rest):
    *piece_refs, out_ref, sem = rest
    sources = len(piece_refs) // chunks
    width = piece_refs[0].shape[1]
    me = me_ref[0]
    copies = []
    for i, piece_ref in enumerate(piece_refs):
        chunk, k = divmod(i, sources)
        source = me ^ k
        start = (source % cores * chunks + chunk) * width
        target = out_ref.at[0, source // cores, :, pl.ds(pl.multiple_of(start, width), width)]
        copies.append(pltpu.make_async_copy(piece_ref, target, sem.at[i]))
    for copy in copies:
        copy.start()
    for copy in copies:
        copy.wait()


def assemble(me, chunks, ranks, cores):
    pieces = [piece for chunk in chunks for piece in chunk]
    capacity, width = pieces[0].shape
    return pl.pallas_call(
        functools.partial(place_kernel, len(chunks), cores),
        in_specs=[pl.BlockSpec(memory_space=pltpu.SMEM)]
        + [pl.BlockSpec(memory_space=pltpu.VMEM)] * len(pieces),
        out_specs=pl.BlockSpec(memory_space=pl.ANY),
        out_shape=jax.ShapeDtypeStruct(
            (1, ranks, capacity, cores * len(chunks) * width), jnp.bfloat16
        ),
        scratch_shapes=[pltpu.SemaphoreType.DMA((len(pieces),))],
    )(me, *pieces)


def exchange_order(experts):
    near, far = list(range(1, experts // 2)), list(range(experts // 2, experts))
    early, late = far[len(far) // 2 :], far[: len(far) // 2]
    mixed = []
    while near or early:
        mixed += early[:1] + near[:1]
        early, near = early[1:], near[1:]
    return mixed + late


def local(
    queries,
    key_weight,
    value_weight,
    prefix_latent,
    fresh_latent,
    span_counts,
    prefix_lengths,
    routes,
):
    ranks, cores = lax.axis_size("dp"), lax.axis_size("ep")
    experts = ranks * cores
    direct = experts <= DIRECT
    index = lax.axis_index("dp") * cores + lax.axis_index("ep")
    me = (index if direct else jnp.int32(0)).astype(jnp.int32).reshape(1)
    heads = key_weight.shape[0] // CHUNKS
    chunks = []
    for chunk in range(CHUNKS):
        outgoing = attend(
            chunk,
            heads,
            me,
            queries,
            key_weight,
            value_weight,
            prefix_latent,
            fresh_latent,
            span_counts,
            prefix_lengths,
            routes,
            experts,
            experts if direct else 1,
        )
        if direct:
            arrived = list(outgoing)
            for k in exchange_order(experts):
                pairs = [(i, i ^ k) for i in range(experts)]
                arrived[k] = lax.ppermute(outgoing[k], ("dp", "ep"), pairs)
        else:
            arrived = lax.all_to_all(
                outgoing[0].reshape(experts, -1, outgoing[0].shape[1]),
                ("dp", "ep"),
                split_axis=0,
                concat_axis=0,
                tiled=True,
            )
        chunks.append(arrived)
    if direct:
        return assemble(me, chunks, ranks, cores)
    arrived = jnp.stack(chunks).reshape(CHUNKS, ranks, cores, -1, chunks[0].shape[2])
    arrived = arrived.transpose(1, 3, 2, 0, 4)
    return arrived.reshape(1, ranks, arrived.shape[1], -1)


def solution(mesh):
    in_specs = (
        P(("groups", "dp"), "ep"),
        P("ep", None, None),
        P("ep", None, None),
        P(("groups", "dp"), None),
        P(("groups", "dp"), None),
        P(("groups", "dp")),
        P(("groups", "dp")),
        P(("groups", "dp"), None),
    )
    out_specs = P(("groups", "dp", "ep"), None, None, None)
    return jax.shard_map(local, mesh=mesh, in_specs=in_specs, out_specs=out_specs, check_vma=False)
```

```python
import functools
import math

import jax
import jax.numpy as jnp
from jax import lax
from jax.experimental import pallas as pl
from jax.experimental.pallas import tpu as pltpu
from jax.sharding import PartitionSpec as P

SPAN = 64
GROUP = 4
CHUNKS = (1, 1, 1, 1)
DIRECT = 16
MASKED = -1e30
OPEN = 3e38
NT = (((1,), (1,)), ((), ()))


def dot(left, right):
    return jnp.dot(left, right, preferred_element_type=jnp.float32)


def build_table(me, count, routes_ref, table_ref, capacity):
    slots = routes_ref.shape[1]
    rows = table_ref.shape[0]
    place = lax.broadcasted_iota(jnp.int32, (rows, slots), 0)
    token = lax.broadcasted_iota(jnp.int32, (rows, slots), 1)
    block = place // capacity
    expert = block ^ me
    hit = ((routes_ref[0:1, :] == expert) | (routes_ref[1:2, :] == expert)) & (
        token < count * SPAN
    )
    hit = jnp.where(hit, jnp.float32(1.0), jnp.float32(0.0))
    first = lax.broadcasted_iota(jnp.int32, (slots, slots), 0)
    second = lax.broadcasted_iota(jnp.int32, (slots, slots), 1)
    earlier = jnp.where(first < second, jnp.float32(1.0), jnp.float32(0.0))
    before = dot(hit.astype(jnp.bfloat16), earlier.astype(jnp.bfloat16))
    wanted = (place - block * capacity).astype(jnp.float32)
    table_ref[...] = jnp.where(before == wanted, hit, jnp.float32(0.0)).astype(jnp.bfloat16)


def attend_kernel(
    capacity,
    first,
    me_ref,
    count_ref,
    size_ref,
    routes_ref,
    queries_hbm,
    key_weight_hbm,
    value_weight_hbm,
    prefix_hbm,
    fresh_hbm,
    *rest,
):
    *out_refs, queries_ref, key_weight_ref, value_weight_ref, keys_ref = rest[:-4]
    cap_ref, table_ref, attended_ref, sem = rest[-4:]
    slots = queries_ref.shape[0]
    past = prefix_hbm.shape[0]
    heads, dim, _ = key_weight_ref.shape
    here = pl.ds(first, heads)
    copies = [
        pltpu.make_async_copy(
            queries_hbm.at[:, pl.ds(first * dim, heads * dim)], queries_ref, sem.at[0]
        ),
        pltpu.make_async_copy(key_weight_hbm.at[here], key_weight_ref, sem.at[1]),
        pltpu.make_async_copy(prefix_hbm, keys_ref.at[pl.ds(0, past)], sem.at[2]),
        pltpu.make_async_copy(fresh_hbm, keys_ref.at[pl.ds(past, slots)], sem.at[3]),
        pltpu.make_async_copy(value_weight_hbm.at[here], value_weight_ref, sem.at[4]),
    ]
    for copy in copies:
        copy.start()
    count, size = count_ref[0], size_ref[0]
    lane = lax.broadcasted_iota(jnp.int32, (slots, past), 1)
    cap_ref[:, :past] = jnp.where(lane < size, jnp.float32(OPEN), jnp.float32(MASKED))
    row = lax.broadcasted_iota(jnp.int32, (slots, slots), 0)
    col = lax.broadcasted_iota(jnp.int32, (slots, slots), 1)
    cap_ref[:, past:] = jnp.where(
        (col <= row) & (col < count * SPAN), jnp.float32(OPEN), jnp.float32(MASKED)
    )
    build_table(me_ref[0], count, routes_ref, table_ref, capacity)
    for copy in copies:
        copy.wait()

    scale = math.log2(math.e) / math.sqrt(dim)
    keys = keys_ref[...]
    stacks = heads // GROUP
    scores = []
    for stack in range(stacks):
        lifted = []
        for h in range(stack * GROUP, (stack + 1) * GROUP):
            one = dot(queries_ref[:, h * dim : (h + 1) * dim], key_weight_ref[h])
            lifted.append(one.astype(jnp.bfloat16))
        lifted = jnp.concatenate(lifted, axis=0)
        score = lax.dot_general(lifted, keys, NT, preferred_element_type=jnp.float32)
        scores.append(score)
    for stack in range(stacks):
        score = scores[stack].reshape(GROUP, slots, keys.shape[0])
        score = jnp.minimum(score, cap_ref[...][None])
        highest = jnp.max(score, axis=-1, keepdims=True) * scale
        weights = jnp.exp2(score * scale - highest)
        total = jnp.sum(weights, axis=-1, keepdims=True)
        weights = weights.astype(jnp.bfloat16).reshape(GROUP * slots, keys.shape[0])
        mixed = dot(weights, keys).astype(jnp.bfloat16)
        for g in range(GROUP):
            h = stack * GROUP + g
            projected = dot(mixed[g * slots : (g + 1) * slots], value_weight_ref[h])
            attended_ref[:, h * dim : (h + 1) * dim] = (projected / total[g]).astype(jnp.bfloat16)
    grouped = dot(table_ref[...], attended_ref[...]).astype(jnp.bfloat16)
    rows = out_refs[0].shape[0]
    for k, out_ref in enumerate(out_refs):
        out_ref[...] = grouped[k * rows : (k + 1) * rows]


def attend(
    first, heads, me, queries, key_weight, value_weight, prefix, fresh, count, size, routes, experts, pieces
):
    slots = queries.shape[0]
    _, dim, latent = key_weight.shape
    places = slots * routes.shape[1]
    keys = prefix.shape[0] + slots
    smem = pl.BlockSpec(memory_space=pltpu.SMEM)
    vmem = pl.BlockSpec(memory_space=pltpu.VMEM)
    hbm = pl.BlockSpec(memory_space=pltpu.HBM)
    piece = (places // pieces, heads * dim)
    return pl.pallas_call(
        functools.partial(attend_kernel, places // experts, first),
        in_specs=[smem, smem, smem, vmem, hbm, hbm, hbm, hbm, hbm],
        out_specs=[vmem] * pieces,
        out_shape=[jax.ShapeDtypeStruct(piece, jnp.bfloat16)] * pieces,
        scratch_shapes=[
            pltpu.VMEM((slots, heads * dim), jnp.bfloat16),
            pltpu.VMEM((heads, dim, latent), jnp.bfloat16),
            pltpu.VMEM((heads, latent, dim), jnp.bfloat16),
            pltpu.VMEM((keys, latent), jnp.bfloat16),
            pltpu.VMEM((slots, keys), jnp.float32),
            pltpu.VMEM((places, slots), jnp.bfloat16),
            pltpu.VMEM((slots, heads * dim), jnp.bfloat16),
            pltpu.SemaphoreType.DMA((5,)),
        ],
        compiler_params=pltpu.CompilerParams(vmem_limit_bytes=54 * 1024 * 1024),
        cost_estimate=pl.CostEstimate(
            flops=4 * slots * heads * keys * latent,
            bytes_accessed=4 * heads * dim * latent,
            transcendentals=heads * slots * keys,
        ),
    )(me, count, size, routes.T, queries, key_weight, value_weight, prefix, fresh)


def run_copies(copies):
    for copy in copies:
        copy.start()
    for copy in copies:
        copy.wait()


def pass_on_kernel(cores, *refs):
    *piece_refs, out_ref, sem = refs
    capacity = piece_refs[0].shape[0] // cores
    run_copies(
        [
            pltpu.make_async_copy(
                piece_ref.at[pl.ds(capacity, capacity)],
                out_ref.at[pl.ds(j * capacity, capacity)],
                sem.at[j],
            )
            for j, piece_ref in enumerate(piece_refs)
        ]
    )


def pass_on(pieces, cores):
    rows, width = pieces[0].shape
    return pl.pallas_call(
        functools.partial(pass_on_kernel, cores),
        in_specs=[pl.BlockSpec(memory_space=pl.ANY)] * len(pieces),
        out_specs=pl.BlockSpec(memory_space=pltpu.VMEM),
        out_shape=jax.ShapeDtypeStruct((len(pieces) * rows // cores, width), jnp.bfloat16),
        scratch_shapes=[pltpu.SemaphoreType.DMA((len(pieces),))],
    )(*pieces)


def place_kernel(plan, cores, me_ref, *rest):
    *refs, out_ref, whole_ref, sem = rest
    _, capacity, features = whole_ref.shape
    features //= cores
    me = me_ref[0]
    copies = []
    for i, (ref, (first, start, source)) in enumerate(plan):
        ref = refs[ref]
        width = ref.shape[1]
        who = me ^ source
        left = pl.multiple_of(who % cores * features + first, math.gcd(features, first))
        copies.append(
            pltpu.make_async_copy(
                ref.at[pl.ds(start, capacity)],
                whole_ref.at[who // cores, :, pl.ds(left, width)],
                sem.at[i],
            )
        )
    run_copies(copies)
    run_copies([pltpu.make_async_copy(whole_ref, out_ref.at[0], sem.at[0])])


def assemble(me, arrays, plan, shape, cores):
    return pl.pallas_call(
        functools.partial(place_kernel, plan, cores),
        in_specs=[pl.BlockSpec(memory_space=pltpu.SMEM)]
        + [pl.BlockSpec(memory_space=pl.ANY)] * len(arrays),
        out_specs=pl.BlockSpec(memory_space=pl.ANY),
        out_shape=jax.ShapeDtypeStruct(shape, jnp.bfloat16),
        scratch_shapes=[
            pltpu.VMEM(shape[1:], jnp.bfloat16),
            pltpu.SemaphoreType.DMA((len(plan),)),
        ],
    )(me, *arrays)


def exchange_order(ranks):
    near, far = list(range(1, ranks // 2)), list(range(ranks // 2, ranks))
    mixed = []
    while len(far) > 2 or near:
        mixed += near[:1] + (far[:1] if len(far) > 2 else [])
        near, far = near[1:], (far[1:] if len(far) > 2 else far)
    return mixed + far


def local(
    queries,
    key_weight,
    value_weight,
    prefix_latent,
    fresh_latent,
    span_counts,
    prefix_lengths,
    routes,
):
    ranks, cores = lax.axis_size("dp"), lax.axis_size("ep")
    experts = ranks * cores
    slots = queries.shape[0]
    heads, dim, _ = key_weight.shape
    capacity = slots * routes.shape[1] // experts
    direct = ranks <= DIRECT and capacity % 16 == 0
    index = lax.axis_index("dp") * cores + lax.axis_index("ep")
    me = (index if direct else jnp.int32(0)).astype(jnp.int32).reshape(1)
    shares = [heads * share // sum(CHUNKS) for share in CHUNKS]
    chunks, plan = [], []
    first = 0
    for share in shares:
        outgoing = attend(
            first,
            share,
            me,
            queries,
            key_weight,
            value_weight,
            prefix_latent,
            fresh_latent,
            span_counts,
            prefix_lengths,
            routes,
            experts,
            ranks if direct else 1,
        )
        if direct:
            order = exchange_order(ranks)
            pieces = [outgoing[0]]
            for j in order:
                pairs = [(i, i ^ j) for i in range(ranks)]
                pieces.append(lax.ppermute(outgoing[j], "dp", pairs))
            swapped = lax.ppermute(
                pass_on(pieces, cores), "ep", [(i, i ^ 1) for i in range(cores)]
            )
            for at, j in enumerate([0] + order):
                plan.append((len(chunks) + at, (first * dim, 0, j * cores)))
                plan.append((len(chunks) + ranks, (first * dim, at * capacity, j * cores + 1)))
            chunks += pieces + [swapped]
        else:
            arrived = lax.all_to_all(
                outgoing[0].reshape(experts, capacity, share * dim),
                ("dp", "ep"),
                split_axis=0,
                concat_axis=0,
                tiled=True,
            )
            chunks.append(arrived.reshape(ranks, cores, capacity, share * dim))
        first += share
    if direct:
        return assemble(me, chunks, plan, (1, ranks, capacity, cores * heads * dim), cores)
    arrived = jnp.concatenate(chunks, axis=3).transpose(0, 2, 1, 3)
    return arrived.reshape(1, ranks, capacity, cores * heads * dim)


def solution(mesh):
    in_specs = (
        P(("groups", "dp"), "ep"),
        P("ep", None, None),
        P("ep", None, None),
        P(("groups", "dp"), None),
        P(("groups", "dp"), None),
        P(("groups", "dp")),
        P(("groups", "dp")),
        P(("groups", "dp"), None),
    )
    out_specs = P(("groups", "dp", "ep"), None, None, None)
    return jax.shard_map(local, mesh=mesh, in_specs=in_specs, out_specs=out_specs, check_vma=False)
```

```python
import functools
import math

import jax
import jax.numpy as jnp
from jax import lax
from jax.experimental import pallas as pl
from jax.experimental.pallas import tpu as pltpu
from jax.sharding import PartitionSpec as P

SPAN = 64
GROUP = 4
CHUNKS = (1, 1)
DIRECT = 16
VMEM = 58 * 1024 * 1024
MASKED = -1e30
OPEN = 3e38
NT = (((1,), (1,)), ((), ()))


def dot(left, right):
    return jnp.dot(left, right, preferred_element_type=jnp.float32)


def build_table(me, count, routes_ref, table_ref, capacity):
    slots = routes_ref.shape[1]
    rows = table_ref.shape[0]
    place = lax.broadcasted_iota(jnp.int32, (rows, slots), 0)
    token = lax.broadcasted_iota(jnp.int32, (rows, slots), 1)
    block = place // capacity
    expert = block ^ me
    hit = ((routes_ref[0:1, :] == expert) | (routes_ref[1:2, :] == expert)) & (
        token < count * SPAN
    )
    hit = jnp.where(hit, jnp.float32(1.0), jnp.float32(0.0))
    first = lax.broadcasted_iota(jnp.int32, (slots, slots), 0)
    second = lax.broadcasted_iota(jnp.int32, (slots, slots), 1)
    earlier = jnp.where(first < second, jnp.float32(1.0), jnp.float32(0.0))
    before = dot(hit.astype(jnp.bfloat16), earlier.astype(jnp.bfloat16))
    wanted = (place - block * capacity).astype(jnp.float32)
    table_ref[...] = jnp.where(before == wanted, hit, jnp.float32(0.0)).astype(jnp.bfloat16)


def attend_kernel(
    capacity,
    first,
    me_ref,
    count_ref,
    size_ref,
    routes_ref,
    queries_hbm,
    key_weight_hbm,
    value_weight_hbm,
    prefix_hbm,
    fresh_hbm,
    *rest,
):
    *out_refs, queries_ref, key_weight_ref, value_weight_ref, keys_ref = rest[:-4]
    cap_ref, table_ref, attended_ref, sem = rest[-4:]
    slots = queries_ref.shape[0]
    past = prefix_hbm.shape[0]
    heads, dim, _ = key_weight_ref.shape
    here = pl.ds(first, heads)
    copies = [
        pltpu.make_async_copy(
            queries_hbm.at[:, pl.ds(first * dim, heads * dim)], queries_ref, sem.at[0]
        ),
        pltpu.make_async_copy(key_weight_hbm.at[here], key_weight_ref, sem.at[1]),
        pltpu.make_async_copy(prefix_hbm, keys_ref.at[pl.ds(0, past)], sem.at[2]),
        pltpu.make_async_copy(fresh_hbm, keys_ref.at[pl.ds(past, slots)], sem.at[3]),
        pltpu.make_async_copy(value_weight_hbm.at[here], value_weight_ref, sem.at[4]),
    ]
    for copy in copies:
        copy.start()
    for_queries, for_keys, for_values = copies[:2], copies[2:4], copies[4:]
    count, size = count_ref[0], size_ref[0]
    lane = lax.broadcasted_iota(jnp.int32, (slots, past), 1)
    cap_ref[:, :past] = jnp.where(lane < size, jnp.float32(OPEN), jnp.float32(MASKED))
    row = lax.broadcasted_iota(jnp.int32, (slots, slots), 0)
    col = lax.broadcasted_iota(jnp.int32, (slots, slots), 1)
    cap_ref[:, past:] = jnp.where(
        (col <= row) & (col < count * SPAN), jnp.float32(OPEN), jnp.float32(MASKED)
    )
    build_table(me_ref[0], count, routes_ref, table_ref, capacity)

    scale = math.log2(math.e) / math.sqrt(dim)
    stacks = heads // GROUP
    for copy in for_queries:
        copy.wait()
    lifted = []
    for h in range(heads):
        one = dot(queries_ref[:, h * dim : (h + 1) * dim], key_weight_ref[h])
        lifted.append(one.astype(jnp.bfloat16))
    for copy in for_keys:
        copy.wait()
    keys = keys_ref[...]
    scores = []
    for stack in range(stacks):
        rows = jnp.concatenate(lifted[stack * GROUP : (stack + 1) * GROUP], axis=0)
        scores.append(lax.dot_general(rows, keys, NT, preferred_element_type=jnp.float32))
    for copy in for_values:
        copy.wait()
    for stack in range(stacks):
        score = scores[stack].reshape(GROUP, slots, keys.shape[0])
        score = jnp.minimum(score, cap_ref[...][None])
        highest = jnp.max(score, axis=-1, keepdims=True) * scale
        weights = jnp.exp2(score * scale - highest)
        total = jnp.sum(weights, axis=-1, keepdims=True)
        weights = weights.astype(jnp.bfloat16).reshape(GROUP * slots, keys.shape[0])
        mixed = dot(weights, keys).astype(jnp.bfloat16)
        for g in range(GROUP):
            h = stack * GROUP + g
            projected = dot(mixed[g * slots : (g + 1) * slots], value_weight_ref[h])
            attended_ref[:, h * dim : (h + 1) * dim] = (projected / total[g]).astype(jnp.bfloat16)
    grouped = dot(table_ref[...], attended_ref[...]).astype(jnp.bfloat16)
    rows = out_refs[0].shape[0]
    for k, out_ref in enumerate(out_refs):
        out_ref[...] = grouped[k * rows : (k + 1) * rows]


def attend(
    first, heads, me, queries, key_weight, value_weight, prefix, fresh, count, size, routes, experts, pieces
):
    slots = queries.shape[0]
    _, dim, latent = key_weight.shape
    places = slots * routes.shape[1]
    keys = prefix.shape[0] + slots
    smem = pl.BlockSpec(memory_space=pltpu.SMEM)
    vmem = pl.BlockSpec(memory_space=pltpu.VMEM)
    hbm = pl.BlockSpec(memory_space=pltpu.HBM)
    piece = (places // pieces, heads * dim)
    return pl.pallas_call(
        functools.partial(attend_kernel, places // experts, first),
        in_specs=[smem, smem, smem, vmem, hbm, hbm, hbm, hbm, hbm],
        out_specs=[vmem] * pieces,
        out_shape=[jax.ShapeDtypeStruct(piece, jnp.bfloat16)] * pieces,
        scratch_shapes=[
            pltpu.VMEM((slots, heads * dim), jnp.bfloat16),
            pltpu.VMEM((heads, dim, latent), jnp.bfloat16),
            pltpu.VMEM((heads, latent, dim), jnp.bfloat16),
            pltpu.VMEM((keys, latent), jnp.bfloat16),
            pltpu.VMEM((slots, keys), jnp.float32),
            pltpu.VMEM((places, slots), jnp.bfloat16),
            pltpu.VMEM((slots, heads * dim), jnp.bfloat16),
            pltpu.SemaphoreType.DMA((5,)),
        ],
        compiler_params=pltpu.CompilerParams(vmem_limit_bytes=VMEM),
        cost_estimate=pl.CostEstimate(
            flops=4 * slots * heads * keys * latent,
            bytes_accessed=4 * heads * dim * latent,
            transcendentals=heads * slots * keys,
        ),
    )(me, count, size, routes.T, queries, key_weight, value_weight, prefix, fresh)


def run_copies(copies):
    for copy in copies:
        copy.start()
    for copy in copies:
        copy.wait()


def exchange(piece, axis, size, bits):
    pairs = [[i, i ^ bits] for i in range(size) if i < i ^ bits]
    return lax.all_gather(piece, axis, axis_index_groups=pairs)


def partner(ref, me, bits):
    return ref.at[((me ^ bits) > me).astype(jnp.int32)] if bits else ref


def pass_on_kernel(cores, order, me_ref, *refs):
    *piece_refs, out_ref, sem = refs
    capacity = piece_refs[0].shape[0] // cores
    copies = []
    for i, (piece_ref, j) in enumerate(zip(piece_refs, order)):
        piece_ref = partner(piece_ref, me_ref[0], j * cores)
        copies.append(
            pltpu.make_async_copy(
                piece_ref.at[pl.ds(capacity, capacity)],
                out_ref.at[pl.ds(i * capacity, capacity)],
                sem.at[i],
            )
        )
    run_copies(copies)


def pass_on(me, pieces, order, cores):
    rows, width = pieces[0].shape
    return pl.pallas_call(
        functools.partial(pass_on_kernel, cores, order),
        in_specs=[pl.BlockSpec(memory_space=pltpu.SMEM)]
        + [pl.BlockSpec(memory_space=pl.ANY)] * len(pieces),
        out_specs=pl.BlockSpec(memory_space=pltpu.VMEM),
        out_shape=jax.ShapeDtypeStruct((len(pieces) * rows // cores, width), jnp.bfloat16),
        scratch_shapes=[pltpu.SemaphoreType.DMA((len(pieces),))],
        compiler_params=pltpu.CompilerParams(vmem_limit_bytes=VMEM),
    )(me, *pieces)


def place_kernel(plan, cores, me_ref, *rest):
    *refs, out_ref, whole_ref, sem = rest
    _, capacity, features = whole_ref.shape
    features //= cores
    me = me_ref[0]
    copies = []
    for i, (ref, (first, start, source, bits)) in enumerate(plan):
        ref = partner(refs[ref], me, bits)
        width = ref.shape[-1]
        who = me ^ source
        left = pl.multiple_of(who % cores * features + first, math.gcd(features, first))
        copies.append(
            pltpu.make_async_copy(
                ref.at[pl.ds(start, capacity)],
                whole_ref.at[who // cores, :, pl.ds(left, width)],
                sem.at[i],
            )
        )
    run_copies(copies)
    run_copies([pltpu.make_async_copy(whole_ref, out_ref.at[0], sem.at[0])])


def assemble(me, arrays, plan, shape, cores):
    return pl.pallas_call(
        functools.partial(place_kernel, plan, cores),
        in_specs=[pl.BlockSpec(memory_space=pltpu.SMEM)]
        + [pl.BlockSpec(memory_space=pl.ANY)] * len(arrays),
        out_specs=pl.BlockSpec(memory_space=pl.ANY),
        out_shape=jax.ShapeDtypeStruct(shape, jnp.bfloat16),
        scratch_shapes=[
            pltpu.VMEM(shape[1:], jnp.bfloat16),
            pltpu.SemaphoreType.DMA((len(plan),)),
        ],
        compiler_params=pltpu.CompilerParams(vmem_limit_bytes=VMEM),
    )(me, *arrays)


def exchange_order(ranks):
    near, far = list(range(1, ranks // 2)), list(range(ranks // 2, ranks))
    mixed = []
    while len(far) > 2 or near:
        mixed += near[:1] + (far[:1] if len(far) > 2 else [])
        near, far = near[1:], (far[1:] if len(far) > 2 else far)
    return mixed + far


def local(
    queries,
    key_weight,
    value_weight,
    prefix_latent,
    fresh_latent,
    span_counts,
    prefix_lengths,
    routes,
):
    ranks, cores = lax.axis_size("dp"), lax.axis_size("ep")
    experts = ranks * cores
    slots = queries.shape[0]
    heads, dim, _ = key_weight.shape
    capacity = slots * routes.shape[1] // experts
    direct = ranks <= DIRECT and capacity % 16 == 0
    index = lax.axis_index("dp") * cores + lax.axis_index("ep")
    me = (index if direct else jnp.int32(0)).astype(jnp.int32).reshape(1)
    shares = [heads * share // sum(CHUNKS) for share in CHUNKS]
    chunks, plan = [], []
    first = 0
    for share in shares:
        outgoing = attend(
            first,
            share,
            me,
            queries,
            key_weight,
            value_weight,
            prefix_latent,
            fresh_latent,
            span_counts,
            prefix_lengths,
            routes,
            experts,
            ranks if direct else 1,
        )
        if direct:
            order = exchange_order(ranks)
            pieces = [outgoing[0]]
            for j in order:
                pieces.append(exchange(outgoing[j], "dp", ranks, j))
            swapped = exchange(pass_on(me, pieces, [0] + order, cores), "ep", cores, 1)
            for at, j in enumerate([0] + order):
                plan.append((len(chunks) + at, (first * dim, 0, j * cores, j * cores)))
                plan.append((len(chunks) + ranks, (first * dim, at * capacity, j * cores + 1, 1)))
            chunks += pieces + [swapped]
        else:
            arrived = lax.all_to_all(
                outgoing[0].reshape(experts, capacity, share * dim),
                ("dp", "ep"),
                split_axis=0,
                concat_axis=0,
                tiled=True,
            )
            chunks.append(arrived.reshape(ranks, cores, capacity, share * dim))
        first += share
    if direct:
        return assemble(me, chunks, plan, (1, ranks, capacity, cores * heads * dim), cores)
    arrived = jnp.concatenate(chunks, axis=3).transpose(0, 2, 1, 3)
    return arrived.reshape(1, ranks, capacity, cores * heads * dim)


def solution(mesh):
    in_specs = (
        P(("groups", "dp"), "ep"),
        P("ep", None, None),
        P("ep", None, None),
        P(("groups", "dp"), None),
        P(("groups", "dp"), None),
        P(("groups", "dp")),
        P(("groups", "dp")),
        P(("groups", "dp"), None),
    )
    out_specs = P(("groups", "dp", "ep"), None, None, None)
    return jax.shard_map(local, mesh=mesh, in_specs=in_specs, out_specs=out_specs, check_vma=False)
```

```python
import functools
import math

import jax
import jax.numpy as jnp
from jax import lax
from jax.experimental import pallas as pl
from jax.experimental.pallas import tpu as pltpu
from jax.sharding import PartitionSpec as P

SPAN = 64
GROUP = 4
CHUNKS = (1, 1)
DIRECT = 16
KEY_PARTS = 2
VMEM = 58 * 1024 * 1024
MASKED = -1e30
OPEN = 3e38
NT = (((1,), (1,)), ((), ()))


def dot(left, right):
    return jnp.dot(left, right, preferred_element_type=jnp.float32)


def build_table(me, count, routes_ref, table_ref, capacity):
    slots = routes_ref.shape[1]
    rows = table_ref.shape[0]
    place = lax.broadcasted_iota(jnp.int32, (rows, slots), 0)
    token = lax.broadcasted_iota(jnp.int32, (rows, slots), 1)
    block = place // capacity
    expert = block ^ me
    hit = ((routes_ref[0:1, :] == expert) | (routes_ref[1:2, :] == expert)) & (
        token < count * SPAN
    )
    hit = jnp.where(hit, jnp.float32(1.0), jnp.float32(0.0))
    first = lax.broadcasted_iota(jnp.int32, (slots, slots), 0)
    second = lax.broadcasted_iota(jnp.int32, (slots, slots), 1)
    earlier = jnp.where(first < second, jnp.float32(1.0), jnp.float32(0.0))
    before = dot(hit.astype(jnp.bfloat16), earlier.astype(jnp.bfloat16))
    wanted = (place - block * capacity).astype(jnp.float32)
    table_ref[...] = jnp.where(before == wanted, hit, jnp.float32(0.0)).astype(jnp.bfloat16)


def attend_kernel(
    capacity,
    first,
    me_ref,
    count_ref,
    size_ref,
    routes_ref,
    queries_hbm,
    key_weight_hbm,
    value_weight_hbm,
    prefix_hbm,
    fresh_hbm,
    *rest,
):
    *out_refs, queries_ref, key_weight_ref, value_weight_ref, keys_ref = rest[:-4]
    cap_ref, table_ref, attended_ref, sem = rest[-4:]
    slots = queries_ref.shape[0]
    past = prefix_hbm.shape[0]
    heads, dim, _ = key_weight_ref.shape
    here = pl.ds(first, heads)
    stacks = heads // GROUP
    part = past // KEY_PARTS

    def copy_stack(source, target, stack, index):
        here, there = pl.ds(stack * GROUP, GROUP), pl.ds(first + stack * GROUP, GROUP)
        return pltpu.make_async_copy(source.at[there], target.at[here], sem.at[index])

    for_queries, for_values = [], []
    for s in range(stacks):
        here, there = pl.ds(s * GROUP * dim, GROUP * dim), pl.ds((first + s * GROUP) * dim, GROUP * dim)
        for_queries += [
            pltpu.make_async_copy(queries_hbm.at[:, there], queries_ref.at[:, here], sem.at[3 * s]),
            copy_stack(key_weight_hbm, key_weight_ref, s, 3 * s + 1),
        ]
        for_values.append(copy_stack(value_weight_hbm, value_weight_ref, s, 3 * s + 2))
    for_keys = [
        pltpu.make_async_copy(
            prefix_hbm.at[pl.ds(i * part, part)],
            keys_ref.at[pl.ds(i * part, part)],
            sem.at[3 * stacks + i],
        )
        for i in range(KEY_PARTS)
    ]
    for_keys.append(
        pltpu.make_async_copy(
            fresh_hbm, keys_ref.at[pl.ds(past, slots)], sem.at[3 * stacks + KEY_PARTS]
        )
    )
    for copy in for_queries[:2] + for_keys + for_queries[2:] + for_values:
        copy.start()

    count, size = count_ref[0], size_ref[0]
    lane = lax.broadcasted_iota(jnp.int32, (slots, past), 1)
    cap_ref[:, :past] = jnp.where(lane < size, jnp.float32(OPEN), jnp.float32(MASKED))
    row = lax.broadcasted_iota(jnp.int32, (slots, slots), 0)
    col = lax.broadcasted_iota(jnp.int32, (slots, slots), 1)
    cap_ref[:, past:] = jnp.where(
        (col <= row) & (col < count * SPAN), jnp.float32(OPEN), jnp.float32(MASKED)
    )
    build_table(me_ref[0], count, routes_ref, table_ref, capacity)

    scale = math.log2(math.e) / math.sqrt(dim)

    def score(stack):
        for copy in for_queries[2 * stack : 2 * stack + 2] + (for_keys if stack == 0 else []):
            copy.wait()
        lifted = []
        for h in range(stack * GROUP, (stack + 1) * GROUP):
            one = dot(queries_ref[:, h * dim : (h + 1) * dim], key_weight_ref[h])
            lifted.append(one.astype(jnp.bfloat16))
        lifted = jnp.concatenate(lifted, axis=0)
        return lax.dot_general(lifted, keys_ref[...], NT, preferred_element_type=jnp.float32)

    def finish(stack, scores):
        keys = keys_ref[...]
        scores = scores.reshape(GROUP, slots, keys.shape[0])
        scores = jnp.minimum(scores, cap_ref[...][None])
        highest = jnp.max(scores, axis=-1, keepdims=True) * scale
        weights = jnp.exp2(scores * scale - highest)
        total = jnp.sum(weights, axis=-1, keepdims=True)
        weights = weights.astype(jnp.bfloat16).reshape(GROUP * slots, keys.shape[0])
        mixed = dot(weights, keys).astype(jnp.bfloat16)
        for g in range(GROUP):
            h = stack * GROUP + g
            projected = dot(mixed[g * slots : (g + 1) * slots], value_weight_ref[h])
            attended_ref[:, h * dim : (h + 1) * dim] = (projected / total[g]).astype(jnp.bfloat16)

    before = score(0)
    for stack in range(1, stacks + 1):
        for_values[stack - 1].wait()
        after = score(stack) if stack < stacks else None
        finish(stack - 1, before)
        before = after
    grouped = dot(table_ref[...], attended_ref[...]).astype(jnp.bfloat16)
    rows = out_refs[0].shape[0]
    for k, out_ref in enumerate(out_refs):
        out_ref[...] = grouped[k * rows : (k + 1) * rows]


def attend(
    first, heads, me, queries, key_weight, value_weight, prefix, fresh, count, size, routes, experts, pieces
):
    slots = queries.shape[0]
    _, dim, latent = key_weight.shape
    places = slots * routes.shape[1]
    keys = prefix.shape[0] + slots
    smem = pl.BlockSpec(memory_space=pltpu.SMEM)
    vmem = pl.BlockSpec(memory_space=pltpu.VMEM)
    hbm = pl.BlockSpec(memory_space=pltpu.HBM)
    piece = (places // pieces, heads * dim)
    return pl.pallas_call(
        functools.partial(attend_kernel, places // experts, first),
        in_specs=[smem, smem, smem, vmem, hbm, hbm, hbm, hbm, hbm],
        out_specs=[vmem] * pieces,
        out_shape=[jax.ShapeDtypeStruct(piece, jnp.bfloat16)] * pieces,
        scratch_shapes=[
            pltpu.VMEM((slots, heads * dim), jnp.bfloat16),
            pltpu.VMEM((heads, dim, latent), jnp.bfloat16),
            pltpu.VMEM((heads, latent, dim), jnp.bfloat16),
            pltpu.VMEM((keys, latent), jnp.bfloat16),
            pltpu.VMEM((slots, keys), jnp.float32),
            pltpu.VMEM((places, slots), jnp.bfloat16),
            pltpu.VMEM((slots, heads * dim), jnp.bfloat16),
            pltpu.SemaphoreType.DMA((3 * heads // GROUP + KEY_PARTS + 1,)),
        ],
        compiler_params=pltpu.CompilerParams(vmem_limit_bytes=VMEM),
        cost_estimate=pl.CostEstimate(
            flops=4 * slots * heads * keys * latent,
            bytes_accessed=4 * heads * dim * latent,
            transcendentals=heads * slots * keys,
        ),
    )(me, count, size, routes.T, queries, key_weight, value_weight, prefix, fresh)


def run_copies(copies):
    for copy in copies:
        copy.start()
    for copy in copies:
        copy.wait()


def pass_on_kernel(cores, *refs):
    *piece_refs, out_ref, sem = refs
    capacity = piece_refs[0].shape[0] // cores
    run_copies(
        [
            pltpu.make_async_copy(
                piece_ref.at[pl.ds(capacity, capacity)],
                out_ref.at[pl.ds(j * capacity, capacity)],
                sem.at[j],
            )
            for j, piece_ref in enumerate(piece_refs)
        ]
    )


def pass_on(pieces, cores):
    rows, width = pieces[0].shape
    return pl.pallas_call(
        functools.partial(pass_on_kernel, cores),
        in_specs=[pl.BlockSpec(memory_space=pl.ANY)] * len(pieces),
        out_specs=pl.BlockSpec(memory_space=pltpu.VMEM),
        out_shape=jax.ShapeDtypeStruct((len(pieces) * rows // cores, width), jnp.bfloat16),
        scratch_shapes=[pltpu.SemaphoreType.DMA((len(pieces),))],
        compiler_params=pltpu.CompilerParams(vmem_limit_bytes=VMEM),
    )(*pieces)


def place_kernel(plan, cores, me_ref, *rest):
    *refs, out_ref, whole_ref, sem = rest
    _, capacity, features = whole_ref.shape
    features //= cores
    me = me_ref[0]
    copies = []
    for i, (ref, (first, start, source)) in enumerate(plan):
        ref = refs[ref]
        width = ref.shape[1]
        who = me ^ source
        left = pl.multiple_of(who % cores * features + first, math.gcd(features, first))
        copies.append(
            pltpu.make_async_copy(
                ref.at[pl.ds(start, capacity)],
                whole_ref.at[who // cores, :, pl.ds(left, width)],
                sem.at[i],
            )
        )
    run_copies(copies)
    run_copies([pltpu.make_async_copy(whole_ref, out_ref.at[0], sem.at[0])])


def assemble(me, arrays, plan, shape, cores):
    return pl.pallas_call(
        functools.partial(place_kernel, plan, cores),
        in_specs=[pl.BlockSpec(memory_space=pltpu.SMEM)]
        + [pl.BlockSpec(memory_space=pl.ANY)] * len(arrays),
        out_specs=pl.BlockSpec(memory_space=pl.ANY),
        out_shape=jax.ShapeDtypeStruct(shape, jnp.bfloat16),
        scratch_shapes=[
            pltpu.VMEM(shape[1:], jnp.bfloat16),
            pltpu.SemaphoreType.DMA((len(plan),)),
        ],
        compiler_params=pltpu.CompilerParams(vmem_limit_bytes=VMEM),
    )(me, *arrays)


def exchange_order(ranks):
    near, far = list(range(1, ranks // 2)), list(range(ranks // 2, ranks))
    far = far[::2] + far[1::2]
    half = len(far) // 2
    return far[:half] + near[:1] + far[half:] + near[1:]


def local(
    queries,
    key_weight,
    value_weight,
    prefix_latent,
    fresh_latent,
    span_counts,
    prefix_lengths,
    routes,
):
    ranks, cores = lax.axis_size("dp"), lax.axis_size("ep")
    experts = ranks * cores
    slots = queries.shape[0]
    heads, dim, _ = key_weight.shape
    capacity = slots * routes.shape[1] // experts
    direct = ranks <= DIRECT and capacity % 16 == 0
    index = lax.axis_index("dp") * cores + lax.axis_index("ep")
    me = (index if direct else jnp.int32(0)).astype(jnp.int32).reshape(1)
    shares = [heads * share // sum(CHUNKS) for share in CHUNKS]
    chunks, plan = [], []
    first = 0
    for share in shares:
        outgoing = attend(
            first,
            share,
            me,
            queries,
            key_weight,
            value_weight,
            prefix_latent,
            fresh_latent,
            span_counts,
            prefix_lengths,
            routes,
            experts,
            ranks if direct else 1,
        )
        if direct:
            order = exchange_order(ranks)
            pieces = [outgoing[0]]
            for j in order:
                pairs = [(i, i ^ j) for i in range(ranks)]
                pieces.append(lax.ppermute(outgoing[j], "dp", pairs))
            swapped = lax.ppermute(
                pass_on(pieces, cores), "ep", [(i, i ^ 1) for i in range(cores)]
            )
            for at, j in enumerate([0] + order):
                plan.append((len(chunks) + at, (first * dim, 0, j * cores)))
                plan.append((len(chunks) + ranks, (first * dim, at * capacity, j * cores + 1)))
            chunks += pieces + [swapped]
        else:
            arrived = lax.all_to_all(
                outgoing[0].reshape(experts, capacity, share * dim),
                ("dp", "ep"),
                split_axis=0,
                concat_axis=0,
                tiled=True,
            )
            chunks.append(arrived.reshape(ranks, cores, capacity, share * dim))
        first += share
    if direct:
        return assemble(me, chunks, plan, (1, ranks, capacity, cores * heads * dim), cores)
    arrived = jnp.concatenate(chunks, axis=3).transpose(0, 2, 1, 3)
    return arrived.reshape(1, ranks, capacity, cores * heads * dim)


def solution(mesh):
    in_specs = (
        P(("groups", "dp"), "ep"),
        P("ep", None, None),
        P("ep", None, None),
        P(("groups", "dp"), None),
        P(("groups", "dp"), None),
        P(("groups", "dp")),
        P(("groups", "dp")),
        P(("groups", "dp"), None),
    )
    out_specs = P(("groups", "dp", "ep"), None, None, None)
    return jax.shard_map(local, mesh=mesh, in_specs=in_specs, out_specs=out_specs, check_vma=False)
```

```python
import functools
import math

import jax
import jax.numpy as jnp
from jax import lax
from jax.experimental import pallas as pl
from jax.experimental.pallas import tpu as pltpu
from jax.sharding import PartitionSpec as P

SPAN = 64
GROUPS = (2, 4)
UNROLL = 2
CHUNKS = (1, 1)
DIRECT = 16
KEY_PARTS = 2
VMEM = 58 * 1024 * 1024
MASKED = -1e30
OPEN = 3e38
NT = (((1,), (1,)), ((), ()))


def dot(left, right):
    return jnp.dot(left, right, preferred_element_type=jnp.float32)


def build_table(me, count, routes_ref, table_ref, capacity):
    slots = routes_ref.shape[1]
    rows = table_ref.shape[0]
    place = lax.broadcasted_iota(jnp.int32, (rows, slots), 0)
    token = lax.broadcasted_iota(jnp.int32, (rows, slots), 1)
    block = place // capacity
    expert = block ^ me
    hit = ((routes_ref[0:1, :] == expert) | (routes_ref[1:2, :] == expert)) & (
        token < count * SPAN
    )
    hit = jnp.where(hit, jnp.float32(1.0), jnp.float32(0.0))
    first = lax.broadcasted_iota(jnp.int32, (slots, slots), 0)
    second = lax.broadcasted_iota(jnp.int32, (slots, slots), 1)
    earlier = jnp.where(first < second, jnp.float32(1.0), jnp.float32(0.0))
    before = dot(hit.astype(jnp.bfloat16), earlier.astype(jnp.bfloat16))
    wanted = (place - block * capacity).astype(jnp.float32)
    table_ref[...] = jnp.where(before == wanted, hit, jnp.float32(0.0)).astype(jnp.bfloat16)


def attend_kernel(
    capacity,
    group,
    first,
    me_ref,
    count_ref,
    size_ref,
    routes_ref,
    queries_hbm,
    key_weight_hbm,
    value_weight_hbm,
    prefix_hbm,
    fresh_hbm,
    *rest,
):
    *out_refs, queries_ref, key_weight_ref, value_weight_ref, keys_ref = rest[:-4]
    cap_ref, table_ref, attended_ref, sem = rest[-4:]
    slots = queries_ref.shape[0]
    past = prefix_hbm.shape[0]
    heads, dim, _ = key_weight_ref.shape
    here = pl.ds(first, heads)
    step = group * UNROLL
    steps = heads // step
    part = past // KEY_PARTS

    def copy_step(i):
        def of(source, target, index):
            here, there = pl.ds(i * step, step), pl.ds(first + i * step, step)
            return pltpu.make_async_copy(source.at[there], target.at[here], sem.at[3 * i + index])

        here, there = pl.ds(i * step * dim, step * dim), pl.ds((first + i * step) * dim, step * dim)
        return [
            pltpu.make_async_copy(queries_hbm.at[:, there], queries_ref.at[:, here], sem.at[3 * i]),
            of(key_weight_hbm, key_weight_ref, 1),
            of(value_weight_hbm, value_weight_ref, 2),
        ]

    for_keys = [
        pltpu.make_async_copy(
            prefix_hbm.at[pl.ds(i * part, part)],
            keys_ref.at[pl.ds(i * part, part)],
            sem.at[3 * steps + i],
        )
        for i in range(KEY_PARTS)
    ]
    for_keys.append(
        pltpu.make_async_copy(
            fresh_hbm, keys_ref.at[pl.ds(past, slots)], sem.at[3 * steps + KEY_PARTS]
        )
    )
    opening = copy_step(0)
    for copy in opening[:2] + for_keys + opening[2:]:
        copy.start()
    for i in range(1, steps):
        for copy in copy_step(i):
            copy.start()

    count, size = count_ref[0], size_ref[0]
    lane = lax.broadcasted_iota(jnp.int32, (slots, past), 1)
    cap_ref[:, :past] = jnp.where(lane < size, jnp.float32(OPEN), jnp.float32(MASKED))
    row = lax.broadcasted_iota(jnp.int32, (slots, slots), 0)
    col = lax.broadcasted_iota(jnp.int32, (slots, slots), 1)
    cap_ref[:, past:] = jnp.where(
        (col <= row) & (col < count * SPAN), jnp.float32(OPEN), jnp.float32(MASKED)
    )
    build_table(me_ref[0], count, routes_ref, table_ref, capacity)

    scale = math.log2(math.e) / math.sqrt(dim)
    for copy in for_keys:
        copy.wait()

    def body(i, carry):
        for copy in copy_step(i):
            copy.wait()
        keys = keys_ref[...]
        scores = []
        for stack in range(UNROLL):
            lifted = []
            for g in range(group):
                h = i * step + stack * group + g
                query = queries_ref[:, pl.ds(pl.multiple_of(h * dim, dim), dim)]
                lifted.append(dot(query, key_weight_ref[h]).astype(jnp.bfloat16))
            lifted = jnp.concatenate(lifted, axis=0)
            scores.append(lax.dot_general(lifted, keys, NT, preferred_element_type=jnp.float32))
        for stack in range(UNROLL):
            score = scores[stack].reshape(group, slots, keys.shape[0])
            score = jnp.minimum(score, cap_ref[...][None])
            highest = jnp.max(score, axis=-1, keepdims=True) * scale
            weights = jnp.exp2(score * scale - highest)
            total = jnp.sum(weights, axis=-1, keepdims=True)
            weights = weights.astype(jnp.bfloat16).reshape(group * slots, keys.shape[0])
            mixed = dot(weights, keys).astype(jnp.bfloat16)
            for g in range(group):
                h = i * step + stack * group + g
                projected = dot(mixed[g * slots : (g + 1) * slots], value_weight_ref[h])
                attended_ref[:, pl.ds(pl.multiple_of(h * dim, dim), dim)] = (
                    projected / total[g]
                ).astype(jnp.bfloat16)
        return carry

    lax.fori_loop(0, steps, body, 0)
    grouped = dot(table_ref[...], attended_ref[...]).astype(jnp.bfloat16)
    rows = out_refs[0].shape[0]
    for k, out_ref in enumerate(out_refs):
        out_ref[...] = grouped[k * rows : (k + 1) * rows]


def attend(
    group,
    first,
    heads,
    me,
    queries,
    key_weight,
    value_weight,
    prefix,
    fresh,
    count,
    size,
    routes,
    experts,
    pieces,
):
    slots = queries.shape[0]
    _, dim, latent = key_weight.shape
    places = slots * routes.shape[1]
    keys = prefix.shape[0] + slots
    smem = pl.BlockSpec(memory_space=pltpu.SMEM)
    vmem = pl.BlockSpec(memory_space=pltpu.VMEM)
    hbm = pl.BlockSpec(memory_space=pltpu.HBM)
    piece = (places // pieces, heads * dim)
    return pl.pallas_call(
        functools.partial(attend_kernel, places // experts, group, first),
        in_specs=[smem, smem, smem, vmem, hbm, hbm, hbm, hbm, hbm],
        out_specs=[vmem] * pieces,
        out_shape=[jax.ShapeDtypeStruct(piece, jnp.bfloat16)] * pieces,
        scratch_shapes=[
            pltpu.VMEM((slots, heads * dim), jnp.bfloat16),
            pltpu.VMEM((heads, dim, latent), jnp.bfloat16),
            pltpu.VMEM((heads, latent, dim), jnp.bfloat16),
            pltpu.VMEM((keys, latent), jnp.bfloat16),
            pltpu.VMEM((slots, keys), jnp.float32),
            pltpu.VMEM((places, slots), jnp.bfloat16),
            pltpu.VMEM((slots, heads * dim), jnp.bfloat16),
            pltpu.SemaphoreType.DMA((3 * heads // (group * UNROLL) + KEY_PARTS + 1,)),
        ],
        compiler_params=pltpu.CompilerParams(vmem_limit_bytes=VMEM),
        cost_estimate=pl.CostEstimate(
            flops=4 * slots * heads * keys * latent,
            bytes_accessed=4 * heads * dim * latent,
            transcendentals=heads * slots * keys,
        ),
    )(me, count, size, routes.T, queries, key_weight, value_weight, prefix, fresh)


def run_copies(copies):
    for copy in copies:
        copy.start()
    for copy in copies:
        copy.wait()


def pass_on_kernel(cores, *refs):
    *piece_refs, out_ref, sem = refs
    capacity = piece_refs[0].shape[0] // cores
    run_copies(
        [
            pltpu.make_async_copy(
                piece_ref.at[pl.ds(capacity, capacity)],
                out_ref.at[pl.ds(j * capacity, capacity)],
                sem.at[j],
            )
            for j, piece_ref in enumerate(piece_refs)
        ]
    )


def pass_on(pieces, cores):
    rows, width = pieces[0].shape
    return pl.pallas_call(
        functools.partial(pass_on_kernel, cores),
        in_specs=[pl.BlockSpec(memory_space=pl.ANY)] * len(pieces),
        out_specs=pl.BlockSpec(memory_space=pltpu.VMEM),
        out_shape=jax.ShapeDtypeStruct((len(pieces) * rows // cores, width), jnp.bfloat16),
        scratch_shapes=[pltpu.SemaphoreType.DMA((len(pieces),))],
        compiler_params=pltpu.CompilerParams(vmem_limit_bytes=VMEM),
    )(*pieces)


def place_kernel(plan, cores, me_ref, *rest):
    *refs, out_ref, whole_ref, sem = rest
    _, capacity, features = whole_ref.shape
    features //= cores
    me = me_ref[0]
    copies = []
    for i, (ref, (first, start, source)) in enumerate(plan):
        ref = refs[ref]
        width = ref.shape[1]
        who = me ^ source
        left = pl.multiple_of(who % cores * features + first, math.gcd(features, first))
        copies.append(
            pltpu.make_async_copy(
                ref.at[pl.ds(start, capacity)],
                whole_ref.at[who // cores, :, pl.ds(left, width)],
                sem.at[i],
            )
        )
    run_copies(copies)
    run_copies([pltpu.make_async_copy(whole_ref, out_ref.at[0], sem.at[0])])


def assemble(me, arrays, plan, shape, cores):
    return pl.pallas_call(
        functools.partial(place_kernel, plan, cores),
        in_specs=[pl.BlockSpec(memory_space=pltpu.SMEM)]
        + [pl.BlockSpec(memory_space=pl.ANY)] * len(arrays),
        out_specs=pl.BlockSpec(memory_space=pl.ANY),
        out_shape=jax.ShapeDtypeStruct(shape, jnp.bfloat16),
        scratch_shapes=[
            pltpu.VMEM(shape[1:], jnp.bfloat16),
            pltpu.SemaphoreType.DMA((len(plan),)),
        ],
        compiler_params=pltpu.CompilerParams(vmem_limit_bytes=VMEM),
    )(me, *arrays)


def exchange_order(ranks):
    near, far = list(range(1, ranks // 2)), list(range(ranks // 2, ranks))
    far = far[::2] + far[1::2]
    half = len(far) // 2
    return far[:half] + near[:1] + far[half:] + near[1:]


def local(
    queries,
    key_weight,
    value_weight,
    prefix_latent,
    fresh_latent,
    span_counts,
    prefix_lengths,
    routes,
):
    ranks, cores = lax.axis_size("dp"), lax.axis_size("ep")
    experts = ranks * cores
    slots = queries.shape[0]
    heads, dim, _ = key_weight.shape
    capacity = slots * routes.shape[1] // experts
    direct = ranks <= DIRECT and capacity % 16 == 0
    index = lax.axis_index("dp") * cores + lax.axis_index("ep")
    me = (index if direct else jnp.int32(0)).astype(jnp.int32).reshape(1)
    shares = [heads * share // sum(CHUNKS) for share in CHUNKS]
    chunks, plan = [], []
    first = 0
    for group, share in zip(GROUPS, shares):
        outgoing = attend(
            group,
            first,
            share,
            me,
            queries,
            key_weight,
            value_weight,
            prefix_latent,
            fresh_latent,
            span_counts,
            prefix_lengths,
            routes,
            experts,
            ranks if direct else 1,
        )
        if direct:
            order = exchange_order(ranks)
            pieces = [outgoing[0]]
            for j in order:
                pairs = [(i, i ^ j) for i in range(ranks)]
                pieces.append(lax.ppermute(outgoing[j], "dp", pairs))
            swapped = lax.ppermute(
                pass_on(pieces, cores), "ep", [(i, i ^ 1) for i in range(cores)]
            )
            for at, j in enumerate([0] + order):
                plan.append((len(chunks) + at, (first * dim, 0, j * cores)))
                plan.append((len(chunks) + ranks, (first * dim, at * capacity, j * cores + 1)))
            chunks += pieces + [swapped]
        else:
            arrived = lax.all_to_all(
                outgoing[0].reshape(experts, capacity, share * dim),
                ("dp", "ep"),
                split_axis=0,
                concat_axis=0,
                tiled=True,
            )
            chunks.append(arrived.reshape(ranks, cores, capacity, share * dim))
        first += share
    if direct:
        return assemble(me, chunks, plan, (1, ranks, capacity, cores * heads * dim), cores)
    arrived = jnp.concatenate(chunks, axis=3).transpose(0, 2, 1, 3)
    return arrived.reshape(1, ranks, capacity, cores * heads * dim)


def solution(mesh):
    in_specs = (
        P(("groups", "dp"), "ep"),
        P("ep", None, None),
        P("ep", None, None),
        P(("groups", "dp"), None),
        P(("groups", "dp"), None),
        P(("groups", "dp")),
        P(("groups", "dp")),
        P(("groups", "dp"), None),
    )
    out_specs = P(("groups", "dp", "ep"), None, None, None)
    return jax.shard_map(local, mesh=mesh, in_specs=in_specs, out_specs=out_specs, check_vma=False)
```

```python
import functools
import math

import jax
import jax.numpy as jnp
from jax import lax
from jax.experimental import pallas as pl
from jax.experimental.pallas import tpu as pltpu
from jax.sharding import PartitionSpec as P

SPAN = 64
STACKS = ((2, 2), (1, 4))
CHUNKS = (1, 1)
DIRECT = 16
KEY_PARTS = 2
VMEM = 58 * 1024 * 1024
SHORT = pl.CostEstimate(flops=0, bytes_accessed=0, transcendentals=0)
MASKED = -1e30
OPEN = 3e38
NT = (((1,), (1,)), ((), ()))


def dot(left, right):
    return jnp.dot(left, right, preferred_element_type=jnp.float32)


def build_table(me, count, routes_ref, table_ref, capacity):
    slots = routes_ref.shape[1]
    rows = table_ref.shape[0]
    place = lax.broadcasted_iota(jnp.int32, (rows, slots), 0)
    token = lax.broadcasted_iota(jnp.int32, (rows, slots), 1)
    block = place // capacity
    expert = block ^ me
    hit = ((routes_ref[0:1, :] == expert) | (routes_ref[1:2, :] == expert)) & (
        token < count * SPAN
    )
    hit = jnp.where(hit, jnp.float32(1.0), jnp.float32(0.0))
    first = lax.broadcasted_iota(jnp.int32, (slots, slots), 0)
    second = lax.broadcasted_iota(jnp.int32, (slots, slots), 1)
    earlier = jnp.where(first < second, jnp.float32(1.0), jnp.float32(0.0))
    before = dot(hit.astype(jnp.bfloat16), earlier.astype(jnp.bfloat16))
    wanted = (place - block * capacity).astype(jnp.float32)
    table_ref[...] = jnp.where(before == wanted, hit, jnp.float32(0.0)).astype(jnp.bfloat16)


def attend_kernel(
    capacity,
    group,
    unroll,
    first,
    me_ref,
    count_ref,
    size_ref,
    routes_ref,
    queries_hbm,
    key_weight_hbm,
    value_weight_hbm,
    prefix_hbm,
    fresh_hbm,
    *rest,
):
    *out_refs, queries_ref, key_weight_ref, value_weight_ref, keys_ref = rest[:-4]
    cap_ref, table_ref, attended_ref, sem = rest[-4:]
    slots = queries_ref.shape[0]
    past = prefix_hbm.shape[0]
    heads, dim, _ = key_weight_ref.shape
    here = pl.ds(first, heads)
    step = group * unroll
    steps = heads // step
    part = past // KEY_PARTS

    def copy_step(i):
        def of(source, target, index):
            here, there = pl.ds(i * step, step), pl.ds(first + i * step, step)
            return pltpu.make_async_copy(source.at[there], target.at[here], sem.at[3 * i + index])

        here, there = pl.ds(i * step * dim, step * dim), pl.ds((first + i * step) * dim, step * dim)
        return [
            pltpu.make_async_copy(queries_hbm.at[:, there], queries_ref.at[:, here], sem.at[3 * i]),
            of(key_weight_hbm, key_weight_ref, 1),
            of(value_weight_hbm, value_weight_ref, 2),
        ]

    for_keys = [
        pltpu.make_async_copy(
            prefix_hbm.at[pl.ds(i * part, part)],
            keys_ref.at[pl.ds(i * part, part)],
            sem.at[3 * steps + i],
        )
        for i in range(KEY_PARTS)
    ]
    for_keys.append(
        pltpu.make_async_copy(
            fresh_hbm, keys_ref.at[pl.ds(past, slots)], sem.at[3 * steps + KEY_PARTS]
        )
    )
    opening = copy_step(0)
    for copy in opening[:2] + for_keys + opening[2:]:
        copy.start()

    count, size = count_ref[0], size_ref[0]
    lane = lax.broadcasted_iota(jnp.int32, (slots, past), 1)
    cap_ref[:, :past] = jnp.where(lane < size, jnp.float32(OPEN), jnp.float32(MASKED))
    row = lax.broadcasted_iota(jnp.int32, (slots, slots), 0)
    col = lax.broadcasted_iota(jnp.int32, (slots, slots), 1)
    cap_ref[:, past:] = jnp.where(
        (col <= row) & (col < count * SPAN), jnp.float32(OPEN), jnp.float32(MASKED)
    )
    build_table(me_ref[0], count, routes_ref, table_ref, capacity)

    scale = math.log2(math.e) / math.sqrt(dim)
    for copy in opening[:2] + for_keys:
        copy.wait()
    for i in range(1, steps):
        for copy in copy_step(i):
            copy.start()
    opening[2].wait()

    def body(i, carry):
        @pl.when(i > 0)
        def _():
            for copy in copy_step(i):
                copy.wait()

        keys = keys_ref[...]
        scores = []
        for stack in range(unroll):
            lifted = []
            for g in range(group):
                h = i * step + stack * group + g
                query = queries_ref[:, pl.ds(pl.multiple_of(h * dim, dim), dim)]
                lifted.append(dot(query, key_weight_ref[h]).astype(jnp.bfloat16))
            lifted = jnp.concatenate(lifted, axis=0)
            scores.append(lax.dot_general(lifted, keys, NT, preferred_element_type=jnp.float32))
        for stack in range(unroll):
            score = scores[stack].reshape(group, slots, keys.shape[0])
            score = jnp.minimum(score, cap_ref[...][None])
            highest = jnp.max(score, axis=-1, keepdims=True) * scale
            weights = jnp.exp2(score * scale - highest)
            total = jnp.sum(weights, axis=-1, keepdims=True)
            weights = weights.astype(jnp.bfloat16).reshape(group * slots, keys.shape[0])
            mixed = dot(weights, keys).astype(jnp.bfloat16)
            for g in range(group):
                h = i * step + stack * group + g
                projected = dot(mixed[g * slots : (g + 1) * slots], value_weight_ref[h])
                attended_ref[:, pl.ds(pl.multiple_of(h * dim, dim), dim)] = (
                    projected / total[g]
                ).astype(jnp.bfloat16)
        return carry

    lax.fori_loop(0, steps, body, 0)
    grouped = dot(table_ref[...], attended_ref[...]).astype(jnp.bfloat16)
    row = 0
    for out_ref in out_refs:
        out_ref[...] = grouped[row : row + out_ref.shape[0]]
        row += out_ref.shape[0]


def attend(
    group,
    unroll,
    first,
    heads,
    me,
    queries,
    key_weight,
    value_weight,
    prefix,
    fresh,
    count,
    size,
    routes,
    experts,
    parts,
):
    slots = queries.shape[0]
    _, dim, latent = key_weight.shape
    places = slots * routes.shape[1]
    keys = prefix.shape[0] + slots
    smem = pl.BlockSpec(memory_space=pltpu.SMEM)
    vmem = pl.BlockSpec(memory_space=pltpu.VMEM)
    hbm = pl.BlockSpec(memory_space=pltpu.HBM)
    pieces = [(rows, heads * dim) for rows in parts]
    return pl.pallas_call(
        functools.partial(attend_kernel, places // experts, group, unroll, first),
        in_specs=[smem, smem, smem, vmem] + [hbm] * 5,
        out_specs=[vmem] * len(pieces),
        out_shape=[jax.ShapeDtypeStruct(piece, jnp.bfloat16) for piece in pieces],
        scratch_shapes=[
            pltpu.VMEM((slots, heads * dim), jnp.bfloat16),
            pltpu.VMEM((heads, dim, latent), jnp.bfloat16),
            pltpu.VMEM((heads, latent, dim), jnp.bfloat16),
            pltpu.VMEM((keys, latent), jnp.bfloat16),
            pltpu.VMEM((slots, keys), jnp.float32),
            pltpu.VMEM((places, slots), jnp.bfloat16),
            pltpu.VMEM((slots, heads * dim), jnp.bfloat16),
            pltpu.SemaphoreType.DMA((3 * heads // (group * unroll) + KEY_PARTS + 1,)),
        ],
        compiler_params=pltpu.CompilerParams(vmem_limit_bytes=VMEM),
        cost_estimate=SHORT,
    )(me, count, size, routes.T, queries, key_weight, value_weight, prefix, fresh)


def run_copies(copies):
    for copy in copies:
        copy.start()
    for copy in copies:
        copy.wait()


def pass_on_kernel(cores, *refs):
    *piece_refs, out_ref, sem = refs
    capacity = piece_refs[0].shape[0] // cores
    copies = []
    for i, piece_ref in enumerate(piece_refs):
        target = out_ref.at[pl.ds(i * capacity, capacity)]
        copies.append(
            pltpu.make_async_copy(piece_ref.at[pl.ds(capacity, capacity)], target, sem.at[i])
        )
    run_copies(copies)


def pass_on(pieces, cores):
    rows, width = pieces[0].shape
    return pl.pallas_call(
        functools.partial(pass_on_kernel, cores),
        in_specs=[pl.BlockSpec(memory_space=pltpu.VMEM)] * len(pieces),
        out_specs=pl.BlockSpec(memory_space=pl.ANY),
        out_shape=jax.ShapeDtypeStruct((len(pieces) * rows // cores, width), jnp.bfloat16),
        scratch_shapes=[pltpu.SemaphoreType.DMA((len(pieces),))],
        compiler_params=pltpu.CompilerParams(vmem_limit_bytes=VMEM),
        cost_estimate=SHORT,
    )(*pieces)


def place_kernel(first, order, cores, me_ref, *refs):
    *piece_refs, swapped_ref = refs[: len(order) + 1]
    out_ref, sem = refs[-2:]
    me = me_ref[0]
    _, _, capacity, features = out_ref.shape
    features //= cores
    width = swapped_ref.shape[1]
    copies = []
    for i, (j, piece_ref) in enumerate(zip(order, piece_refs)):
        rows = swapped_ref.at[pl.ds(i * capacity, capacity)]
        for core, ref in enumerate((piece_ref.at[pl.ds(0, capacity)], rows)):
            who = me ^ (j * cores + core)
            left = pl.multiple_of(who % cores * features + first, math.gcd(features, first))
            target = out_ref.at[0, who // cores, :, pl.ds(left, width)]
            copies.append(pltpu.make_async_copy(ref, target, sem.at[len(copies)]))
    run_copies(copies)


def place(me, pieces, swapped, first, order, cores, shape, placed):
    anywhere = pl.BlockSpec(memory_space=pl.ANY)
    operands = [me, *pieces, swapped] + placed
    return pl.pallas_call(
        functools.partial(place_kernel, first, order, cores),
        in_specs=[pl.BlockSpec(memory_space=pltpu.SMEM)]
        + [pl.BlockSpec(memory_space=pltpu.VMEM)] * (len(pieces) + 1)
        + [anywhere] * len(placed),
        out_specs=anywhere,
        out_shape=jax.ShapeDtypeStruct(shape, jnp.bfloat16),
        scratch_shapes=[pltpu.SemaphoreType.DMA((2 * len(pieces),))],
        input_output_aliases={len(operands) - 1: 0} if placed else {},
        compiler_params=pltpu.CompilerParams(vmem_limit_bytes=VMEM),
        cost_estimate=SHORT,
    )(*operands)


def exchange_order(ranks):
    near, far = list(range(1, ranks // 2)), list(range(ranks // 2, ranks))
    far = far[::2] + far[1::2]
    half = len(far) // 2
    return far[:half] + near[:1] + far[half:] + near[1:]


def local(
    queries,
    key_weight,
    value_weight,
    prefix_latent,
    fresh_latent,
    span_counts,
    prefix_lengths,
    routes,
):
    ranks, cores = lax.axis_size("dp"), lax.axis_size("ep")
    experts = ranks * cores
    slots = queries.shape[0]
    heads, dim, _ = key_weight.shape
    capacity = slots * routes.shape[1] // experts
    direct = ranks <= DIRECT and capacity % 16 == 0
    index = lax.axis_index("dp") * cores + lax.axis_index("ep")
    me = (index if direct else jnp.int32(0)).astype(jnp.int32).reshape(1)
    shares = [heads * share // sum(CHUNKS) for share in CHUNKS]
    sent, start = [], 0
    for (group, unroll), share in zip(STACKS, shares):
        outgoing = attend(
            group,
            unroll,
            start,
            share,
            me,
            queries,
            key_weight,
            value_weight,
            prefix_latent,
            fresh_latent,
            span_counts,
            prefix_lengths,
            routes,
            experts,
            [cores * capacity] * ranks if direct else [experts * capacity],
        )
        sent.append(outgoing)
        start += share
    if not direct:
        arrays = []
        for (outgoing,) in sent:
            arrived = lax.all_to_all(
                outgoing.reshape(experts, capacity, -1),
                ("dp", "ep"),
                split_axis=0,
                concat_axis=0,
                tiled=True,
            )
            arrays.append(arrived.reshape(ranks, cores, capacity, -1))
        arrived = jnp.concatenate(arrays, axis=3).transpose(0, 2, 1, 3)
        return arrived.reshape(1, ranks, capacity, cores * heads * dim)
    order = exchange_order(ranks)
    shape = (1, ranks, capacity, cores * heads * dim)
    placed, start = [], 0
    for outgoing, share in zip(sent, shares):
        pieces = [outgoing[0]]
        for j in order:
            pairs = [(i, i ^ j) for i in range(ranks)]
            pieces.append(lax.ppermute(outgoing[j], "dp", pairs))
        swapped = lax.ppermute(pass_on(pieces, cores), "ep", [(i, i ^ 1) for i in range(cores)])
        placed = [place(me, pieces, swapped, start * dim, [0] + order, cores, shape, placed)]
        start += share
    return placed[0]


def solution(mesh):
    in_specs = (
        P(("groups", "dp"), "ep"),
        P("ep", None, None),
        P("ep", None, None),
        P(("groups", "dp"), None),
        P(("groups", "dp"), None),
        P(("groups", "dp")),
        P(("groups", "dp")),
        P(("groups", "dp"), None),
    )
    out_specs = P(("groups", "dp", "ep"), None, None, None)
    return jax.shard_map(local, mesh=mesh, in_specs=in_specs, out_specs=out_specs, check_vma=False)
```

```python
import functools
import math

import jax
import jax.numpy as jnp
from jax import lax
from jax.experimental import pallas as pl
from jax.experimental.pallas import tpu as pltpu
from jax.sharding import PartitionSpec as P

SPAN = 64
STACKS = (4, 4)
UNROLL = 2
CHUNKS = (3, 5)
DIRECT = 16
VMEM = 60 * 1024 * 1024
RESIDENT = 40 * 1024 * 1024
SHORT = pl.CostEstimate(flops=0, bytes_accessed=0, transcendentals=0)
MASKED = -1e30
OPEN = 3e38
NT = (((1,), (1,)), ((), ()))


def dot(left, right):
    return jnp.dot(left, right, preferred_element_type=jnp.float32)


def build_table(me, count, routes_ref, table_ref, capacity):
    slots = routes_ref.shape[1]
    rows = table_ref.shape[0]
    place = lax.broadcasted_iota(jnp.int32, (rows, slots), 0)
    token = lax.broadcasted_iota(jnp.int32, (rows, slots), 1)
    block = place // capacity
    side = rows // capacity // 2
    expert = jnp.where(block < side, me // side * side + block, block ^ me)
    hit = ((routes_ref[0:1, :] == expert) | (routes_ref[1:2, :] == expert)) & (
        token < count * SPAN
    )
    hit = jnp.where(hit, jnp.float32(1.0), jnp.float32(0.0))
    first = lax.broadcasted_iota(jnp.int32, (slots, slots), 0)
    second = lax.broadcasted_iota(jnp.int32, (slots, slots), 1)
    earlier = jnp.where(first < second, jnp.float32(1.0), jnp.float32(0.0))
    before = dot(hit.astype(jnp.bfloat16), earlier.astype(jnp.bfloat16))
    wanted = (place - block * capacity).astype(jnp.float32)
    table_ref[...] = jnp.where(before == wanted, hit, jnp.float32(0.0)).astype(jnp.bfloat16)


def attend_kernel(
    capacity,
    stack,
    first,
    heads,
    earlier,
    after,
    resident,
    me_ref,
    count_ref,
    size_ref,
    routes_ref,
    queries_ref,
    key_weight_ref,
    value_weight_ref,
    prefix_ref,
    fresh_ref,
    *rest,
):
    earlier_refs, rest = rest[:earlier], rest[earlier + after :]
    *out_refs, queries_own, key_weight_own, value_weight_own, keys_ref = rest[:-4]
    cap_ref, table_ref, attended_ref, sem = rest[-4:]
    slots = queries_ref.shape[0]
    past = prefix_ref.shape[0]
    dim = key_weight_ref.shape[1]
    steps = heads // stack

    copies = []

    def start_copy(source, target):
        copies.append(pltpu.make_async_copy(source, target, sem.at[len(copies)]))
        copies[-1].start()

    if not resident:
        here = pl.ds(first, heads)
        start_copy(queries_ref.at[:, pl.ds(first * dim, heads * dim)], queries_own)
        start_copy(key_weight_ref.at[here], key_weight_own)
        start_copy(prefix_ref, keys_ref.at[pl.ds(0, past)])
        start_copy(fresh_ref, keys_ref.at[pl.ds(past, slots)])
        start_copy(value_weight_ref.at[here], value_weight_own)
        queries_ref, key_weight_ref, value_weight_ref = queries_own, key_weight_own, value_weight_own
        first = 0
    own = len(copies)
    for piece_ref in earlier_refs:
        start_copy(piece_ref, out_refs[0].at[:, pl.ds(0, piece_ref.shape[1])])
    if resident:
        keys_ref[:past] = prefix_ref[...]
        keys_ref[past:] = fresh_ref[...]

    count, size = count_ref[0], size_ref[0]
    lane = lax.broadcasted_iota(jnp.int32, (slots, past), 1)
    cap_ref[:, :past] = jnp.where(lane < size, jnp.float32(OPEN), jnp.float32(MASKED))
    row = lax.broadcasted_iota(jnp.int32, (slots, slots), 0)
    col = lax.broadcasted_iota(jnp.int32, (slots, slots), 1)
    cap_ref[:, past:] = jnp.where(
        (col <= row) & (col < count * SPAN), jnp.float32(OPEN), jnp.float32(MASKED)
    )
    build_table(me_ref[0], count, routes_ref, table_ref, capacity)
    for copy in copies[:own]:
        copy.wait()

    scale = math.log2(math.e) / math.sqrt(dim)

    def columns(h):
        return pl.ds(pl.multiple_of(h * dim, dim), dim)

    def body(i, carry):
        keys = keys_ref[...]
        lifted = []
        for g in range(stack):
            h = first + i * stack + g
            one = dot(queries_ref[:, columns(h)], key_weight_ref[h])
            lifted.append(one.astype(jnp.bfloat16))
        lifted = jnp.concatenate(lifted, axis=0)
        score = lax.dot_general(lifted, keys, NT, preferred_element_type=jnp.float32)
        score = score.reshape(stack, slots, keys.shape[0])
        score = jnp.minimum(score, cap_ref[...][None])
        highest = jnp.max(score, axis=-1, keepdims=True) * scale
        weights = jnp.exp2(score * scale - highest)
        total = jnp.sum(weights, axis=-1, keepdims=True)
        weights = weights.astype(jnp.bfloat16).reshape(stack * slots, keys.shape[0])
        mixed = dot(weights, keys).astype(jnp.bfloat16)
        for g in range(stack):
            h = i * stack + g
            projected = dot(mixed[g * slots : (g + 1) * slots], value_weight_ref[first + h])
            attended_ref[:, columns(h)] = (projected / total[g]).astype(jnp.bfloat16)
        return carry

    lax.fori_loop(0, steps, body, 0, unroll=min(steps, UNROLL))
    grouped = dot(table_ref[...], attended_ref[...]).astype(jnp.bfloat16)
    row = 0
    for out_ref in out_refs:
        rows, width = out_ref.shape
        out_ref[:, width - heads * dim :] = grouped[row : row + rows]
        row += rows
    for copy in copies[own:]:
        copy.wait()


def attend(
    stack, first, heads, me, queries, key_weight, value_weight, prefix, fresh, count, size, routes, experts, parts, earlier, after
):
    slots = queries.shape[0]
    _, dim, latent = key_weight.shape
    places = slots * routes.shape[1]
    keys = prefix.shape[0] + slots
    resident = first > 0
    smem = pl.BlockSpec(memory_space=pltpu.SMEM)
    vmem = pl.BlockSpec(memory_space=pltpu.VMEM)
    hbm = pl.BlockSpec(memory_space=pltpu.HBM)
    pieces = [(rows, heads * dim) for rows in parts]
    if earlier:
        pieces[0] = (parts[0], heads * dim + earlier[0].shape[1])
    own = 0 if resident else heads
    return pl.pallas_call(
        functools.partial(
            attend_kernel,
            places // experts,
            stack,
            first,
            heads,
            len(earlier),
            len(after),
            resident,
        ),
        in_specs=[smem, smem, smem, vmem] + [vmem if resident else hbm] * 5 + [hbm] * len(earlier + after),
        out_specs=[vmem] * len(pieces),
        out_shape=[jax.ShapeDtypeStruct(piece, jnp.bfloat16) for piece in pieces],
        scratch_shapes=[
            pltpu.VMEM((slots, max(own, 1) * dim), jnp.bfloat16),
            pltpu.VMEM((max(own, 1), dim, latent), jnp.bfloat16),
            pltpu.VMEM((max(own, 1), latent, dim), jnp.bfloat16),
            pltpu.VMEM((keys, latent), jnp.bfloat16),
            pltpu.VMEM((slots, keys), jnp.float32),
            pltpu.VMEM((places, slots), jnp.bfloat16),
            pltpu.VMEM((slots, heads * dim), jnp.bfloat16),
            pltpu.SemaphoreType.DMA((5 + len(earlier),)),
        ],
        compiler_params=pltpu.CompilerParams(vmem_limit_bytes=RESIDENT if resident else VMEM),
        cost_estimate=SHORT,
    )(me, count, size, routes.T, queries, key_weight, value_weight, prefix, fresh, *earlier, *after)


def run_copies(copies):
    for copy in copies:
        copy.start()
    for copy in copies:
        copy.wait()


def pass_on_kernel(count, cores, *refs):
    piece_refs, out_ref = refs[-1 - count : -1], refs[-1]
    capacity = piece_refs[0].shape[0] // cores
    for i, piece_ref in enumerate(piece_refs):
        out_ref[i * capacity : (i + 1) * capacity] = piece_ref[capacity:]


def pass_on(pieces, after, cores):
    rows, width = pieces[0].shape
    vmem = pl.BlockSpec(memory_space=pltpu.VMEM)
    return pl.pallas_call(
        functools.partial(pass_on_kernel, len(pieces), cores),
        in_specs=[pl.BlockSpec(memory_space=pl.ANY)] * len(after) + [vmem] * len(pieces),
        out_specs=vmem,
        out_shape=jax.ShapeDtypeStruct((len(pieces) * rows // cores, width), jnp.bfloat16),
        compiler_params=pltpu.CompilerParams(vmem_limit_bytes=RESIDENT),
        cost_estimate=SHORT,
    )(*after, *pieces)


def place_kernel(plan, cores, me_ref, *refs):
    out_ref, mark_ref, sem = refs[-3:]
    mark_ref[...] = jnp.zeros_like(mark_ref)
    me = me_ref[0]
    _, _, capacity, features = out_ref.shape
    features //= cores
    copies = []
    for ref, row, start, width, bits, side in plan:
        who = me // side * side + bits if side else me ^ bits
        left = pl.multiple_of(who % cores * features + start, math.gcd(features, start))
        target = out_ref.at[0, who // cores, :, pl.ds(left, width)]
        source = refs[ref].at[pl.ds(row, capacity)]
        copies.append(pltpu.make_async_copy(source, target, sem.at[len(copies)]))
    run_copies(copies)


def place(me, arrays, plan, cores, shape, placed):
    anywhere = pl.BlockSpec(memory_space=pl.ANY)
    operands = [me, *arrays] + placed
    return pl.pallas_call(
        functools.partial(place_kernel, plan, cores),
        in_specs=[pl.BlockSpec(memory_space=pltpu.SMEM)]
        + [pl.BlockSpec(memory_space=pltpu.VMEM)] * len(arrays)
        + [anywhere] * len(placed),
        out_specs=[anywhere, pl.BlockSpec(memory_space=pltpu.VMEM)],
        out_shape=[
            jax.ShapeDtypeStruct(shape, jnp.bfloat16),
            jax.ShapeDtypeStruct((8, 128), jnp.float32),
        ],
        scratch_shapes=[pltpu.SemaphoreType.DMA((len(plan),))],
        input_output_aliases={len(operands) - 1: 0} if placed else {},
        compiler_params=pltpu.CompilerParams(vmem_limit_bytes=RESIDENT),
        cost_estimate=SHORT,
    )(*operands)


def local(
    queries,
    key_weight,
    value_weight,
    prefix_latent,
    fresh_latent,
    span_counts,
    prefix_lengths,
    routes,
):
    ranks, cores = lax.axis_size("dp"), lax.axis_size("ep")
    experts = ranks * cores
    slots = queries.shape[0]
    heads, dim, _ = key_weight.shape
    capacity = slots * routes.shape[1] // experts
    direct = ranks <= DIRECT and capacity % 16 == 0
    index = lax.axis_index("dp") * cores + lax.axis_index("ep")
    me = (index if direct else jnp.int32(0)).astype(jnp.int32).reshape(1)
    shares = [heads * share // sum(CHUNKS) for share in CHUNKS]
    far = list(range(ranks // 2, ranks, 2)) + list(range(ranks // 2 + 1, ranks, 2))
    side = experts // 2
    starts = [0]
    for share in shares:
        starts.append(starts[-1] + share)

    def run(chunk, earlier, after):
        return attend(
            STACKS[chunk],
            starts[chunk],
            shares[chunk],
            me,
            queries,
            key_weight,
            value_weight,
            prefix_latent,
            fresh_latent,
            span_counts,
            prefix_lengths,
            routes,
            experts,
            [side * capacity] + [cores * capacity] * len(far) if direct else [experts * capacity],
            earlier,
            after,
        )

    if not direct:
        arrays = []
        for chunk in range(len(shares)):
            arrived = lax.all_to_all(
                run(chunk, [], [])[0].reshape(experts, capacity, -1),
                ("dp", "ep"),
                split_axis=0,
                concat_axis=0,
                tiled=True,
            )
            arrays.append(arrived.reshape(ranks, cores, capacity, -1))
        arrived = jnp.concatenate(arrays, axis=3).transpose(0, 2, 1, 3)
        return arrived.reshape(1, ranks, capacity, cores * heads * dim)

    def to_chip(piece, j):
        return lax.ppermute(piece, "dp", [(i, i ^ j) for i in range(ranks)])

    def to_core(piece):
        return lax.ppermute(piece, "ep", [(i, i ^ 1) for i in range(cores)])

    def far_pieces(outgoing):
        return [to_chip(outgoing[1 + j - ranks // 2], j) for j in far]

    first = run(0, [], [])
    first_far = far_pieces(first)
    last = run(1, first[:1], first[1:2])
    last_far = far_pieces(last)
    near = lax.all_to_all(
        last[0].reshape(side, capacity, -1),
        ("dp", "ep"),
        split_axis=0,
        concat_axis=0,
        axis_index_groups=[list(range(i, i + side)) for i in range(0, experts, side)],
        tiled=True,
    ).reshape(side * capacity, -1)
    first_message = pass_on(first_far, last[1:2], cores)
    first_swapped = to_core(first_message)

    def plan_of(at, start, width):
        plan = []
        for i, j in enumerate(far):
            plan.append((at + i, 0, start, width, j * cores, 0))
            plan.append((at + len(far), i * capacity, start, width, j * cores + 1, 0))
        return plan

    shape = (1, ranks, capacity, cores * heads * dim)
    middle = shares[0] * dim
    plan = plan_of(0, 0, middle)
    plan += [(len(far) + 1, i * capacity, 0, heads * dim, i, side) for i in range(side)]
    placed, mark = place(me, first_far + [first_swapped, near], plan, cores, shape, [])
    last_swapped = to_core(pass_on(last_far, [mark], cores))
    plan = plan_of(0, middle, shares[1] * dim)
    return place(me, last_far + [last_swapped], plan, cores, shape, [placed])[0]


def solution(mesh):
    in_specs = (
        P(("groups", "dp"), "ep"),
        P("ep", None, None),
        P("ep", None, None),
        P(("groups", "dp"), None),
        P(("groups", "dp"), None),
        P(("groups", "dp")),
        P(("groups", "dp")),
        P(("groups", "dp"), None),
    )
    out_specs = P(("groups", "dp", "ep"), None, None, None)
    return jax.shard_map(local, mesh=mesh, in_specs=in_specs, out_specs=out_specs, check_vma=False)
```

```python
import functools
import math

import jax
import jax.numpy as jnp
from jax import lax
from jax.experimental import pallas as pl
from jax.experimental.pallas import tpu as pltpu
from jax.sharding import PartitionSpec as P

SPAN = 64
STACK = 4
CHUNKS = (2, 3, 3)
VMEM = 60 * 1024 * 1024
SHORT = pl.CostEstimate(flops=0, bytes_accessed=0, transcendentals=0)
MASKED = -1e30
OPEN = 3e38
NT = (((1,), (1,)), ((), ()))


def dot(left, right):
    return jnp.dot(left, right, preferred_element_type=jnp.float32)


def build_table(count, routes_ref, table_ref, capacity):
    slots = routes_ref.shape[1]
    rows = table_ref.shape[0]
    place = lax.broadcasted_iota(jnp.int32, (rows, slots), 0)
    token = lax.broadcasted_iota(jnp.int32, (rows, slots), 1)
    expert = place // capacity
    hit = ((routes_ref[0:1, :] == expert) | (routes_ref[1:2, :] == expert)) & (
        token < count * SPAN
    )
    hit = jnp.where(hit, jnp.float32(1.0), jnp.float32(0.0))
    first = lax.broadcasted_iota(jnp.int32, (slots, slots), 0)
    second = lax.broadcasted_iota(jnp.int32, (slots, slots), 1)
    earlier = jnp.where(first < second, jnp.float32(1.0), jnp.float32(0.0))
    before = dot(hit.astype(jnp.bfloat16), earlier.astype(jnp.bfloat16))
    wanted = (place - expert * capacity).astype(jnp.float32)
    table_ref[...] = jnp.where(before == wanted, hit, jnp.float32(0.0)).astype(jnp.bfloat16)


def attend_kernel(
    capacity,
    first,
    count_ref,
    size_ref,
    routes_ref,
    queries_hbm,
    key_weight_hbm,
    value_weight_hbm,
    prefix_hbm,
    fresh_hbm,
    *rest,
):
    out_ref, mark_ref, queries_ref, key_weight_ref, value_weight_ref, keys_ref = rest[-10:-4]
    cap_ref, table_ref, attended_ref, sem = rest[-4:]
    slots = queries_ref.shape[0]
    past = prefix_hbm.shape[0]
    heads, dim, _ = key_weight_ref.shape
    here = pl.ds(first, heads)
    copies = [
        pltpu.make_async_copy(
            queries_hbm.at[:, pl.ds(first * dim, heads * dim)], queries_ref, sem.at[0]
        ),
        pltpu.make_async_copy(key_weight_hbm.at[here], key_weight_ref, sem.at[1]),
        pltpu.make_async_copy(prefix_hbm, keys_ref.at[pl.ds(0, past)], sem.at[2]),
        pltpu.make_async_copy(fresh_hbm, keys_ref.at[pl.ds(past, slots)], sem.at[3]),
        pltpu.make_async_copy(value_weight_hbm.at[here], value_weight_ref, sem.at[4]),
    ]
    for copy in copies:
        copy.start()
    mark_ref[...] = jnp.zeros_like(mark_ref)
    count, size = count_ref[0], size_ref[0]
    lane = lax.broadcasted_iota(jnp.int32, (slots, past), 1)
    cap_ref[:, :past] = jnp.where(lane < size, jnp.float32(OPEN), jnp.float32(MASKED))
    row = lax.broadcasted_iota(jnp.int32, (slots, slots), 0)
    col = lax.broadcasted_iota(jnp.int32, (slots, slots), 1)
    cap_ref[:, past:] = jnp.where(
        (col <= row) & (col < count * SPAN), jnp.float32(OPEN), jnp.float32(MASKED)
    )
    build_table(count, routes_ref, table_ref, capacity)
    for copy in copies:
        copy.wait()

    scale = math.log2(math.e) / math.sqrt(dim)
    keys = keys_ref[...]
    stacks = heads // STACK
    scores = []
    for stack in range(stacks):
        lifted = []
        for h in range(stack * STACK, (stack + 1) * STACK):
            one = dot(queries_ref[:, h * dim : (h + 1) * dim], key_weight_ref[h])
            lifted.append(one.astype(jnp.bfloat16))
        lifted = jnp.concatenate(lifted, axis=0)
        scores.append(lax.dot_general(lifted, keys, NT, preferred_element_type=jnp.float32))
    for stack in range(stacks):
        score = scores[stack].reshape(STACK, slots, keys.shape[0])
        score = jnp.minimum(score, cap_ref[...][None])
        highest = jnp.max(score, axis=-1, keepdims=True) * scale
        weights = jnp.exp2(score * scale - highest)
        total = jnp.sum(weights, axis=-1, keepdims=True)
        weights = weights.astype(jnp.bfloat16).reshape(STACK * slots, keys.shape[0])
        mixed = dot(weights, keys).astype(jnp.bfloat16)
        for g in range(STACK):
            h = stack * STACK + g
            projected = dot(mixed[g * slots : (g + 1) * slots], value_weight_ref[h])
            attended_ref[:, h * dim : (h + 1) * dim] = (projected / total[g]).astype(jnp.bfloat16)
    out_ref[...] = dot(table_ref[...], attended_ref[...]).astype(jnp.bfloat16)


def attend(first, heads, operands, experts, after):
    count, size, routes, queries, key_weight, value_weight, prefix, fresh = operands
    slots = queries.shape[0]
    _, dim, latent = key_weight.shape
    places = slots * routes.shape[0]
    keys = prefix.shape[0] + slots
    smem = pl.BlockSpec(memory_space=pltpu.SMEM)
    vmem = pl.BlockSpec(memory_space=pltpu.VMEM)
    hbm = pl.BlockSpec(memory_space=pltpu.HBM)
    return pl.pallas_call(
        functools.partial(attend_kernel, places // experts, first),
        in_specs=[smem, smem, vmem] + [hbm] * 5 + [vmem] * len(after),
        out_specs=[vmem, vmem],
        out_shape=[
            jax.ShapeDtypeStruct((places, heads * dim), jnp.bfloat16),
            jax.ShapeDtypeStruct((8, 128), jnp.float32),
        ],
        scratch_shapes=[
            pltpu.VMEM((slots, heads * dim), jnp.bfloat16),
            pltpu.VMEM((heads, dim, latent), jnp.bfloat16),
            pltpu.VMEM((heads, latent, dim), jnp.bfloat16),
            pltpu.VMEM((keys, latent), jnp.bfloat16),
            pltpu.VMEM((slots, keys), jnp.float32),
            pltpu.VMEM((places, slots), jnp.bfloat16),
            pltpu.VMEM((slots, heads * dim), jnp.bfloat16),
            pltpu.SemaphoreType.DMA((5,)),
        ],
        compiler_params=pltpu.CompilerParams(vmem_limit_bytes=VMEM),
    )(*operands, *after)


def place_kernel(starts, cores, *refs):
    out_ref, sem = refs[-2:]
    _, ranks, capacity, features = out_ref.shape
    features //= cores
    copies = []
    for ref, start in zip(refs, starts):
        width = ref.shape[1]
        for source in range(ranks * cores):
            left = source % cores * features + start
            target = out_ref.at[0, source // cores, :, pl.ds(left, width)]
            rows = ref.at[pl.ds(source * capacity, capacity)]
            copies.append(pltpu.make_async_copy(rows, target, sem.at[len(copies)]))
    for copy in copies:
        copy.start()
    for copy in copies:
        copy.wait()


def place(chunks, starts, cores, shape, placed):
    anywhere = pl.BlockSpec(memory_space=pl.ANY)
    return pl.pallas_call(
        functools.partial(place_kernel, starts, cores),
        in_specs=[pl.BlockSpec(memory_space=pltpu.VMEM)] * len(chunks) + [anywhere] * len(placed),
        out_specs=anywhere,
        out_shape=jax.ShapeDtypeStruct(shape, jnp.bfloat16),
        scratch_shapes=[pltpu.SemaphoreType.DMA((len(chunks) * shape[1] * cores,))],
        input_output_aliases={len(chunks): 0} if placed else {},
        compiler_params=pltpu.CompilerParams(vmem_limit_bytes=VMEM),
        cost_estimate=SHORT,
    )(*chunks, *placed)


def local(
    queries,
    key_weight,
    value_weight,
    prefix_latent,
    fresh_latent,
    span_counts,
    prefix_lengths,
    routes,
):
    ranks, cores = lax.axis_size("dp"), lax.axis_size("ep")
    experts = ranks * cores
    heads, dim, _ = key_weight.shape
    capacity = queries.shape[0] * routes.shape[1] // experts
    operands = (
        span_counts,
        prefix_lengths,
        routes.T,
        queries,
        key_weight,
        value_weight,
        prefix_latent,
        fresh_latent,
    )
    chunks, starts, after = [], [], []
    first = 0
    for share in CHUNKS:
        size = heads * share // sum(CHUNKS)
        outgoing, mark = attend(first, size, operands, experts, after)
        arrived = lax.all_to_all(
            outgoing.reshape(experts, capacity, size * dim),
            ("dp", "ep"),
            split_axis=0,
            concat_axis=0,
            tiled=True,
        )
        chunks.append(arrived.reshape(experts * capacity, size * dim))
        starts.append(first * dim)
        after = [mark]
        first += size
    shape = (1, ranks, capacity, cores * heads * dim)
    if capacity % 16:
        arrived = jnp.concatenate(chunks, axis=1).reshape(ranks, cores, capacity, heads * dim)
        return arrived.transpose(0, 2, 1, 3).reshape(shape)
    placed = place(chunks[:-1], starts[:-1], cores, shape, [])
    return place(chunks[-1:], starts[-1:], cores, shape, [placed])


def solution(mesh):
    in_specs = (
        P(("groups", "dp"), "ep"),
        P("ep", None, None),
        P("ep", None, None),
        P(("groups", "dp"), None),
        P(("groups", "dp"), None),
        P(("groups", "dp")),
        P(("groups", "dp")),
        P(("groups", "dp"), None),
    )
    out_specs = P(("groups", "dp", "ep"), None, None, None)
    return jax.shard_map(local, mesh=mesh, in_specs=in_specs, out_specs=out_specs, check_vma=False)
```

```python
import functools
import math

import jax
import jax.numpy as jnp
from jax import lax
from jax.experimental import pallas as pl
from jax.experimental.pallas import tpu as pltpu
from jax.sharding import PartitionSpec as P

SPAN = 64
GROUPS = (2, 2)
UNROLL = 2
CHUNKS = (1, 1)
DIRECT = 16
KEY_PARTS = 2
VMEM = 60 * 1024 * 1024
SHORT = pl.CostEstimate(flops=0, bytes_accessed=0, transcendentals=0)
MARK = (8, 128)
MASKED = -1e30
OPEN = 3e38
NT = (((1,), (1,)), ((), ()))


def dot(left, right):
    return jnp.dot(left, right, preferred_element_type=jnp.float32)


def build_table(me, count, routes_ref, table_ref, capacity, cores):
    slots = routes_ref.shape[1]
    rows = table_ref.shape[0]
    place = lax.broadcasted_iota(jnp.int32, (rows, slots), 0)
    token = lax.broadcasted_iota(jnp.int32, (rows, slots), 1)
    block = place // capacity
    chips = rows // (capacity * cores)
    expert = ((block % chips) * cores + block // chips) ^ me
    hit = ((routes_ref[0:1, :] == expert) | (routes_ref[1:2, :] == expert)) & (
        token < count * SPAN
    )
    hit = jnp.where(hit, jnp.float32(1.0), jnp.float32(0.0))
    first = lax.broadcasted_iota(jnp.int32, (slots, slots), 0)
    second = lax.broadcasted_iota(jnp.int32, (slots, slots), 1)
    earlier = jnp.where(first < second, jnp.float32(1.0), jnp.float32(0.0))
    before = dot(hit.astype(jnp.bfloat16), earlier.astype(jnp.bfloat16))
    wanted = (place - block * capacity).astype(jnp.float32)
    table_ref[...] = jnp.where(before == wanted, hit, jnp.float32(0.0)).astype(jnp.bfloat16)


def attend_kernel(
    capacity,
    group,
    first,
    cores,
    after,
    me_ref,
    count_ref,
    size_ref,
    routes_ref,
    queries_hbm,
    key_weight_hbm,
    value_weight_hbm,
    prefix_hbm,
    fresh_hbm,
    *rest,
):
    *out_refs, mark_ref, queries_ref, key_weight_ref, value_weight_ref, keys_ref = rest[after:-4]
    mark_ref[...] = jnp.zeros_like(mark_ref)
    cap_ref, table_ref, attended_ref, sem = rest[-4:]
    slots = queries_ref.shape[0]
    past = prefix_hbm.shape[0]
    heads, dim, _ = key_weight_ref.shape
    here = pl.ds(first, heads)
    step = group * UNROLL
    steps = heads // step
    part = past // KEY_PARTS

    def copy_step(i):
        def of(source, target, index):
            here, there = pl.ds(i * step, step), pl.ds(first + i * step, step)
            return pltpu.make_async_copy(source.at[there], target.at[here], sem.at[3 * i + index])

        here, there = pl.ds(i * step * dim, step * dim), pl.ds((first + i * step) * dim, step * dim)
        return [
            pltpu.make_async_copy(queries_hbm.at[:, there], queries_ref.at[:, here], sem.at[3 * i]),
            of(key_weight_hbm, key_weight_ref, 1),
            of(value_weight_hbm, value_weight_ref, 2),
        ]

    for_keys = [
        pltpu.make_async_copy(
            prefix_hbm.at[pl.ds(i * part, part)],
            keys_ref.at[pl.ds(i * part, part)],
            sem.at[3 * steps + i],
        )
        for i in range(KEY_PARTS)
    ]
    for_keys.append(
        pltpu.make_async_copy(
            fresh_hbm, keys_ref.at[pl.ds(past, slots)], sem.at[3 * steps + KEY_PARTS]
        )
    )
    opening = copy_step(0)
    for copy in opening[:2] + for_keys + opening[2:]:
        copy.start()
    for i in range(1, steps):
        for copy in copy_step(i):
            copy.start()

    count, size = count_ref[0], size_ref[0]
    lane = lax.broadcasted_iota(jnp.int32, (slots, past), 1)
    cap_ref[:, :past] = jnp.where(lane < size, jnp.float32(OPEN), jnp.float32(MASKED))
    row = lax.broadcasted_iota(jnp.int32, (slots, slots), 0)
    col = lax.broadcasted_iota(jnp.int32, (slots, slots), 1)
    cap_ref[:, past:] = jnp.where(
        (col <= row) & (col < count * SPAN), jnp.float32(OPEN), jnp.float32(MASKED)
    )
    build_table(me_ref[0], count, routes_ref, table_ref, capacity, cores)

    scale = math.log2(math.e) / math.sqrt(dim)
    for copy in for_keys:
        copy.wait()

    def body(i, carry):
        for copy in copy_step(i):
            copy.wait()
        keys = keys_ref[...]
        scores = []
        for stack in range(UNROLL):
            lifted = []
            for g in range(group):
                h = i * step + stack * group + g
                query = queries_ref[:, pl.ds(pl.multiple_of(h * dim, dim), dim)]
                lifted.append(dot(query, key_weight_ref[h]).astype(jnp.bfloat16))
            lifted = jnp.concatenate(lifted, axis=0)
            scores.append(lax.dot_general(lifted, keys, NT, preferred_element_type=jnp.float32))
        for stack in range(UNROLL):
            score = scores[stack].reshape(group, slots, keys.shape[0])
            score = jnp.minimum(score, cap_ref[...][None])
            highest = jnp.max(score, axis=-1, keepdims=True) * scale
            weights = jnp.exp2(score * scale - highest)
            total = jnp.sum(weights, axis=-1, keepdims=True)
            weights = weights.astype(jnp.bfloat16).reshape(group * slots, keys.shape[0])
            mixed = dot(weights, keys).astype(jnp.bfloat16)
            for g in range(group):
                h = i * step + stack * group + g
                projected = dot(mixed[g * slots : (g + 1) * slots], value_weight_ref[h])
                attended_ref[:, pl.ds(pl.multiple_of(h * dim, dim), dim)] = (
                    projected / total[g]
                ).astype(jnp.bfloat16)
        return carry

    lax.fori_loop(0, steps, body, 0)
    grouped = dot(table_ref[...], attended_ref[...]).astype(jnp.bfloat16)
    row = 0
    for out_ref in out_refs:
        out_ref[...] = grouped[row : row + out_ref.shape[0]]
        row += out_ref.shape[0]


def attend(
    group,
    first,
    heads,
    me,
    queries,
    key_weight,
    value_weight,
    prefix,
    fresh,
    count,
    size,
    routes,
    experts,
    parts,
    cores,
    after,
):
    slots = queries.shape[0]
    _, dim, latent = key_weight.shape
    places = slots * routes.shape[1]
    keys = prefix.shape[0] + slots
    smem = pl.BlockSpec(memory_space=pltpu.SMEM)
    vmem = pl.BlockSpec(memory_space=pltpu.VMEM)
    hbm = pl.BlockSpec(memory_space=pltpu.HBM)
    pieces = [jax.ShapeDtypeStruct((rows, heads * dim), jnp.bfloat16) for rows in parts]
    return pl.pallas_call(
        functools.partial(attend_kernel, places // experts, group, first, cores, len(after)),
        in_specs=[smem, smem, smem, vmem] + [hbm] * 5 + [vmem] * len(after),
        out_specs=[vmem] * (len(pieces) + 1),
        out_shape=pieces + [jax.ShapeDtypeStruct(MARK, jnp.float32)],
        scratch_shapes=[
            pltpu.VMEM((slots, heads * dim), jnp.bfloat16),
            pltpu.VMEM((heads, dim, latent), jnp.bfloat16),
            pltpu.VMEM((heads, latent, dim), jnp.bfloat16),
            pltpu.VMEM((keys, latent), jnp.bfloat16),
            pltpu.VMEM((slots, keys), jnp.float32),
            pltpu.VMEM((places, slots), jnp.bfloat16),
            pltpu.VMEM((slots, heads * dim), jnp.bfloat16),
            pltpu.SemaphoreType.DMA((3 * heads // (group * UNROLL) + KEY_PARTS + 1,)),
        ],
        compiler_params=pltpu.CompilerParams(vmem_limit_bytes=VMEM),
        cost_estimate=pl.CostEstimate(
            flops=4 * slots * heads * keys * latent,
            bytes_accessed=4 * heads * dim * latent,
            transcendentals=heads * slots * keys,
        ),
    )(me, count, size, routes.T, queries, key_weight, value_weight, prefix, fresh, *after)


def run_copies(copies):
    for copy in copies:
        copy.start()
    for copy in copies:
        copy.wait()


def join_kernel(*refs):
    *refs, sem = refs
    count = (len(refs) - 1) // 2
    copies = []
    for i, (kept_ref, out_ref) in enumerate(zip(refs[:count], refs[count + 1 :])):
        rows = kept_ref.shape[0]
        swapped = refs[count].at[pl.ds((i + 1) * rows, rows)]
        copies += [
            pltpu.make_async_copy(kept_ref, out_ref.at[pl.ds(0, rows)], sem.at[2 * i]),
            pltpu.make_async_copy(swapped, out_ref.at[pl.ds(rows, rows)], sem.at[2 * i + 1]),
        ]
    run_copies(copies)


def join(kept, swapped):
    rows, width = kept[0].shape
    return pl.pallas_call(
        join_kernel,
        in_specs=[pl.BlockSpec(memory_space=pl.ANY)] * (len(kept) + 1),
        out_specs=[pl.BlockSpec(memory_space=pltpu.VMEM)] * len(kept),
        out_shape=[jax.ShapeDtypeStruct((2 * rows, width), jnp.bfloat16)] * len(kept),
        scratch_shapes=[pltpu.SemaphoreType.DMA((2 * len(kept),))],
        compiler_params=pltpu.CompilerParams(vmem_limit_bytes=VMEM),
        cost_estimate=SHORT,
    )(*kept, swapped)


def place_kernel(plan, cores, me_ref, *refs):
    out_ref, sem = refs[-2:]
    _, _, capacity, features = out_ref.shape
    features //= cores
    me = me_ref[0]
    copies = []
    for ref, row, start, bits in plan:
        ref = refs[ref]
        who = me ^ bits
        left = pl.multiple_of(who % cores * features + start, math.gcd(features, start))
        target = out_ref.at[0, who // cores, :, pl.ds(left, ref.shape[1])]
        copies.append(
            pltpu.make_async_copy(ref.at[pl.ds(row, capacity)], target, sem.at[len(copies)])
        )
    run_copies(copies)


def place(me, arrays, plan, cores, shape, placed):
    anywhere = pl.BlockSpec(memory_space=pl.ANY)
    operands = [me, *arrays, *placed]
    return pl.pallas_call(
        functools.partial(place_kernel, plan, cores),
        in_specs=[pl.BlockSpec(memory_space=pltpu.SMEM)]
        + [pl.BlockSpec(memory_space=pltpu.VMEM)] * len(arrays)
        + [anywhere] * len(placed),
        out_specs=anywhere,
        out_shape=jax.ShapeDtypeStruct(shape, jnp.bfloat16),
        scratch_shapes=[pltpu.SemaphoreType.DMA((len(plan),))],
        input_output_aliases={len(operands) - 1: 0} if placed else {},
        compiler_params=pltpu.CompilerParams(vmem_limit_bytes=VMEM),
    )(*operands)


def exchange_order(ranks):
    near, far = list(range(1, ranks // 2)), list(range(ranks // 2, ranks))
    return far[::2] + far[1::2] + near


def local(
    queries,
    key_weight,
    value_weight,
    prefix_latent,
    fresh_latent,
    span_counts,
    prefix_lengths,
    routes,
):
    ranks, cores = lax.axis_size("dp"), lax.axis_size("ep")
    experts = ranks * cores
    slots = queries.shape[0]
    heads, dim, _ = key_weight.shape
    capacity = slots * routes.shape[1] // experts
    direct = ranks <= DIRECT and capacity % 16 == 0
    me = (lax.axis_index("dp") * cores + lax.axis_index("ep")).astype(jnp.int32).reshape(1)
    nobody = jnp.zeros((1,), jnp.int32)
    shares = [heads * share // sum(CHUNKS) for share in CHUNKS]

    def run(chunk, order, parts, cores, after):
        return attend(
            GROUPS[chunk],
            sum(shares[:chunk]),
            shares[chunk],
            order,
            queries,
            key_weight,
            value_weight,
            prefix_latent,
            fresh_latent,
            span_counts,
            prefix_lengths,
            routes,
            experts,
            parts,
            cores,
            after,
        )

    def to_all(outgoing):
        return lax.all_to_all(
            outgoing.reshape(experts, capacity, -1),
            ("dp", "ep"),
            split_axis=0,
            concat_axis=0,
            tiled=True,
        )

    if not direct:
        outgoing = [run(chunk, nobody, [experts * capacity], 1, [])[0] for chunk in range(len(shares))]
        arrived = jnp.concatenate([to_all(rows) for rows in outgoing], axis=2)
        arrived = arrived.reshape(ranks, cores, capacity, -1).transpose(0, 2, 1, 3)
        return arrived.reshape(1, ranks, capacity, cores * heads * dim)
    opening, mark = run(0, nobody, [experts * capacity], 1, [])
    first = to_all(opening).reshape(experts * capacity, -1)
    parts = [capacity] * ranks + [(cores - 1) * ranks * capacity]
    *kept, message, mark = run(1, me, parts, cores, [mark])
    swapped = lax.ppermute(message, "ep", [(i, i ^ 1) for i in range(cores)])
    order = exchange_order(ranks)
    joined = dict(zip(range(1, ranks), join(kept[1:], swapped)))
    arrays = [kept[0], swapped]
    middle = shares[0] * dim
    plan = [(0, 0, middle, 0), (1, 0, middle, 1)]
    for j in order:
        plan.append((len(arrays), 0, middle, j * cores))
        plan.append((len(arrays), capacity, middle, j * cores + 1))
        arrays.append(lax.ppermute(joined[j], "dp", [(i, i ^ j) for i in range(ranks)]))
    shape = (1, ranks, capacity, cores * heads * dim)
    first_plan = [(0, i * capacity, 0, i) for i in range(experts)]
    placed = place(nobody, [first], first_plan, cores, shape, [])
    return place(me, arrays, plan, cores, shape, [placed])


def solution(mesh):
    in_specs = (
        P(("groups", "dp"), "ep"),
        P("ep", None, None),
        P("ep", None, None),
        P(("groups", "dp"), None),
        P(("groups", "dp"), None),
        P(("groups", "dp")),
        P(("groups", "dp")),
        P(("groups", "dp"), None),
    )
    out_specs = P(("groups", "dp", "ep"), None, None, None)
    return jax.shard_map(local, mesh=mesh, in_specs=in_specs, out_specs=out_specs, check_vma=False)
```

```python
import functools
import math

import jax
import jax.numpy as jnp
from jax import lax
from jax.experimental import pallas as pl
from jax.experimental.pallas import tpu as pltpu
from jax.sharding import PartitionSpec as P

SPAN = 64
GROUPS = (2, 2)
UNROLL = 2
CHUNKS = (1, 1)
DIRECT = 16
KEY_PARTS = 2
VMEM = 60 * 1024 * 1024
SHORT = pl.CostEstimate(flops=0, bytes_accessed=0, transcendentals=0)
MARK = (8, 128)
MASKED = -1e30
OPEN = 3e38
NT = (((1,), (1,)), ((), ()))


def dot(left, right):
    return jnp.dot(left, right, preferred_element_type=jnp.float32)


def build_table(me, count, routes_ref, table_ref, capacity, cores):
    slots = routes_ref.shape[1]
    rows = table_ref.shape[0]
    place = lax.broadcasted_iota(jnp.int32, (rows, slots), 0)
    token = lax.broadcasted_iota(jnp.int32, (rows, slots), 1)
    block = place // capacity
    chips = rows // (capacity * cores)
    expert = ((block % chips) * cores + block // chips) ^ me
    hit = ((routes_ref[0:1, :] == expert) | (routes_ref[1:2, :] == expert)) & (
        token < count * SPAN
    )
    hit = jnp.where(hit, jnp.float32(1.0), jnp.float32(0.0))
    first = lax.broadcasted_iota(jnp.int32, (slots, slots), 0)
    second = lax.broadcasted_iota(jnp.int32, (slots, slots), 1)
    earlier = jnp.where(first < second, jnp.float32(1.0), jnp.float32(0.0))
    before = dot(hit.astype(jnp.bfloat16), earlier.astype(jnp.bfloat16))
    wanted = (place - block * capacity).astype(jnp.float32)
    table_ref[...] = jnp.where(before == wanted, hit, jnp.float32(0.0)).astype(jnp.bfloat16)


def attend_kernel(
    capacity,
    group,
    first,
    cores,
    after,
    me_ref,
    count_ref,
    size_ref,
    routes_ref,
    queries_hbm,
    key_weight_hbm,
    value_weight_hbm,
    prefix_hbm,
    fresh_hbm,
    *rest,
):
    *out_refs, mark_ref, queries_ref, key_weight_ref, value_weight_ref, keys_ref = rest[after:-4]
    mark_ref[...] = jnp.zeros_like(mark_ref)
    cap_ref, table_ref, attended_ref, sem = rest[-4:]
    slots = queries_ref.shape[0]
    past = prefix_hbm.shape[0]
    heads, dim, _ = key_weight_ref.shape
    here = pl.ds(first, heads)
    step = group * UNROLL
    steps = heads // step
    part = past // KEY_PARTS

    def copy_step(i):
        def of(source, target, index):
            here, there = pl.ds(i * step, step), pl.ds(first + i * step, step)
            return pltpu.make_async_copy(source.at[there], target.at[here], sem.at[3 * i + index])

        here, there = pl.ds(i * step * dim, step * dim), pl.ds((first + i * step) * dim, step * dim)
        return [
            pltpu.make_async_copy(queries_hbm.at[:, there], queries_ref.at[:, here], sem.at[3 * i]),
            of(key_weight_hbm, key_weight_ref, 1),
            of(value_weight_hbm, value_weight_ref, 2),
        ]

    for_keys = [
        pltpu.make_async_copy(
            prefix_hbm.at[pl.ds(i * part, part)],
            keys_ref.at[pl.ds(i * part, part)],
            sem.at[3 * steps + i],
        )
        for i in range(KEY_PARTS)
    ]
    for_keys.append(
        pltpu.make_async_copy(
            fresh_hbm, keys_ref.at[pl.ds(past, slots)], sem.at[3 * steps + KEY_PARTS]
        )
    )
    opening = copy_step(0)
    for copy in opening[:2] + for_keys + opening[2:]:
        copy.start()
    for i in range(1, steps):
        for copy in copy_step(i):
            copy.start()

    count, size = count_ref[0], size_ref[0]
    lane = lax.broadcasted_iota(jnp.int32, (slots, past), 1)
    cap_ref[:, :past] = jnp.where(lane < size, jnp.float32(OPEN), jnp.float32(MASKED))
    row = lax.broadcasted_iota(jnp.int32, (slots, slots), 0)
    col = lax.broadcasted_iota(jnp.int32, (slots, slots), 1)
    cap_ref[:, past:] = jnp.where(
        (col <= row) & (col < count * SPAN), jnp.float32(OPEN), jnp.float32(MASKED)
    )
    build_table(me_ref[0], count, routes_ref, table_ref, capacity, cores)

    scale = math.log2(math.e) / math.sqrt(dim)
    for copy in for_keys:
        copy.wait()

    def body(i, carry):
        for copy in copy_step(i):
            copy.wait()
        keys = keys_ref[...]
        scores = []
        for stack in range(UNROLL):
            lifted = []
            for g in range(group):
                h = i * step + stack * group + g
                query = queries_ref[:, pl.ds(pl.multiple_of(h * dim, dim), dim)]
                lifted.append(dot(query, key_weight_ref[h]).astype(jnp.bfloat16))
            lifted = jnp.concatenate(lifted, axis=0)
            scores.append(lax.dot_general(lifted, keys, NT, preferred_element_type=jnp.float32))
        for stack in range(UNROLL):
            score = scores[stack].reshape(group, slots, keys.shape[0])
            score = jnp.minimum(score, cap_ref[...][None])
            highest = jnp.max(score, axis=-1, keepdims=True) * scale
            weights = jnp.exp2(score * scale - highest)
            total = jnp.sum(weights, axis=-1, keepdims=True)
            weights = weights.astype(jnp.bfloat16).reshape(group * slots, keys.shape[0])
            mixed = dot(weights, keys).astype(jnp.bfloat16)
            for g in range(group):
                h = i * step + stack * group + g
                projected = dot(mixed[g * slots : (g + 1) * slots], value_weight_ref[h])
                attended_ref[:, pl.ds(pl.multiple_of(h * dim, dim), dim)] = (
                    projected / total[g]
                ).astype(jnp.bfloat16)
        return carry

    lax.fori_loop(0, steps, body, 0)
    grouped = dot(table_ref[...], attended_ref[...]).astype(jnp.bfloat16)
    row = 0
    for out_ref in out_refs:
        out_ref[...] = grouped[row : row + out_ref.shape[0]]
        row += out_ref.shape[0]


def attend(
    group,
    first,
    heads,
    me,
    queries,
    key_weight,
    value_weight,
    prefix,
    fresh,
    count,
    size,
    routes,
    experts,
    parts,
    cores,
    after,
):
    slots = queries.shape[0]
    _, dim, latent = key_weight.shape
    places = slots * routes.shape[1]
    keys = prefix.shape[0] + slots
    smem = pl.BlockSpec(memory_space=pltpu.SMEM)
    vmem = pl.BlockSpec(memory_space=pltpu.VMEM)
    hbm = pl.BlockSpec(memory_space=pltpu.HBM)
    pieces = [jax.ShapeDtypeStruct((rows, heads * dim), jnp.bfloat16) for rows in parts]
    return pl.pallas_call(
        functools.partial(attend_kernel, places // experts, group, first, cores, len(after)),
        in_specs=[smem, smem, smem, vmem] + [hbm] * 5 + [vmem] * len(after),
        out_specs=[vmem] * (len(pieces) + 1),
        out_shape=pieces + [jax.ShapeDtypeStruct(MARK, jnp.float32)],
        scratch_shapes=[
            pltpu.VMEM((slots, heads * dim), jnp.bfloat16),
            pltpu.VMEM((heads, dim, latent), jnp.bfloat16),
            pltpu.VMEM((heads, latent, dim), jnp.bfloat16),
            pltpu.VMEM((keys, latent), jnp.bfloat16),
            pltpu.VMEM((slots, keys), jnp.float32),
            pltpu.VMEM((places, slots), jnp.bfloat16),
            pltpu.VMEM((slots, heads * dim), jnp.bfloat16),
            pltpu.SemaphoreType.DMA((3 * heads // (group * UNROLL) + KEY_PARTS + 1,)),
        ],
        compiler_params=pltpu.CompilerParams(vmem_limit_bytes=VMEM),
        cost_estimate=pl.CostEstimate(
            flops=4 * slots * heads * keys * latent,
            bytes_accessed=4 * heads * dim * latent,
            transcendentals=heads * slots * keys,
        ),
    )(me, count, size, routes.T, queries, key_weight, value_weight, prefix, fresh, *after)


def run_copies(copies):
    for copy in copies:
        copy.start()
    for copy in copies:
        copy.wait()


def join_kernel(*refs):
    *refs, sem = refs
    count = (len(refs) - 1) // 2
    copies = []
    for i, (kept_ref, out_ref) in enumerate(zip(refs[:count], refs[count + 1 :])):
        rows = kept_ref.shape[0]
        swapped = refs[count].at[pl.ds((i + 1) * rows, rows)]
        copies += [
            pltpu.make_async_copy(kept_ref, out_ref.at[pl.ds(0, rows)], sem.at[2 * i]),
            pltpu.make_async_copy(swapped, out_ref.at[pl.ds(rows, rows)], sem.at[2 * i + 1]),
        ]
    run_copies(copies)


def join(kept, swapped):
    rows, width = kept[0].shape
    return pl.pallas_call(
        join_kernel,
        in_specs=[pl.BlockSpec(memory_space=pl.ANY)] * (len(kept) + 1),
        out_specs=[pl.BlockSpec(memory_space=pltpu.VMEM)] * len(kept),
        out_shape=[jax.ShapeDtypeStruct((2 * rows, width), jnp.bfloat16)] * len(kept),
        scratch_shapes=[pltpu.SemaphoreType.DMA((2 * len(kept),))],
        compiler_params=pltpu.CompilerParams(vmem_limit_bytes=VMEM),
        cost_estimate=SHORT,
    )(*kept, swapped)


def place_kernel(plan, cores, me_ref, *refs):
    out_ref, sem = refs[-2:]
    _, _, capacity, features = out_ref.shape
    features //= cores
    me = me_ref[0]
    copies = []
    for ref, row, start, bits in plan:
        ref = refs[ref]
        who = me ^ bits
        left = pl.multiple_of(who % cores * features + start, math.gcd(features, start))
        target = out_ref.at[0, who // cores, :, pl.ds(left, ref.shape[1])]
        copies.append(
            pltpu.make_async_copy(ref.at[pl.ds(row, capacity)], target, sem.at[len(copies)])
        )
    run_copies(copies)


def place(me, arrays, plan, cores, shape, placed):
    anywhere = pl.BlockSpec(memory_space=pl.ANY)
    operands = [me, *arrays, *placed]
    return pl.pallas_call(
        functools.partial(place_kernel, plan, cores),
        in_specs=[pl.BlockSpec(memory_space=pltpu.SMEM)]
        + [pl.BlockSpec(memory_space=pltpu.VMEM)] * len(arrays)
        + [anywhere] * len(placed),
        out_specs=anywhere,
        out_shape=jax.ShapeDtypeStruct(shape, jnp.bfloat16),
        scratch_shapes=[pltpu.SemaphoreType.DMA((len(plan),))],
        input_output_aliases={len(operands) - 1: 0} if placed else {},
        compiler_params=pltpu.CompilerParams(vmem_limit_bytes=VMEM),
    )(*operands)


def exchange_order(ranks):
    near, far = list(range(1, ranks // 2)), list(range(ranks // 2, ranks))
    far = far[::2] + far[1::2]
    return far[:1] + near[:-1] + far[1:] + near[-1:]


def local(
    queries,
    key_weight,
    value_weight,
    prefix_latent,
    fresh_latent,
    span_counts,
    prefix_lengths,
    routes,
):
    ranks, cores = lax.axis_size("dp"), lax.axis_size("ep")
    experts = ranks * cores
    slots = queries.shape[0]
    heads, dim, _ = key_weight.shape
    capacity = slots * routes.shape[1] // experts
    direct = ranks <= DIRECT and capacity % 16 == 0
    me = (lax.axis_index("dp") * cores + lax.axis_index("ep")).astype(jnp.int32).reshape(1)
    nobody = jnp.zeros((1,), jnp.int32)
    shares = [heads * share // sum(CHUNKS) for share in CHUNKS]

    def run(chunk, order, parts, cores, after):
        return attend(
            GROUPS[chunk],
            sum(shares[:chunk]),
            shares[chunk],
            order,
            queries,
            key_weight,
            value_weight,
            prefix_latent,
            fresh_latent,
            span_counts,
            prefix_lengths,
            routes,
            experts,
            parts,
            cores,
            after,
        )

    def to_all(outgoing):
        return lax.all_to_all(
            outgoing.reshape(experts, capacity, -1),
            ("dp", "ep"),
            split_axis=0,
            concat_axis=0,
            tiled=True,
        )

    if not direct:
        outgoing = [run(chunk, nobody, [experts * capacity], 1, [])[0] for chunk in range(len(shares))]
        arrived = jnp.concatenate([to_all(rows) for rows in outgoing], axis=2)
        arrived = arrived.reshape(ranks, cores, capacity, -1).transpose(0, 2, 1, 3)
        return arrived.reshape(1, ranks, capacity, cores * heads * dim)
    opening, mark = run(0, nobody, [experts * capacity], 1, [])
    first = to_all(opening).reshape(experts * capacity, -1)
    parts = [capacity] * ranks + [(cores - 1) * ranks * capacity]
    *kept, message, mark = run(1, me, parts, cores, [mark])
    swapped = lax.ppermute(message, "ep", [(i, i ^ 1) for i in range(cores)])
    order = exchange_order(ranks)
    joined = dict(zip(range(1, ranks), join(kept[1:], swapped)))
    arrays = [kept[0], swapped]
    middle = shares[0] * dim
    plan = [(0, 0, middle, 0), (1, 0, middle, 1)]
    for j in order:
        plan.append((len(arrays), 0, middle, j * cores))
        plan.append((len(arrays), capacity, middle, j * cores + 1))
        arrays.append(lax.ppermute(joined[j], "dp", [(i, i ^ j) for i in range(ranks)]))
    shape = (1, ranks, capacity, cores * heads * dim)
    first_plan = [(0, i * capacity, 0, i) for i in range(experts)]
    placed = place(nobody, [first], first_plan, cores, shape, [])
    return place(me, arrays, plan, cores, shape, [placed])


def solution(mesh):
    in_specs = (
        P(("groups", "dp"), "ep"),
        P("ep", None, None),
        P("ep", None, None),
        P(("groups", "dp"), None),
        P(("groups", "dp"), None),
        P(("groups", "dp")),
        P(("groups", "dp")),
        P(("groups", "dp"), None),
    )
    out_specs = P(("groups", "dp", "ep"), None, None, None)
    return jax.shard_map(local, mesh=mesh, in_specs=in_specs, out_specs=out_specs, check_vma=False)
```

```python
import functools
import math

import jax
import jax.numpy as jnp
from jax import lax
from jax.experimental import pallas as pl
from jax.experimental.pallas import tpu as pltpu
from jax.sharding import PartitionSpec as P

SPAN = 64
STACK = 4
CHUNKS = (3, 5)
VMEM = 63_400_000
SHORT = pl.CostEstimate(flops=0, bytes_accessed=0, transcendentals=0)
MASKED = -1e30
OPEN = 3e38
NT = (((1,), (1,)), ((), ()))


def dot(left, right):
    return jnp.dot(left, right, preferred_element_type=jnp.float32)


def build_table(count, routes_ref, table_ref, capacity):
    slots = routes_ref.shape[1]
    rows = table_ref.shape[0]
    place = lax.broadcasted_iota(jnp.int32, (rows, slots), 0)
    token = lax.broadcasted_iota(jnp.int32, (rows, slots), 1)
    expert = place // capacity
    hit = ((routes_ref[0:1, :] == expert) | (routes_ref[1:2, :] == expert)) & (
        token < count * SPAN
    )
    hit = jnp.where(hit, jnp.float32(1.0), jnp.float32(0.0))
    first = lax.broadcasted_iota(jnp.int32, (slots, slots), 0)
    second = lax.broadcasted_iota(jnp.int32, (slots, slots), 1)
    earlier = jnp.where(first < second, jnp.float32(1.0), jnp.float32(0.0))
    before = dot(hit.astype(jnp.bfloat16), earlier.astype(jnp.bfloat16))
    wanted = (place - expert * capacity).astype(jnp.float32)
    table_ref[...] = jnp.where(before == wanted, hit, jnp.float32(0.0)).astype(jnp.bfloat16)


def attend_kernel(
    capacity,
    first,
    count_ref,
    size_ref,
    routes_ref,
    queries_hbm,
    key_weight_hbm,
    value_weight_hbm,
    prefix_hbm,
    fresh_hbm,
    *rest,
):
    out_hbm, mark_ref, queries_ref, key_weight_ref, value_weight_ref, keys_ref = rest[-10:-4]
    cap_ref, table_ref, rows_ref, sem = rest[-4:]
    slots = queries_ref.shape[0]
    past = prefix_hbm.shape[0]
    heads, dim, _ = key_weight_ref.shape
    here = pl.ds(first, heads)
    copies = [
        pltpu.make_async_copy(
            queries_hbm.at[:, pl.ds(first * dim, heads * dim)], queries_ref, sem.at[0]
        ),
        pltpu.make_async_copy(key_weight_hbm.at[here], key_weight_ref, sem.at[1]),
        pltpu.make_async_copy(prefix_hbm, keys_ref.at[pl.ds(0, past)], sem.at[2]),
        pltpu.make_async_copy(fresh_hbm, keys_ref.at[pl.ds(past, slots)], sem.at[3]),
        pltpu.make_async_copy(value_weight_hbm.at[here], value_weight_ref, sem.at[4]),
    ]
    *needed, for_values = copies
    for copy in needed:
        copy.start()
    mark_ref[...] = jnp.zeros_like(mark_ref)
    count, size = count_ref[0], size_ref[0]
    lane = lax.broadcasted_iota(jnp.int32, (slots, past), 1)
    cap_ref[:, :past] = jnp.where(lane < size, jnp.float32(OPEN), jnp.float32(MASKED))
    row = lax.broadcasted_iota(jnp.int32, (slots, slots), 0)
    col = lax.broadcasted_iota(jnp.int32, (slots, slots), 1)
    cap_ref[:, past:] = jnp.where(
        (col <= row) & (col < count * SPAN), jnp.float32(OPEN), jnp.float32(MASKED)
    )
    build_table(count, routes_ref, table_ref, capacity)
    for copy in needed:
        copy.wait()
    for_values.start()

    scale = math.log2(math.e) / math.sqrt(dim)
    keys = keys_ref[...]
    stacks = heads // STACK
    scores = []
    for stack in range(stacks):
        lifted = []
        for h in range(stack * STACK, (stack + 1) * STACK):
            one = dot(queries_ref[:, h * dim : (h + 1) * dim], key_weight_ref[h])
            lifted.append(one.astype(jnp.bfloat16))
        lifted = jnp.concatenate(lifted, axis=0)
        scores.append(lax.dot_general(lifted, keys, NT, preferred_element_type=jnp.float32))
    for_values.wait()
    width = STACK * dim
    sends = []
    for stack in range(stacks):
        score = scores[stack].reshape(STACK, slots, keys.shape[0])
        score = jnp.minimum(score, cap_ref[...][None])
        highest = jnp.max(score, axis=-1, keepdims=True) * scale
        weights = jnp.exp2(score * scale - highest)
        total = jnp.sum(weights, axis=-1, keepdims=True)
        weights = weights.astype(jnp.bfloat16).reshape(STACK * slots, keys.shape[0])
        mixed = dot(weights, keys).astype(jnp.bfloat16)
        attended = []
        for g in range(STACK):
            projected = dot(mixed[g * slots : (g + 1) * slots], value_weight_ref[stack * STACK + g])
            attended.append((projected / total[g]).astype(jnp.bfloat16))
        attended = jnp.concatenate(attended, axis=1)
        rows_ref[stack] = dot(table_ref[...], attended).astype(jnp.bfloat16)
        there = out_hbm.at[:, pl.ds(stack * width, width)]
        sends.append(pltpu.make_async_copy(rows_ref.at[stack], there, sem.at[5 + stack]))
        sends[-1].start()
    for send in sends:
        send.wait()


def attend(first, heads, operands, experts, after):
    count, size, routes, queries, key_weight, value_weight, prefix, fresh = operands
    slots = queries.shape[0]
    _, dim, latent = key_weight.shape
    places = slots * routes.shape[0]
    keys = prefix.shape[0] + slots
    smem = pl.BlockSpec(memory_space=pltpu.SMEM)
    vmem = pl.BlockSpec(memory_space=pltpu.VMEM)
    hbm = pl.BlockSpec(memory_space=pltpu.HBM)
    return pl.pallas_call(
        functools.partial(attend_kernel, places // experts, first),
        in_specs=[smem, smem, vmem] + [hbm] * 5 + [vmem] * len(after),
        out_specs=[hbm, vmem],
        out_shape=[
            jax.ShapeDtypeStruct((places, heads * dim), jnp.bfloat16),
            jax.ShapeDtypeStruct((8, 128), jnp.float32),
        ],
        scratch_shapes=[
            pltpu.VMEM((slots, heads * dim), jnp.bfloat16),
            pltpu.VMEM((heads, dim, latent), jnp.bfloat16),
            pltpu.VMEM((heads, latent, dim), jnp.bfloat16),
            pltpu.VMEM((keys, latent), jnp.bfloat16),
            pltpu.VMEM((slots, keys), jnp.float32),
            pltpu.VMEM((places, slots), jnp.bfloat16),
            pltpu.VMEM((heads // STACK, places, STACK * dim), jnp.bfloat16),
            pltpu.SemaphoreType.DMA((5 + heads // STACK,)),
        ],
        compiler_params=pltpu.CompilerParams(vmem_limit_bytes=VMEM),
    )(*operands, *after)


def place_kernel(starts, cores, *refs):
    chunk_refs, out_ref = refs[: len(starts)], refs[-3 - len(starts)]
    held_refs, arrive, leave = refs[-2 - len(starts) : -2], refs[-2], refs[-1]
    _, ranks, capacity, features = out_ref.shape
    features //= cores
    arrivals, leaves = [], []
    for ref, held_ref, start in zip(chunk_refs, held_refs, starts):
        width = ref.shape[1]
        for source in range(ranks * cores):
            rows = pl.ds(source * capacity, capacity)
            columns = pl.ds(source % cores * features + start, width)
            target = out_ref.at[0, source // cores, :, columns]
            i = len(arrivals)
            arrivals.append(pltpu.make_async_copy(ref.at[rows], held_ref.at[rows], arrive.at[i]))
            leaves.append(pltpu.make_async_copy(held_ref.at[rows], target, leave.at[i]))
    for copy in arrivals:
        copy.start()
    for arrival, leaving in zip(arrivals, leaves):
        arrival.wait()
        leaving.start()
    for copy in leaves:
        copy.wait()


def place(chunks, starts, cores, shape, placed):
    anywhere = pl.BlockSpec(memory_space=pl.ANY)
    pieces = len(chunks) * shape[1] * cores
    return pl.pallas_call(
        functools.partial(place_kernel, starts, cores),
        in_specs=[anywhere] * (len(chunks) + len(placed)),
        out_specs=anywhere,
        out_shape=jax.ShapeDtypeStruct(shape, jnp.bfloat16),
        scratch_shapes=[pltpu.VMEM(chunk.shape, chunk.dtype) for chunk in chunks]
        + [pltpu.SemaphoreType.DMA((pieces,))] * 2,
        input_output_aliases={len(chunks): 0} if placed else {},
        compiler_params=pltpu.CompilerParams(vmem_limit_bytes=VMEM),
        cost_estimate=SHORT,
    )(*chunks, *placed)


def local(
    queries,
    key_weight,
    value_weight,
    prefix_latent,
    fresh_latent,
    span_counts,
    prefix_lengths,
    routes,
):
    ranks, cores = lax.axis_size("dp"), lax.axis_size("ep")
    experts = ranks * cores
    heads, dim, _ = key_weight.shape
    capacity = queries.shape[0] * routes.shape[1] // experts
    operands = (
        span_counts,
        prefix_lengths,
        routes.T,
        queries,
        key_weight,
        value_weight,
        prefix_latent,
        fresh_latent,
    )
    chunks, starts, after = [], [], []
    first = 0
    for share in CHUNKS:
        size = heads * share // sum(CHUNKS)
        outgoing, mark = attend(first, size, operands, experts, after)
        arrived = lax.all_to_all(
            outgoing.reshape(experts, capacity, size * dim),
            ("dp", "ep"),
            split_axis=0,
            concat_axis=0,
            tiled=True,
        )
        chunks.append(arrived.reshape(experts * capacity, size * dim))
        starts.append(first * dim)
        after = [mark]
        first += size
    shape = (1, ranks, capacity, cores * heads * dim)
    if capacity % 16:
        arrived = jnp.concatenate(chunks, axis=1).reshape(ranks, cores, capacity, heads * dim)
        return arrived.transpose(0, 2, 1, 3).reshape(shape)
    placed = place(chunks[:-1], starts[:-1], cores, shape, [])
    return place(chunks[-1:], starts[-1:], cores, shape, [placed])


def solution(mesh):
    in_specs = (
        P(("groups", "dp"), "ep"),
        P("ep", None, None),
        P("ep", None, None),
        P(("groups", "dp"), None),
        P(("groups", "dp"), None),
        P(("groups", "dp")),
        P(("groups", "dp")),
        P(("groups", "dp"), None),
    )
    out_specs = P(("groups", "dp", "ep"), None, None, None)
    return jax.shard_map(local, mesh=mesh, in_specs=in_specs, out_specs=out_specs, check_vma=False)
```

```python
import functools
import math

import jax
import jax.numpy as jnp
from jax import lax
from jax.experimental import pallas as pl
from jax.experimental.pallas import tpu as pltpu
from jax.sharding import PartitionSpec as P

SPAN = 64
STACK = 4
CHUNKS = (1, 1)
DIRECT = 16
VMEM = 60 * 1024 * 1024
SHORT = pl.CostEstimate(flops=0, bytes_accessed=0, transcendentals=0)
MARK = (8, 128)
MASKED = -1e30
OPEN = 3e38
NT = (((1,), (1,)), ((), ()))


def dot(left, right):
    return jnp.dot(left, right, preferred_element_type=jnp.float32)


def build_table(me, count, routes_ref, table_ref, capacity, cores):
    slots = routes_ref.shape[1]
    rows = table_ref.shape[0]
    place = lax.broadcasted_iota(jnp.int32, (rows, slots), 0)
    token = lax.broadcasted_iota(jnp.int32, (rows, slots), 1)
    block = place // capacity
    chips = rows // (capacity * cores)
    expert = ((block % chips) * cores + block // chips) ^ me
    hit = ((routes_ref[0:1, :] == expert) | (routes_ref[1:2, :] == expert)) & (
        token < count * SPAN
    )
    hit = jnp.where(hit, jnp.float32(1.0), jnp.float32(0.0))
    first = lax.broadcasted_iota(jnp.int32, (slots, slots), 0)
    second = lax.broadcasted_iota(jnp.int32, (slots, slots), 1)
    earlier = jnp.where(first < second, jnp.float32(1.0), jnp.float32(0.0))
    before = dot(hit.astype(jnp.bfloat16), earlier.astype(jnp.bfloat16))
    wanted = (place - block * capacity).astype(jnp.float32)
    table_ref[...] = jnp.where(before == wanted, hit, jnp.float32(0.0)).astype(jnp.bfloat16)


def attend_kernel(
    capacity,
    first,
    cores,
    after,
    me_ref,
    count_ref,
    size_ref,
    routes_ref,
    queries_hbm,
    key_weight_hbm,
    value_weight_hbm,
    prefix_hbm,
    fresh_hbm,
    *rest,
):
    *out_refs, mark_ref, queries_ref, key_weight_ref, value_weight_ref, keys_ref = rest[after:-4]
    mark_ref[...] = jnp.zeros_like(mark_ref)
    cap_ref, table_ref, attended_ref, sem = rest[-4:]
    slots = queries_ref.shape[0]
    past = prefix_hbm.shape[0]
    heads, dim, _ = key_weight_ref.shape
    here = pl.ds(first, heads)
    here = pl.ds(first, heads)
    copies = [
        pltpu.make_async_copy(
            queries_hbm.at[:, pl.ds(first * dim, heads * dim)], queries_ref, sem.at[0]
        ),
        pltpu.make_async_copy(key_weight_hbm.at[here], key_weight_ref, sem.at[1]),
        pltpu.make_async_copy(prefix_hbm, keys_ref.at[pl.ds(0, past)], sem.at[2]),
        pltpu.make_async_copy(fresh_hbm, keys_ref.at[pl.ds(past, slots)], sem.at[3]),
        pltpu.make_async_copy(value_weight_hbm.at[here], value_weight_ref, sem.at[4]),
    ]
    for copy in copies:
        copy.start()
    count, size = count_ref[0], size_ref[0]
    lane = lax.broadcasted_iota(jnp.int32, (slots, past), 1)
    cap_ref[:, :past] = jnp.where(lane < size, jnp.float32(OPEN), jnp.float32(MASKED))
    row = lax.broadcasted_iota(jnp.int32, (slots, slots), 0)
    col = lax.broadcasted_iota(jnp.int32, (slots, slots), 1)
    cap_ref[:, past:] = jnp.where(
        (col <= row) & (col < count * SPAN), jnp.float32(OPEN), jnp.float32(MASKED)
    )
    build_table(me_ref[0], count, routes_ref, table_ref, capacity, cores)
    for copy in copies:
        copy.wait()

    scale = math.log2(math.e) / math.sqrt(dim)
    keys = keys_ref[...]
    stacks = heads // STACK
    scores = []
    for stack in range(stacks):
        lifted = []
        for h in range(stack * STACK, (stack + 1) * STACK):
            one = dot(queries_ref[:, h * dim : (h + 1) * dim], key_weight_ref[h])
            lifted.append(one.astype(jnp.bfloat16))
        lifted = jnp.concatenate(lifted, axis=0)
        scores.append(lax.dot_general(lifted, keys, NT, preferred_element_type=jnp.float32))
    for stack in range(stacks):
        score = scores[stack].reshape(STACK, slots, keys.shape[0])
        score = jnp.minimum(score, cap_ref[...][None])
        highest = jnp.max(score, axis=-1, keepdims=True) * scale
        weights = jnp.exp2(score * scale - highest)
        total = jnp.sum(weights, axis=-1, keepdims=True)
        weights = weights.astype(jnp.bfloat16).reshape(STACK * slots, keys.shape[0])
        mixed = dot(weights, keys).astype(jnp.bfloat16)
        for g in range(STACK):
            h = stack * STACK + g
            projected = dot(mixed[g * slots : (g + 1) * slots], value_weight_ref[h])
            attended_ref[:, h * dim : (h + 1) * dim] = (projected / total[g]).astype(jnp.bfloat16)
    grouped = dot(table_ref[...], attended_ref[...]).astype(jnp.bfloat16)
    row = 0
    for out_ref in out_refs:
        out_ref[...] = grouped[row : row + out_ref.shape[0]]
        row += out_ref.shape[0]


def attend(
    first,
    heads,
    me,
    queries,
    key_weight,
    value_weight,
    prefix,
    fresh,
    count,
    size,
    routes,
    experts,
    parts,
    cores,
    after,
):
    slots = queries.shape[0]
    _, dim, latent = key_weight.shape
    places = slots * routes.shape[1]
    keys = prefix.shape[0] + slots
    smem = pl.BlockSpec(memory_space=pltpu.SMEM)
    vmem = pl.BlockSpec(memory_space=pltpu.VMEM)
    hbm = pl.BlockSpec(memory_space=pltpu.HBM)
    pieces = [jax.ShapeDtypeStruct((rows, heads * dim), jnp.bfloat16) for rows in parts]
    return pl.pallas_call(
        functools.partial(attend_kernel, places // experts, first, cores, len(after)),
        in_specs=[smem, smem, smem, vmem] + [hbm] * 5 + [vmem] * len(after),
        out_specs=[vmem] * (len(pieces) + 1),
        out_shape=pieces + [jax.ShapeDtypeStruct(MARK, jnp.float32)],
        scratch_shapes=[
            pltpu.VMEM((slots, heads * dim), jnp.bfloat16),
            pltpu.VMEM((heads, dim, latent), jnp.bfloat16),
            pltpu.VMEM((heads, latent, dim), jnp.bfloat16),
            pltpu.VMEM((keys, latent), jnp.bfloat16),
            pltpu.VMEM((slots, keys), jnp.float32),
            pltpu.VMEM((places, slots), jnp.bfloat16),
            pltpu.VMEM((slots, heads * dim), jnp.bfloat16),
            pltpu.SemaphoreType.DMA((5,)),
        ],
        compiler_params=pltpu.CompilerParams(vmem_limit_bytes=VMEM),
        cost_estimate=pl.CostEstimate(
            flops=4 * slots * heads * keys * latent,
            bytes_accessed=4 * heads * dim * latent,
            transcendentals=heads * slots * keys,
        ),
    )(me, count, size, routes.T, queries, key_weight, value_weight, prefix, fresh, *after)


def run_copies(copies):
    for copy in copies:
        copy.start()
    for copy in copies:
        copy.wait()


def join_kernel(*refs):
    *refs, sem = refs
    count = (len(refs) - 1) // 2
    copies = []
    for i, (kept_ref, out_ref) in enumerate(zip(refs[:count], refs[count + 1 :])):
        rows = kept_ref.shape[0]
        swapped = refs[count].at[pl.ds((i + 1) * rows, rows)]
        copies += [
            pltpu.make_async_copy(kept_ref, out_ref.at[pl.ds(0, rows)], sem.at[2 * i]),
            pltpu.make_async_copy(swapped, out_ref.at[pl.ds(rows, rows)], sem.at[2 * i + 1]),
        ]
    run_copies(copies)


def join(kept, swapped):
    rows, width = kept[0].shape
    return pl.pallas_call(
        join_kernel,
        in_specs=[pl.BlockSpec(memory_space=pl.ANY)] * (len(kept) + 1),
        out_specs=[pl.BlockSpec(memory_space=pltpu.VMEM)] * len(kept),
        out_shape=[jax.ShapeDtypeStruct((2 * rows, width), jnp.bfloat16)] * len(kept),
        scratch_shapes=[pltpu.SemaphoreType.DMA((2 * len(kept),))],
        compiler_params=pltpu.CompilerParams(vmem_limit_bytes=VMEM),
        cost_estimate=SHORT,
    )(*kept, swapped)


def place_kernel(plan, cores, me_ref, *refs):
    out_ref, sem = refs[-2:]
    _, _, capacity, features = out_ref.shape
    features //= cores
    me = me_ref[0]
    copies = []
    for ref, row, start, bits, apart in plan:
        ref = refs[ref]
        who = me ^ bits if apart else jnp.int32(bits)
        left = pl.multiple_of(who % cores * features + start, math.gcd(features, start))
        target = out_ref.at[0, who // cores, :, pl.ds(left, ref.shape[1])]
        copies.append(
            pltpu.make_async_copy(ref.at[pl.ds(row, capacity)], target, sem.at[len(copies)])
        )
    run_copies(copies)


def place(me, arrays, plan, cores, shape, placed):
    anywhere = pl.BlockSpec(memory_space=pl.ANY)
    operands = [me, *arrays, *placed]
    return pl.pallas_call(
        functools.partial(place_kernel, plan, cores),
        in_specs=[pl.BlockSpec(memory_space=pltpu.SMEM)]
        + [pl.BlockSpec(memory_space=pltpu.VMEM)] * len(arrays)
        + [anywhere] * len(placed),
        out_specs=anywhere,
        out_shape=jax.ShapeDtypeStruct(shape, jnp.bfloat16),
        scratch_shapes=[pltpu.SemaphoreType.DMA((len(plan),))],
        input_output_aliases={len(operands) - 1: 0} if placed else {},
        compiler_params=pltpu.CompilerParams(vmem_limit_bytes=VMEM),
    )(*operands)


def exchange_order(ranks):
    near, far = list(range(1, ranks // 2)), list(range(ranks // 2, ranks))
    return near[:-1] + far[::2] + far[1::2] + near[-1:]


def local(
    queries,
    key_weight,
    value_weight,
    prefix_latent,
    fresh_latent,
    span_counts,
    prefix_lengths,
    routes,
):
    ranks, cores = lax.axis_size("dp"), lax.axis_size("ep")
    experts = ranks * cores
    slots = queries.shape[0]
    heads, dim, _ = key_weight.shape
    capacity = slots * routes.shape[1] // experts
    direct = ranks <= DIRECT and capacity % 16 == 0
    me = (lax.axis_index("dp") * cores + lax.axis_index("ep")).astype(jnp.int32).reshape(1)
    nobody = jnp.zeros((1,), jnp.int32)
    shares = [heads * share // sum(CHUNKS) for share in CHUNKS]

    def run(chunk, order, parts, cores, after):
        return attend(
            sum(shares[:chunk]),
            shares[chunk],
            order,
            queries,
            key_weight,
            value_weight,
            prefix_latent,
            fresh_latent,
            span_counts,
            prefix_lengths,
            routes,
            experts,
            parts,
            cores,
            after,
        )

    def to_all(outgoing):
        return lax.all_to_all(
            outgoing.reshape(experts, capacity, -1),
            ("dp", "ep"),
            split_axis=0,
            concat_axis=0,
            tiled=True,
        )

    if not direct:
        outgoing = [run(chunk, nobody, [experts * capacity], 1, [])[0] for chunk in range(len(shares))]
        arrived = jnp.concatenate([to_all(rows) for rows in outgoing], axis=2)
        arrived = arrived.reshape(ranks, cores, capacity, -1).transpose(0, 2, 1, 3)
        return arrived.reshape(1, ranks, capacity, cores * heads * dim)
    opening, mark = run(0, nobody, [experts * capacity], 1, [])
    first = to_all(opening).reshape(experts * capacity, -1)
    parts = [capacity] * ranks + [(cores - 1) * ranks * capacity]
    *kept, message, mark = run(1, me, parts, cores, [mark])
    swapped = lax.ppermute(message, "ep", [(i, i ^ 1) for i in range(cores)])
    order = exchange_order(ranks)
    joined = dict(zip(range(1, ranks), join(kept[1:], swapped)))
    middle = shares[0] * dim
    soon, late = [first, kept[0], swapped], []
    soon_plan = [(0, i * capacity, 0, i, False) for i in range(experts)]
    soon_plan += [(1, 0, middle, 0, True), (2, 0, middle, 1, True)]
    late_plan = []
    for j in order:
        piece = lax.ppermute(joined[j], "dp", [(i, i ^ j) for i in range(ranks)])
        arrays, plan = (soon, soon_plan) if j < ranks // 2 else (late, late_plan)
        plan.append((len(arrays), 0, middle, j * cores, True))
        plan.append((len(arrays), capacity, middle, j * cores + 1, True))
        arrays.append(piece)
    shape = (1, ranks, capacity, cores * heads * dim)
    placed = place(me, soon, soon_plan, cores, shape, [])
    return place(me, late, late_plan, cores, shape, [placed])


def solution(mesh):
    in_specs = (
        P(("groups", "dp"), "ep"),
        P("ep", None, None),
        P("ep", None, None),
        P(("groups", "dp"), None),
        P(("groups", "dp"), None),
        P(("groups", "dp")),
        P(("groups", "dp")),
        P(("groups", "dp"), None),
    )
    out_specs = P(("groups", "dp", "ep"), None, None, None)
    return jax.shard_map(local, mesh=mesh, in_specs=in_specs, out_specs=out_specs, check_vma=False)
```

```python
import functools
import math

import jax
import jax.numpy as jnp
from jax import lax
from jax.experimental import pallas as pl
from jax.experimental.pallas import tpu as pltpu
from jax.sharding import PartitionSpec as P

SPAN = 64
STACK = 4
CHUNKS = (1, 1)
DIRECT = 16
ALL_VMEM = 60 * 1024 * 1024
VMEM = 52 * 1024 * 1024
SHORT = pl.CostEstimate(flops=0, bytes_accessed=0, transcendentals=0)
MARK = (8, 128)
MASKED = -1e30
OPEN = 3e38
NT = (((1,), (1,)), ((), ()))


def dot(left, right):
    return jnp.dot(left, right, preferred_element_type=jnp.float32)


def build_table(me, count, routes_ref, table_ref, capacity, cores):
    slots = routes_ref.shape[1]
    rows = table_ref.shape[0]
    place = lax.broadcasted_iota(jnp.int32, (rows, slots), 0)
    token = lax.broadcasted_iota(jnp.int32, (rows, slots), 1)
    block = place // capacity
    chips = rows // (capacity * cores)
    expert = ((block % chips) * cores + block // chips) ^ me
    hit = ((routes_ref[0:1, :] == expert) | (routes_ref[1:2, :] == expert)) & (
        token < count * SPAN
    )
    hit = jnp.where(hit, jnp.float32(1.0), jnp.float32(0.0))
    first = lax.broadcasted_iota(jnp.int32, (slots, slots), 0)
    second = lax.broadcasted_iota(jnp.int32, (slots, slots), 1)
    earlier = jnp.where(first < second, jnp.float32(1.0), jnp.float32(0.0))
    before = dot(hit.astype(jnp.bfloat16), earlier.astype(jnp.bfloat16))
    wanted = (place - block * capacity).astype(jnp.float32)
    table_ref[...] = jnp.where(before == wanted, hit, jnp.float32(0.0)).astype(jnp.bfloat16)


def attend_kernel(
    capacity,
    first,
    cores,
    after,
    me_ref,
    count_ref,
    size_ref,
    routes_ref,
    queries_hbm,
    key_weight_hbm,
    value_weight_hbm,
    prefix_hbm,
    fresh_hbm,
    *rest,
):
    *out_refs, mark_ref, queries_ref, key_weight_ref, value_weight_ref, keys_ref = rest[after:-4]
    mark_ref[...] = jnp.zeros_like(mark_ref)
    cap_ref, table_ref, attended_ref, sem = rest[-4:]
    slots = queries_ref.shape[0]
    past = prefix_hbm.shape[0]
    heads, dim, _ = key_weight_ref.shape
    here = pl.ds(first, heads)
    here = pl.ds(first, heads)
    copies = [
        pltpu.make_async_copy(
            queries_hbm.at[:, pl.ds(first * dim, heads * dim)], queries_ref, sem.at[0]
        ),
        pltpu.make_async_copy(key_weight_hbm.at[here], key_weight_ref, sem.at[1]),
        pltpu.make_async_copy(prefix_hbm, keys_ref.at[pl.ds(0, past)], sem.at[2]),
        pltpu.make_async_copy(fresh_hbm, keys_ref.at[pl.ds(past, slots)], sem.at[3]),
        pltpu.make_async_copy(value_weight_hbm.at[here], value_weight_ref, sem.at[4]),
    ]
    for copy in copies:
        copy.start()
    count, size = count_ref[0], size_ref[0]
    lane = lax.broadcasted_iota(jnp.int32, (slots, past), 1)
    cap_ref[:, :past] = jnp.where(lane < size, jnp.float32(OPEN), jnp.float32(MASKED))
    row = lax.broadcasted_iota(jnp.int32, (slots, slots), 0)
    col = lax.broadcasted_iota(jnp.int32, (slots, slots), 1)
    cap_ref[:, past:] = jnp.where(
        (col <= row) & (col < count * SPAN), jnp.float32(OPEN), jnp.float32(MASKED)
    )
    build_table(me_ref[0], count, routes_ref, table_ref, capacity, cores)
    for copy in copies:
        copy.wait()

    scale = math.log2(math.e) / math.sqrt(dim)
    keys = keys_ref[...]
    stacks = heads // STACK
    scores = []
    for stack in range(stacks):
        lifted = []
        for h in range(stack * STACK, (stack + 1) * STACK):
            one = dot(queries_ref[:, h * dim : (h + 1) * dim], key_weight_ref[h])
            lifted.append(one.astype(jnp.bfloat16))
        lifted = jnp.concatenate(lifted, axis=0)
        scores.append(lax.dot_general(lifted, keys, NT, preferred_element_type=jnp.float32))
    for stack in range(stacks):
        score = scores[stack].reshape(STACK, slots, keys.shape[0])
        score = jnp.minimum(score, cap_ref[...][None])
        highest = jnp.max(score, axis=-1, keepdims=True) * scale
        weights = jnp.exp2(score * scale - highest)
        total = jnp.sum(weights, axis=-1, keepdims=True)
        weights = weights.astype(jnp.bfloat16).reshape(STACK * slots, keys.shape[0])
        mixed = dot(weights, keys).astype(jnp.bfloat16)
        for g in range(STACK):
            h = stack * STACK + g
            projected = dot(mixed[g * slots : (g + 1) * slots], value_weight_ref[h])
            attended_ref[:, h * dim : (h + 1) * dim] = (projected / total[g]).astype(jnp.bfloat16)
    grouped = dot(table_ref[...], attended_ref[...]).astype(jnp.bfloat16)
    row = 0
    for out_ref in out_refs:
        out_ref[...] = grouped[row : row + out_ref.shape[0]]
        row += out_ref.shape[0]


def attend(
    first,
    heads,
    me,
    queries,
    key_weight,
    value_weight,
    prefix,
    fresh,
    count,
    size,
    routes,
    experts,
    parts,
    cores,
    after,
):
    slots = queries.shape[0]
    _, dim, latent = key_weight.shape
    places = slots * routes.shape[1]
    keys = prefix.shape[0] + slots
    smem = pl.BlockSpec(memory_space=pltpu.SMEM)
    vmem = pl.BlockSpec(memory_space=pltpu.VMEM)
    hbm = pl.BlockSpec(memory_space=pltpu.HBM)
    pieces = [jax.ShapeDtypeStruct((rows, heads * dim), jnp.bfloat16) for rows in parts]
    return pl.pallas_call(
        functools.partial(attend_kernel, places // experts, first, cores, len(after)),
        in_specs=[smem, smem, smem, vmem] + [hbm] * (5 + len(after)),
        out_specs=[vmem] * (len(pieces) + 1),
        out_shape=pieces + [jax.ShapeDtypeStruct(MARK, jnp.float32)],
        scratch_shapes=[
            pltpu.VMEM((slots, heads * dim), jnp.bfloat16),
            pltpu.VMEM((heads, dim, latent), jnp.bfloat16),
            pltpu.VMEM((heads, latent, dim), jnp.bfloat16),
            pltpu.VMEM((keys, latent), jnp.bfloat16),
            pltpu.VMEM((slots, keys), jnp.float32),
            pltpu.VMEM((places, slots), jnp.bfloat16),
            pltpu.VMEM((slots, heads * dim), jnp.bfloat16),
            pltpu.SemaphoreType.DMA((5,)),
        ],
        compiler_params=pltpu.CompilerParams(vmem_limit_bytes=VMEM if first else ALL_VMEM),
        cost_estimate=pl.CostEstimate(
            flops=4 * slots * heads * keys * latent,
            bytes_accessed=4 * heads * dim * latent,
            transcendentals=heads * slots * keys,
        ),
    )(me, count, size, routes.T, queries, key_weight, value_weight, prefix, fresh, *after)


def run_copies(copies):
    for copy in copies:
        copy.start()
    for copy in copies:
        copy.wait()


def join_kernel(*refs):
    *refs, sem = refs
    count = (len(refs) - 1) // 2
    copies = []
    for i, (kept_ref, out_ref) in enumerate(zip(refs[:count], refs[count + 1 :])):
        rows = kept_ref.shape[0]
        swapped = refs[count].at[pl.ds((i + 1) * rows, rows)]
        copies += [
            pltpu.make_async_copy(kept_ref, out_ref.at[pl.ds(0, rows)], sem.at[2 * i]),
            pltpu.make_async_copy(swapped, out_ref.at[pl.ds(rows, rows)], sem.at[2 * i + 1]),
        ]
    run_copies(copies)


def join(kept, swapped):
    rows, width = kept[0].shape
    return pl.pallas_call(
        join_kernel,
        in_specs=[pl.BlockSpec(memory_space=pl.ANY)] * (len(kept) + 1),
        out_specs=[pl.BlockSpec(memory_space=pltpu.VMEM)] * len(kept),
        out_shape=[jax.ShapeDtypeStruct((2 * rows, width), jnp.bfloat16)] * len(kept),
        scratch_shapes=[pltpu.SemaphoreType.DMA((2 * len(kept),))],
        compiler_params=pltpu.CompilerParams(vmem_limit_bytes=VMEM),
        cost_estimate=SHORT,
    )(*kept, swapped)


def place_kernel(plan, cores, me_ref, *refs):
    out_ref, sem = refs[-2:]
    _, _, capacity, features = out_ref.shape
    features //= cores
    me = me_ref[0]
    copies = []
    for ref, row, start, bits, apart in plan:
        ref = refs[ref]
        who = me ^ bits if apart else jnp.int32(bits)
        left = pl.multiple_of(who % cores * features + start, math.gcd(features, start))
        target = out_ref.at[0, who // cores, :, pl.ds(left, ref.shape[1])]
        copies.append(
            pltpu.make_async_copy(ref.at[pl.ds(row, capacity)], target, sem.at[len(copies)])
        )
    run_copies(copies)


def place(me, arrays, plan, cores, shape, placed):
    anywhere = pl.BlockSpec(memory_space=pl.ANY)
    operands = [me, *arrays, *placed]
    return pl.pallas_call(
        functools.partial(place_kernel, plan, cores),
        in_specs=[pl.BlockSpec(memory_space=pltpu.SMEM)]
        + [pl.BlockSpec(memory_space=pltpu.VMEM)] * len(arrays)
        + [anywhere] * len(placed),
        out_specs=anywhere,
        out_shape=jax.ShapeDtypeStruct(shape, jnp.bfloat16),
        scratch_shapes=[pltpu.SemaphoreType.DMA((len(plan),))],
        input_output_aliases={len(operands) - 1: 0} if placed else {},
        compiler_params=pltpu.CompilerParams(vmem_limit_bytes=VMEM),
    )(*operands)


def exchange_order(ranks):
    near, far = list(range(1, ranks // 2)), list(range(ranks // 2, ranks))
    return near[:-1] + far[::2] + far[1::2] + near[-1:]


def local(
    queries,
    key_weight,
    value_weight,
    prefix_latent,
    fresh_latent,
    span_counts,
    prefix_lengths,
    routes,
):
    ranks, cores = lax.axis_size("dp"), lax.axis_size("ep")
    experts = ranks * cores
    slots = queries.shape[0]
    heads, dim, _ = key_weight.shape
    capacity = slots * routes.shape[1] // experts
    direct = ranks <= DIRECT and capacity % 16 == 0
    me = (lax.axis_index("dp") * cores + lax.axis_index("ep")).astype(jnp.int32).reshape(1)
    nobody = jnp.zeros((1,), jnp.int32)
    shares = [heads * share // sum(CHUNKS) for share in CHUNKS]

    def run(chunk, order, parts, cores, after):
        return attend(
            sum(shares[:chunk]),
            shares[chunk],
            order,
            queries,
            key_weight,
            value_weight,
            prefix_latent,
            fresh_latent,
            span_counts,
            prefix_lengths,
            routes,
            experts,
            parts,
            cores,
            after,
        )

    def to_all(outgoing):
        return lax.all_to_all(
            outgoing.reshape(experts, capacity, -1),
            ("dp", "ep"),
            split_axis=0,
            concat_axis=0,
            tiled=True,
        )

    if not direct:
        outgoing = [run(chunk, nobody, [experts * capacity], 1, [])[0] for chunk in range(len(shares))]
        arrived = jnp.concatenate([to_all(rows) for rows in outgoing], axis=2)
        arrived = arrived.reshape(ranks, cores, capacity, -1).transpose(0, 2, 1, 3)
        return arrived.reshape(1, ranks, capacity, cores * heads * dim)
    opening, mark = run(0, nobody, [experts * capacity], 1, [])
    first = to_all(opening).reshape(experts * capacity, -1)
    parts = [capacity] * ranks + [(cores - 1) * ranks * capacity]
    *kept, message, mark = run(1, me, parts, cores, [mark])
    swapped = lax.ppermute(message, "ep", [(i, i ^ 1) for i in range(cores)])
    order = exchange_order(ranks)
    joined = dict(zip(range(1, ranks), join(kept[1:], swapped)))
    middle = shares[0] * dim
    soon, late = [first, kept[0], swapped], []
    soon_plan = [(0, i * capacity, 0, i, False) for i in range(experts)]
    soon_plan += [(1, 0, middle, 0, True), (2, 0, middle, 1, True)]
    late_plan = []
    for j in order:
        piece = lax.ppermute(joined[j], "dp", [(i, i ^ j) for i in range(ranks)])
        arrays, plan = (soon, soon_plan) if j < ranks // 2 else (late, late_plan)
        plan.append((len(arrays), 0, middle, j * cores, True))
        plan.append((len(arrays), capacity, middle, j * cores + 1, True))
        arrays.append(piece)
    shape = (1, ranks, capacity, cores * heads * dim)
    placed = place(me, soon, soon_plan, cores, shape, [])
    return place(me, late, late_plan, cores, shape, [placed])


def solution(mesh):
    in_specs = (
        P(("groups", "dp"), "ep"),
        P("ep", None, None),
        P("ep", None, None),
        P(("groups", "dp"), None),
        P(("groups", "dp"), None),
        P(("groups", "dp")),
        P(("groups", "dp")),
        P(("groups", "dp"), None),
    )
    out_specs = P(("groups", "dp", "ep"), None, None, None)
    return jax.shard_map(local, mesh=mesh, in_specs=in_specs, out_specs=out_specs, check_vma=False)
```

```python
import functools
import math

import jax
import jax.numpy as jnp
from jax import lax
from jax.experimental import pallas as pl
from jax.experimental.pallas import tpu as pltpu
from jax.sharding import PartitionSpec as P

SPAN = 64
STACK = 4
CHUNKS = (1, 1)
DIRECT = 16
ALL_VMEM = 60 * 1024 * 1024
VMEM = 52 * 1024 * 1024
SHORT = pl.CostEstimate(flops=0, bytes_accessed=0, transcendentals=0)
MARK = (8, 128)
MASKED = -1e30
OPEN = 3e38
NT = (((1,), (1,)), ((), ()))


def dot(left, right):
    return jnp.dot(left, right, preferred_element_type=jnp.float32)


def build_table(me, count, routes_ref, table_ref, capacity, cores):
    slots = routes_ref.shape[1]
    rows = table_ref.shape[0]
    place = lax.broadcasted_iota(jnp.int32, (rows, slots), 0)
    token = lax.broadcasted_iota(jnp.int32, (rows, slots), 1)
    block = place // capacity
    chips = rows // (capacity * cores)
    expert = ((block % chips) * cores + block // chips) ^ me
    hit = ((routes_ref[0:1, :] == expert) | (routes_ref[1:2, :] == expert)) & (
        token < count * SPAN
    )
    hit = jnp.where(hit, jnp.float32(1.0), jnp.float32(0.0))
    first = lax.broadcasted_iota(jnp.int32, (slots, slots), 0)
    second = lax.broadcasted_iota(jnp.int32, (slots, slots), 1)
    earlier = jnp.where(first < second, jnp.float32(1.0), jnp.float32(0.0))
    before = dot(hit.astype(jnp.bfloat16), earlier.astype(jnp.bfloat16))
    wanted = (place - block * capacity).astype(jnp.float32)
    table_ref[...] = jnp.where(before == wanted, hit, jnp.float32(0.0)).astype(jnp.bfloat16)


def attend_kernel(
    capacity,
    first,
    cores,
    after,
    me_ref,
    count_ref,
    size_ref,
    routes_ref,
    queries_hbm,
    key_weight_hbm,
    value_weight_hbm,
    prefix_hbm,
    fresh_hbm,
    *rest,
):
    *out_refs, mark_ref, queries_ref, key_weight_ref, value_weight_ref, keys_ref = rest[after:-5]
    mark_ref[...] = jnp.zeros_like(mark_ref)
    cap_ref, table_ref, attended_ref, rows_ref, sem = rest[-5:]
    staged = len(out_refs) == 1
    slots = queries_ref.shape[0]
    past = prefix_hbm.shape[0]
    heads, dim, _ = key_weight_ref.shape
    copies = []

    def start_copy(source, target, queue):
        copies.append(pltpu.make_async_copy(source, target, sem.at[len(copies)]))
        copies[-1].start(priority=queue)

    half = heads // 2
    halves = [(pl.ds(first + i * half, half), pl.ds(i * half, half), i) for i in range(2)]
    for there, here, queue in halves:
        start_copy(key_weight_hbm.at[there], key_weight_ref.at[here], queue)
    start_copy(queries_hbm.at[:, pl.ds(first * dim, heads * dim)], queries_ref, 1)
    start_copy(prefix_hbm, keys_ref.at[pl.ds(0, past)], 0)
    start_copy(fresh_hbm, keys_ref.at[pl.ds(past, slots)], 1)
    for there, here, queue in halves:
        start_copy(value_weight_hbm.at[there], value_weight_ref.at[here], queue)
    count, size = count_ref[0], size_ref[0]
    lane = lax.broadcasted_iota(jnp.int32, (slots, past), 1)
    cap_ref[:, :past] = jnp.where(lane < size, jnp.float32(OPEN), jnp.float32(MASKED))
    row = lax.broadcasted_iota(jnp.int32, (slots, slots), 0)
    col = lax.broadcasted_iota(jnp.int32, (slots, slots), 1)
    cap_ref[:, past:] = jnp.where(
        (col <= row) & (col < count * SPAN), jnp.float32(OPEN), jnp.float32(MASKED)
    )
    build_table(me_ref[0], count, routes_ref, table_ref, capacity, cores)
    for copy in copies:
        copy.wait()

    sends = []
    scale = math.log2(math.e) / math.sqrt(dim)
    keys = keys_ref[...]
    stacks = heads // STACK
    scores = []
    for stack in range(stacks):
        lifted = []
        for h in range(stack * STACK, (stack + 1) * STACK):
            one = dot(queries_ref[:, h * dim : (h + 1) * dim], key_weight_ref[h])
            lifted.append(one.astype(jnp.bfloat16))
        lifted = jnp.concatenate(lifted, axis=0)
        scores.append(lax.dot_general(lifted, keys, NT, preferred_element_type=jnp.float32))
    for stack in range(stacks):
        score = scores[stack].reshape(STACK, slots, keys.shape[0])
        score = jnp.minimum(score, cap_ref[...][None])
        highest = jnp.max(score, axis=-1, keepdims=True) * scale
        weights = jnp.exp2(score * scale - highest)
        total = jnp.sum(weights, axis=-1, keepdims=True)
        weights = weights.astype(jnp.bfloat16).reshape(STACK * slots, keys.shape[0])
        mixed = dot(weights, keys).astype(jnp.bfloat16)
        for g in range(STACK):
            h = stack * STACK + g
            projected = dot(mixed[g * slots : (g + 1) * slots], value_weight_ref[h])
            attended_ref[:, h * dim : (h + 1) * dim] = (projected / total[g]).astype(jnp.bfloat16)
        if staged and 2 * (stack + 1) % stacks == 0:
            i = 2 * (stack + 1) // stacks - 1
            columns = pl.ds(i * half * dim, half * dim)
            rows_ref[i] = dot(table_ref[...], attended_ref[:, columns]).astype(jnp.bfloat16)
            sends.append(
                pltpu.make_async_copy(rows_ref.at[i], out_refs[0].at[:, columns], sem.at[7 + i])
            )
            sends[-1].start()
    for send in sends:
        send.wait()
    if staged:
        return
    grouped = dot(table_ref[...], attended_ref[...]).astype(jnp.bfloat16)
    row = 0
    for out_ref in out_refs:
        out_ref[...] = grouped[row : row + out_ref.shape[0]]
        row += out_ref.shape[0]


def attend(
    first,
    heads,
    me,
    queries,
    key_weight,
    value_weight,
    prefix,
    fresh,
    count,
    size,
    routes,
    experts,
    parts,
    cores,
    after,
):
    slots = queries.shape[0]
    _, dim, latent = key_weight.shape
    places = slots * routes.shape[1]
    keys = prefix.shape[0] + slots
    smem = pl.BlockSpec(memory_space=pltpu.SMEM)
    vmem = pl.BlockSpec(memory_space=pltpu.VMEM)
    hbm = pl.BlockSpec(memory_space=pltpu.HBM)
    pieces = [jax.ShapeDtypeStruct((rows, heads * dim), jnp.bfloat16) for rows in parts]
    return pl.pallas_call(
        functools.partial(attend_kernel, places // experts, first, cores, len(after)),
        in_specs=[smem, smem, smem, vmem] + [hbm] * (5 + len(after)),
        out_specs=[vmem if len(pieces) > 1 else hbm] * len(pieces) + [vmem],
        out_shape=pieces + [jax.ShapeDtypeStruct(MARK, jnp.float32)],
        scratch_shapes=[
            pltpu.VMEM((slots, heads * dim), jnp.bfloat16),
            pltpu.VMEM((heads, dim, latent), jnp.bfloat16),
            pltpu.VMEM((heads, latent, dim), jnp.bfloat16),
            pltpu.VMEM((keys, latent), jnp.bfloat16),
            pltpu.VMEM((slots, keys), jnp.float32),
            pltpu.VMEM((places, slots), jnp.bfloat16),
            pltpu.VMEM((slots, heads * dim), jnp.bfloat16),
            pltpu.VMEM((2, places, heads // 2 * dim), jnp.bfloat16),
            pltpu.SemaphoreType.DMA((7 + 2,)),
        ],
        compiler_params=pltpu.CompilerParams(vmem_limit_bytes=VMEM if first else ALL_VMEM),
        cost_estimate=pl.CostEstimate(
            flops=4 * slots * heads * keys * latent,
            bytes_accessed=4 * heads * dim * latent,
            transcendentals=heads * slots * keys,
        ),
    )(me, count, size, routes.T, queries, key_weight, value_weight, prefix, fresh, *after)


def run_copies(copies):
    for copy in copies:
        copy.start()
    for copy in copies:
        copy.wait()


def join_kernel(*refs):
    *refs, sem = refs
    count = (len(refs) - 1) // 2
    copies = []
    for i, (kept_ref, out_ref) in enumerate(zip(refs[:count], refs[count + 1 :])):
        rows = kept_ref.shape[0]
        swapped = refs[count].at[pl.ds((i + 1) * rows, rows)]
        copies += [
            pltpu.make_async_copy(kept_ref, out_ref.at[pl.ds(0, rows)], sem.at[2 * i]),
            pltpu.make_async_copy(swapped, out_ref.at[pl.ds(rows, rows)], sem.at[2 * i + 1]),
        ]
    run_copies(copies)


def join(kept, swapped):
    rows, width = kept[0].shape
    return pl.pallas_call(
        join_kernel,
        in_specs=[pl.BlockSpec(memory_space=pl.ANY)] * (len(kept) + 1),
        out_specs=[pl.BlockSpec(memory_space=pltpu.VMEM)] * len(kept),
        out_shape=[jax.ShapeDtypeStruct((2 * rows, width), jnp.bfloat16)] * len(kept),
        scratch_shapes=[pltpu.SemaphoreType.DMA((2 * len(kept),))],
        compiler_params=pltpu.CompilerParams(vmem_limit_bytes=VMEM),
        cost_estimate=SHORT,
    )(*kept, swapped)


def place_kernel(plan, cores, me_ref, *refs):
    out_ref, sem = refs[-2:]
    _, _, capacity, features = out_ref.shape
    features //= cores
    me = me_ref[0]
    copies = []
    for ref, row, start, bits, apart in plan:
        ref = refs[ref]
        who = me ^ bits if apart else jnp.int32(bits)
        left = pl.multiple_of(who % cores * features + start, math.gcd(features, start))
        target = out_ref.at[0, who // cores, :, pl.ds(left, ref.shape[1])]
        copies.append(
            pltpu.make_async_copy(ref.at[pl.ds(row, capacity)], target, sem.at[len(copies)])
        )
    run_copies(copies)


def place(me, arrays, plan, cores, shape, placed):
    anywhere = pl.BlockSpec(memory_space=pl.ANY)
    operands = [me, *arrays, *placed]
    return pl.pallas_call(
        functools.partial(place_kernel, plan, cores),
        in_specs=[pl.BlockSpec(memory_space=pltpu.SMEM)]
        + [pl.BlockSpec(memory_space=pltpu.VMEM)] * len(arrays)
        + [anywhere] * len(placed),
        out_specs=anywhere,
        out_shape=jax.ShapeDtypeStruct(shape, jnp.bfloat16),
        scratch_shapes=[pltpu.SemaphoreType.DMA((len(plan),))],
        input_output_aliases={len(operands) - 1: 0} if placed else {},
        compiler_params=pltpu.CompilerParams(vmem_limit_bytes=VMEM),
    )(*operands)


def exchange_order(ranks):
    near, far = list(range(1, ranks // 2)), list(range(ranks // 2, ranks))
    return near[:-1] + far[::2] + far[1::2] + near[-1:]


def local(
    queries,
    key_weight,
    value_weight,
    prefix_latent,
    fresh_latent,
    span_counts,
    prefix_lengths,
    routes,
):
    ranks, cores = lax.axis_size("dp"), lax.axis_size("ep")
    experts = ranks * cores
    slots = queries.shape[0]
    heads, dim, _ = key_weight.shape
    capacity = slots * routes.shape[1] // experts
    direct = ranks <= DIRECT and capacity % 16 == 0
    me = (lax.axis_index("dp") * cores + lax.axis_index("ep")).astype(jnp.int32).reshape(1)
    nobody = jnp.zeros((1,), jnp.int32)
    shares = [heads * share // sum(CHUNKS) for share in CHUNKS]

    def run(chunk, order, parts, cores, after):
        return attend(
            sum(shares[:chunk]),
            shares[chunk],
            order,
            queries,
            key_weight,
            value_weight,
            prefix_latent,
            fresh_latent,
            span_counts,
            prefix_lengths,
            routes,
            experts,
            parts,
            cores,
            after,
        )

    def to_all(outgoing):
        return lax.all_to_all(
            outgoing.reshape(experts, capacity, -1),
            ("dp", "ep"),
            split_axis=0,
            concat_axis=0,
            tiled=True,
        )

    if not direct:
        outgoing = [run(chunk, nobody, [experts * capacity], 1, [])[0] for chunk in range(len(shares))]
        arrived = jnp.concatenate([to_all(rows) for rows in outgoing], axis=2)
        arrived = arrived.reshape(ranks, cores, capacity, -1).transpose(0, 2, 1, 3)
        return arrived.reshape(1, ranks, capacity, cores * heads * dim)
    opening, mark = run(0, nobody, [experts * capacity], 1, [])
    first = to_all(opening).reshape(experts * capacity, -1)
    parts = [capacity] * ranks + [(cores - 1) * ranks * capacity]
    *kept, message, mark = run(1, me, parts, cores, [mark])
    swapped = lax.ppermute(message, "ep", [(i, i ^ 1) for i in range(cores)])
    order = exchange_order(ranks)
    joined = dict(zip(range(1, ranks), join(kept[1:], swapped)))
    middle = shares[0] * dim
    soon, late = [first, kept[0], swapped], []
    soon_plan = [(0, i * capacity, 0, i, False) for i in range(experts)]
    soon_plan += [(1, 0, middle, 0, True), (2, 0, middle, 1, True)]
    late_plan = []
    for j in order:
        piece = lax.ppermute(joined[j], "dp", [(i, i ^ j) for i in range(ranks)])
        arrays, plan = (soon, soon_plan) if j < ranks // 2 else (late, late_plan)
        plan.append((len(arrays), 0, middle, j * cores, True))
        plan.append((len(arrays), capacity, middle, j * cores + 1, True))
        arrays.append(piece)
    shape = (1, ranks, capacity, cores * heads * dim)
    placed = place(me, soon, soon_plan, cores, shape, [])
    return place(me, late, late_plan, cores, shape, [placed])


def solution(mesh):
    in_specs = (
        P(("groups", "dp"), "ep"),
        P("ep", None, None),
        P("ep", None, None),
        P(("groups", "dp"), None),
        P(("groups", "dp"), None),
        P(("groups", "dp")),
        P(("groups", "dp")),
        P(("groups", "dp"), None),
    )
    out_specs = P(("groups", "dp", "ep"), None, None, None)
    return jax.shard_map(local, mesh=mesh, in_specs=in_specs, out_specs=out_specs, check_vma=False)
```

```python
import functools
import math

import jax
import jax.numpy as jnp
from jax import lax
from jax.experimental import pallas as pl
from jax.experimental.pallas import tpu as pltpu
from jax.sharding import PartitionSpec as P

SPAN = 64
STACK = 4
CHUNKS = (7, 9)
DIRECT = 16
ALL_VMEM = 63_400_000
VMEM = 51 * 1024 * 1024
SHORT = pl.CostEstimate(flops=0, bytes_accessed=0, transcendentals=0)
MARK = (8, 128)
MASKED = -1e30
OPEN = 3e38
NT = (((1,), (1,)), ((), ()))


def dot(left, right):
    return jnp.dot(left, right, preferred_element_type=jnp.float32)


def build_table(me, count, routes_ref, table_ref, capacity, cores):
    slots = routes_ref.shape[1]
    rows = table_ref.shape[0]
    place = lax.broadcasted_iota(jnp.int32, (rows, slots), 0)
    token = lax.broadcasted_iota(jnp.int32, (rows, slots), 1)
    block = place // capacity
    chips = rows // (capacity * cores)
    expert = ((block % chips) * cores + block // chips) ^ me
    hit = ((routes_ref[0:1, :] == expert) | (routes_ref[1:2, :] == expert)) & (
        token < count * SPAN
    )
    hit = jnp.where(hit, jnp.float32(1.0), jnp.float32(0.0))
    first = lax.broadcasted_iota(jnp.int32, (slots, slots), 0)
    second = lax.broadcasted_iota(jnp.int32, (slots, slots), 1)
    earlier = jnp.where(first < second, jnp.float32(1.0), jnp.float32(0.0))
    before = dot(hit.astype(jnp.bfloat16), earlier.astype(jnp.bfloat16))
    wanted = (place - block * capacity).astype(jnp.float32)
    table_ref[...] = jnp.where(before == wanted, hit, jnp.float32(0.0)).astype(jnp.bfloat16)


def attend_kernel(
    capacity,
    first,
    cores,
    after,
    me_ref,
    count_ref,
    size_ref,
    routes_ref,
    queries_hbm,
    key_weight_hbm,
    value_weight_hbm,
    prefix_hbm,
    fresh_hbm,
    *rest,
):
    *out_refs, mark_ref, queries_ref, key_weight_ref, value_weight_ref, keys_ref = rest[after:-4]
    mark_ref[...] = jnp.zeros_like(mark_ref)
    cap_ref, table_ref, attended_ref, sem = rest[-4:]
    slots = queries_ref.shape[0]
    past = prefix_hbm.shape[0]
    heads, dim, _ = key_weight_ref.shape
    here = pl.ds(first, heads)
    here = pl.ds(first, heads)
    copies = [
        pltpu.make_async_copy(
            queries_hbm.at[:, pl.ds(first * dim, heads * dim)], queries_ref, sem.at[0]
        ),
        pltpu.make_async_copy(key_weight_hbm.at[here], key_weight_ref, sem.at[1]),
        pltpu.make_async_copy(prefix_hbm, keys_ref.at[pl.ds(0, past)], sem.at[2]),
        pltpu.make_async_copy(fresh_hbm, keys_ref.at[pl.ds(past, slots)], sem.at[3]),
        pltpu.make_async_copy(value_weight_hbm.at[here], value_weight_ref, sem.at[4]),
    ]
    for copy in copies:
        copy.start()
    count, size = count_ref[0], size_ref[0]
    lane = lax.broadcasted_iota(jnp.int32, (slots, past), 1)
    cap_ref[:, :past] = jnp.where(lane < size, jnp.float32(OPEN), jnp.float32(MASKED))
    row = lax.broadcasted_iota(jnp.int32, (slots, slots), 0)
    col = lax.broadcasted_iota(jnp.int32, (slots, slots), 1)
    cap_ref[:, past:] = jnp.where(
        (col <= row) & (col < count * SPAN), jnp.float32(OPEN), jnp.float32(MASKED)
    )
    build_table(me_ref[0], count, routes_ref, table_ref, capacity, cores)
    for copy in copies:
        copy.wait()

    scale = math.log2(math.e) / math.sqrt(dim)
    keys = keys_ref[...]
    stacks = [range(h, min(h + STACK, heads)) for h in range(0, heads, STACK)]
    scores = []
    for stack in stacks:
        lifted = []
        for h in stack:
            one = dot(queries_ref[:, h * dim : (h + 1) * dim], key_weight_ref[h])
            lifted.append(one.astype(jnp.bfloat16))
        lifted = jnp.concatenate(lifted, axis=0)
        scores.append(lax.dot_general(lifted, keys, NT, preferred_element_type=jnp.float32))
    for stack, score in zip(stacks, scores):
        score = score.reshape(len(stack), slots, keys.shape[0])
        score = jnp.minimum(score, cap_ref[...][None])
        highest = jnp.max(score, axis=-1, keepdims=True) * scale
        weights = jnp.exp2(score * scale - highest)
        total = jnp.sum(weights, axis=-1, keepdims=True)
        weights = weights.astype(jnp.bfloat16).reshape(len(stack) * slots, keys.shape[0])
        mixed = dot(weights, keys).astype(jnp.bfloat16)
        for g, h in enumerate(stack):
            projected = dot(mixed[g * slots : (g + 1) * slots], value_weight_ref[h])
            attended_ref[:, h * dim : (h + 1) * dim] = (projected / total[g]).astype(jnp.bfloat16)
    grouped = dot(table_ref[...], attended_ref[...]).astype(jnp.bfloat16)
    row = 0
    for out_ref in out_refs:
        out_ref[...] = grouped[row : row + out_ref.shape[0]]
        row += out_ref.shape[0]


def attend(
    first,
    heads,
    me,
    queries,
    key_weight,
    value_weight,
    prefix,
    fresh,
    count,
    size,
    routes,
    experts,
    parts,
    cores,
    after,
):
    slots = queries.shape[0]
    _, dim, latent = key_weight.shape
    places = slots * routes.shape[1]
    keys = prefix.shape[0] + slots
    smem = pl.BlockSpec(memory_space=pltpu.SMEM)
    vmem = pl.BlockSpec(memory_space=pltpu.VMEM)
    hbm = pl.BlockSpec(memory_space=pltpu.HBM)
    pieces = [jax.ShapeDtypeStruct((rows, heads * dim), jnp.bfloat16) for rows in parts]
    return pl.pallas_call(
        functools.partial(attend_kernel, places // experts, first, cores, len(after)),
        in_specs=[smem, smem, smem, vmem] + [hbm] * (5 + len(after)),
        out_specs=[vmem] * (len(pieces) + 1),
        out_shape=pieces + [jax.ShapeDtypeStruct(MARK, jnp.float32)],
        scratch_shapes=[
            pltpu.VMEM((slots, heads * dim), jnp.bfloat16),
            pltpu.VMEM((heads, dim, latent), jnp.bfloat16),
            pltpu.VMEM((heads, latent, dim), jnp.bfloat16),
            pltpu.VMEM((keys, latent), jnp.bfloat16),
            pltpu.VMEM((slots, keys), jnp.float32),
            pltpu.VMEM((places, slots), jnp.bfloat16),
            pltpu.VMEM((slots, heads * dim), jnp.bfloat16),
            pltpu.SemaphoreType.DMA((5,)),
        ],
        compiler_params=pltpu.CompilerParams(vmem_limit_bytes=VMEM if first else ALL_VMEM),
        cost_estimate=pl.CostEstimate(
            flops=4 * slots * heads * keys * latent,
            bytes_accessed=4 * heads * dim * latent,
            transcendentals=heads * slots * keys,
        ),
    )(me, count, size, routes.T, queries, key_weight, value_weight, prefix, fresh, *after)


def run_copies(copies):
    for copy in copies:
        copy.start()
    for copy in copies:
        copy.wait()


def join_kernel(*refs):
    *refs, sem = refs
    count = (len(refs) - 1) // 2
    copies = []
    for i, (kept_ref, out_ref) in enumerate(zip(refs[:count], refs[count + 1 :])):
        rows = kept_ref.shape[0]
        swapped = refs[count].at[pl.ds((i + 1) * rows, rows)]
        copies += [
            pltpu.make_async_copy(kept_ref, out_ref.at[pl.ds(0, rows)], sem.at[2 * i]),
            pltpu.make_async_copy(swapped, out_ref.at[pl.ds(rows, rows)], sem.at[2 * i + 1]),
        ]
    run_copies(copies)


def join(kept, swapped):
    rows, width = kept[0].shape
    return pl.pallas_call(
        join_kernel,
        in_specs=[pl.BlockSpec(memory_space=pl.ANY)] * (len(kept) + 1),
        out_specs=[pl.BlockSpec(memory_space=pltpu.VMEM)] * len(kept),
        out_shape=[jax.ShapeDtypeStruct((2 * rows, width), jnp.bfloat16)] * len(kept),
        scratch_shapes=[pltpu.SemaphoreType.DMA((2 * len(kept),))],
        compiler_params=pltpu.CompilerParams(vmem_limit_bytes=VMEM),
        cost_estimate=SHORT,
    )(*kept, swapped)


def place_kernel(plan, cores, me_ref, *refs):
    out_ref, sem = refs[-2:]
    _, _, capacity, features = out_ref.shape
    features //= cores
    me = me_ref[0]
    copies = []
    for ref, row, start, bits, apart in plan:
        ref = refs[ref]
        who = me ^ bits if apart else jnp.int32(bits)
        left = pl.multiple_of(who % cores * features + start, math.gcd(features, start))
        target = out_ref.at[0, who // cores, :, pl.ds(left, ref.shape[1])]
        copies.append(
            pltpu.make_async_copy(ref.at[pl.ds(row, capacity)], target, sem.at[len(copies)])
        )
    run_copies(copies)


def place(me, arrays, plan, cores, shape, placed):
    anywhere = pl.BlockSpec(memory_space=pl.ANY)
    operands = [me, *arrays, *placed]
    return pl.pallas_call(
        functools.partial(place_kernel, plan, cores),
        in_specs=[pl.BlockSpec(memory_space=pltpu.SMEM)]
        + [pl.BlockSpec(memory_space=pltpu.VMEM)] * len(arrays)
        + [anywhere] * len(placed),
        out_specs=anywhere,
        out_shape=jax.ShapeDtypeStruct(shape, jnp.bfloat16),
        scratch_shapes=[pltpu.SemaphoreType.DMA((len(plan),))],
        input_output_aliases={len(operands) - 1: 0} if placed else {},
        compiler_params=pltpu.CompilerParams(vmem_limit_bytes=VMEM),
    )(*operands)


def exchange_order(ranks):
    near, far = list(range(1, ranks // 2)), list(range(ranks // 2, ranks))
    return far[:1] + near + far[2::2] + far[1::2]


def local(
    queries,
    key_weight,
    value_weight,
    prefix_latent,
    fresh_latent,
    span_counts,
    prefix_lengths,
    routes,
):
    ranks, cores = lax.axis_size("dp"), lax.axis_size("ep")
    experts = ranks * cores
    slots = queries.shape[0]
    heads, dim, _ = key_weight.shape
    capacity = slots * routes.shape[1] // experts
    direct = ranks <= DIRECT and capacity % 16 == 0
    me = (lax.axis_index("dp") * cores + lax.axis_index("ep")).astype(jnp.int32).reshape(1)
    nobody = jnp.zeros((1,), jnp.int32)
    shares = [heads * share // sum(CHUNKS) for share in CHUNKS]

    def run(chunk, order, parts, cores, after):
        return attend(
            sum(shares[:chunk]),
            shares[chunk],
            order,
            queries,
            key_weight,
            value_weight,
            prefix_latent,
            fresh_latent,
            span_counts,
            prefix_lengths,
            routes,
            experts,
            parts,
            cores,
            after,
        )

    def to_all(outgoing):
        return lax.all_to_all(
            outgoing.reshape(experts, capacity, -1),
            ("dp", "ep"),
            split_axis=0,
            concat_axis=0,
            tiled=True,
        )

    if not direct:
        outgoing = [run(chunk, nobody, [experts * capacity], 1, [])[0] for chunk in range(len(shares))]
        arrived = jnp.concatenate([to_all(rows) for rows in outgoing], axis=2)
        arrived = arrived.reshape(ranks, cores, capacity, -1).transpose(0, 2, 1, 3)
        return arrived.reshape(1, ranks, capacity, cores * heads * dim)
    opening, mark = run(0, nobody, [experts * capacity], 1, [])
    first = to_all(opening).reshape(experts * capacity, -1)
    parts = [capacity] * ranks + [(cores - 1) * ranks * capacity]
    *kept, message, mark = run(1, me, parts, cores, [mark])
    swapped = lax.ppermute(message, "ep", [(i, i ^ 1) for i in range(cores)])
    order = exchange_order(ranks)
    joined = dict(zip(range(1, ranks), join(kept[1:], swapped)))
    middle = shares[0] * dim
    soon, late = [first, kept[0], swapped], []
    soon_plan = [(0, i * capacity, 0, i, False) for i in range(experts)]
    soon_plan += [(1, 0, middle, 0, True), (2, 0, middle, 1, True)]
    late_plan = []
    for j in order:
        piece = lax.ppermute(joined[j], "dp", [(i, i ^ j) for i in range(ranks)])
        late_plan.append((len(late), 0, middle, j * cores, True))
        late_plan.append((len(late), capacity, middle, j * cores + 1, True))
        late.append(piece)
    shape = (1, ranks, capacity, cores * heads * dim)
    placed = place(me, soon, soon_plan, cores, shape, [])
    return place(me, late, late_plan, cores, shape, [placed])


def solution(mesh):
    in_specs = (
        P(("groups", "dp"), "ep"),
        P("ep", None, None),
        P("ep", None, None),
        P(("groups", "dp"), None),
        P(("groups", "dp"), None),
        P(("groups", "dp")),
        P(("groups", "dp")),
        P(("groups", "dp"), None),
    )
    out_specs = P(("groups", "dp", "ep"), None, None, None)
    return jax.shard_map(local, mesh=mesh, in_specs=in_specs, out_specs=out_specs, check_vma=False)
```

```python
import functools
import math

import jax
import jax.numpy as jnp
from jax import lax
from jax.experimental import pallas as pl
from jax.experimental.pallas import tpu as pltpu
from jax.sharding import PartitionSpec as P

SPAN = 64
STACK = 4
CHUNKS = (7, 9)
DIRECT = 16
ALL_VMEM = 63_400_000
VMEM = 51 * 1024 * 1024
SHORT = pl.CostEstimate(flops=0, bytes_accessed=0, transcendentals=0)
MARK = (8, 128)
MASKED = -1e30
OPEN = 3e38
NT = (((1,), (1,)), ((), ()))


def dot(left, right):
    return jnp.dot(left, right, preferred_element_type=jnp.float32)


def build_table(me, count, routes_ref, table_ref, capacity, cores):
    slots = routes_ref.shape[1]
    rows = table_ref.shape[0]
    place = lax.broadcasted_iota(jnp.int32, (rows, slots), 0)
    token = lax.broadcasted_iota(jnp.int32, (rows, slots), 1)
    block = place // capacity
    chips = rows // (capacity * cores)
    expert = ((block % chips) * cores + block // chips) ^ me
    hit = ((routes_ref[0:1, :] == expert) | (routes_ref[1:2, :] == expert)) & (
        token < count * SPAN
    )
    hit = jnp.where(hit, jnp.float32(1.0), jnp.float32(0.0))
    first = lax.broadcasted_iota(jnp.int32, (slots, slots), 0)
    second = lax.broadcasted_iota(jnp.int32, (slots, slots), 1)
    earlier = jnp.where(first < second, jnp.float32(1.0), jnp.float32(0.0))
    before = dot(hit.astype(jnp.bfloat16), earlier.astype(jnp.bfloat16))
    wanted = (place - block * capacity).astype(jnp.float32)
    table_ref[...] = jnp.where(before == wanted, hit, jnp.float32(0.0)).astype(jnp.bfloat16)


def attend_kernel(
    capacity,
    first,
    cores,
    after,
    me_ref,
    count_ref,
    size_ref,
    routes_ref,
    queries_hbm,
    key_weight_hbm,
    value_weight_hbm,
    prefix_hbm,
    fresh_hbm,
    *rest,
):
    *out_refs, mark_ref, queries_ref, key_weight_ref, value_weight_ref, keys_ref = rest[after:-4]
    mark_ref[...] = jnp.zeros_like(mark_ref)
    cap_ref, table_ref, attended_ref, sem = rest[-4:]
    slots = queries_ref.shape[0]
    past = prefix_hbm.shape[0]
    heads, dim, _ = key_weight_ref.shape
    here = pl.ds(first, heads)
    here = pl.ds(first, heads)
    copies = [
        pltpu.make_async_copy(
            queries_hbm.at[:, pl.ds(first * dim, heads * dim)], queries_ref, sem.at[0]
        ),
        pltpu.make_async_copy(key_weight_hbm.at[here], key_weight_ref, sem.at[1]),
        pltpu.make_async_copy(prefix_hbm, keys_ref.at[pl.ds(0, past)], sem.at[2]),
        pltpu.make_async_copy(fresh_hbm, keys_ref.at[pl.ds(past, slots)], sem.at[3]),
        pltpu.make_async_copy(value_weight_hbm.at[here], value_weight_ref, sem.at[4]),
    ]
    for copy in copies:
        copy.start()
    count, size = count_ref[0], size_ref[0]
    lane = lax.broadcasted_iota(jnp.int32, (slots, past), 1)
    cap_ref[:, :past] = jnp.where(lane < size, jnp.float32(OPEN), jnp.float32(MASKED))
    row = lax.broadcasted_iota(jnp.int32, (slots, slots), 0)
    col = lax.broadcasted_iota(jnp.int32, (slots, slots), 1)
    cap_ref[:, past:] = jnp.where(
        (col <= row) & (col < count * SPAN), jnp.float32(OPEN), jnp.float32(MASKED)
    )
    build_table(me_ref[0], count, routes_ref, table_ref, capacity, cores)
    for copy in copies:
        copy.wait()

    scale = math.log2(math.e) / math.sqrt(dim)
    keys = keys_ref[...]
    stacks = [range(h, min(h + STACK, heads)) for h in range(0, heads, STACK)]
    scores = []
    for stack in stacks:
        lifted = []
        for h in stack:
            one = dot(queries_ref[:, h * dim : (h + 1) * dim], key_weight_ref[h])
            lifted.append(one.astype(jnp.bfloat16))
        lifted = jnp.concatenate(lifted, axis=0)
        scores.append(lax.dot_general(lifted, keys, NT, preferred_element_type=jnp.float32))
    for stack, score in zip(stacks, scores):
        score = score.reshape(len(stack), slots, keys.shape[0])
        score = jnp.minimum(score, cap_ref[...][None])
        highest = jnp.max(score, axis=-1, keepdims=True) * scale
        weights = jnp.exp2(score * scale - highest)
        total = jnp.sum(weights, axis=-1, keepdims=True)
        weights = weights.astype(jnp.bfloat16).reshape(len(stack) * slots, keys.shape[0])
        mixed = dot(weights, keys).astype(jnp.bfloat16)
        for g, h in enumerate(stack):
            projected = dot(mixed[g * slots : (g + 1) * slots], value_weight_ref[h])
            attended_ref[:, h * dim : (h + 1) * dim] = (projected / total[g]).astype(jnp.bfloat16)
    grouped = dot(table_ref[...], attended_ref[...]).astype(jnp.bfloat16)
    row = 0
    for out_ref in out_refs:
        out_ref[...] = grouped[row : row + out_ref.shape[0]]
        row += out_ref.shape[0]


def attend(
    first,
    heads,
    me,
    queries,
    key_weight,
    value_weight,
    prefix,
    fresh,
    count,
    size,
    routes,
    experts,
    parts,
    cores,
    after,
):
    slots = queries.shape[0]
    _, dim, latent = key_weight.shape
    places = slots * routes.shape[1]
    keys = prefix.shape[0] + slots
    smem = pl.BlockSpec(memory_space=pltpu.SMEM)
    vmem = pl.BlockSpec(memory_space=pltpu.VMEM)
    hbm = pl.BlockSpec(memory_space=pltpu.HBM)
    pieces = [jax.ShapeDtypeStruct((rows, heads * dim), jnp.bfloat16) for rows in parts]
    return pl.pallas_call(
        functools.partial(attend_kernel, places // experts, first, cores, len(after)),
        in_specs=[smem, smem, smem, vmem] + [hbm] * (5 + len(after)),
        out_specs=[vmem] * (len(pieces) + 1),
        out_shape=pieces + [jax.ShapeDtypeStruct(MARK, jnp.float32)],
        scratch_shapes=[
            pltpu.VMEM((slots, heads * dim), jnp.bfloat16),
            pltpu.VMEM((heads, dim, latent), jnp.bfloat16),
            pltpu.VMEM((heads, latent, dim), jnp.bfloat16),
            pltpu.VMEM((keys, latent), jnp.bfloat16),
            pltpu.VMEM((slots, keys), jnp.float32),
            pltpu.VMEM((places, slots), jnp.bfloat16),
            pltpu.VMEM((slots, heads * dim), jnp.bfloat16),
            pltpu.SemaphoreType.DMA((5,)),
        ],
        compiler_params=pltpu.CompilerParams(vmem_limit_bytes=VMEM if first else ALL_VMEM),
        cost_estimate=pl.CostEstimate(
            flops=4 * slots * heads * keys * latent,
            bytes_accessed=4 * heads * dim * latent,
            transcendentals=heads * slots * keys,
        ),
    )(me, count, size, routes.T, queries, key_weight, value_weight, prefix, fresh, *after)


def run_copies(copies):
    for copy in copies:
        copy.start()
    for copy in copies:
        copy.wait()


def join_kernel(*refs):
    *refs, sem = refs
    count = (len(refs) - 1) // 2
    copies = []
    for i, (kept_ref, out_ref) in enumerate(zip(refs[:count], refs[count + 1 :])):
        rows = kept_ref.shape[0]
        swapped = refs[count].at[pl.ds((i + 1) * rows, rows)]
        copies += [
            pltpu.make_async_copy(kept_ref, out_ref.at[pl.ds(0, rows)], sem.at[2 * i]),
            pltpu.make_async_copy(swapped, out_ref.at[pl.ds(rows, rows)], sem.at[2 * i + 1]),
        ]
    run_copies(copies)


def join(kept, swapped):
    rows, width = kept[0].shape
    return pl.pallas_call(
        join_kernel,
        in_specs=[pl.BlockSpec(memory_space=pl.ANY)] * (len(kept) + 1),
        out_specs=[pl.BlockSpec(memory_space=pltpu.VMEM)] * len(kept),
        out_shape=[jax.ShapeDtypeStruct((2 * rows, width), jnp.bfloat16)] * len(kept),
        scratch_shapes=[pltpu.SemaphoreType.DMA((2 * len(kept),))],
        compiler_params=pltpu.CompilerParams(vmem_limit_bytes=VMEM),
        cost_estimate=SHORT,
    )(*kept, swapped)


def place_kernel(plan, cores, me_ref, *refs):
    out_ref, sem = refs[-2:]
    _, _, capacity, features = out_ref.shape
    features //= cores
    me = me_ref[0]
    copies = []
    for ref, row, start, bits, apart in plan:
        ref = refs[ref]
        who = me ^ bits if apart else jnp.int32(bits)
        left = pl.multiple_of(who % cores * features + start, math.gcd(features, start))
        target = out_ref.at[0, who // cores, :, pl.ds(left, ref.shape[1])]
        copies.append(
            pltpu.make_async_copy(ref.at[pl.ds(row, capacity)], target, sem.at[len(copies)])
        )
    run_copies(copies)


def place(me, arrays, plan, cores, shape, placed):
    anywhere = pl.BlockSpec(memory_space=pl.ANY)
    operands = [me, *arrays, *placed]
    return pl.pallas_call(
        functools.partial(place_kernel, plan, cores),
        in_specs=[pl.BlockSpec(memory_space=pltpu.SMEM)]
        + [pl.BlockSpec(memory_space=pltpu.VMEM)] * len(arrays)
        + [anywhere] * len(placed),
        out_specs=anywhere,
        out_shape=jax.ShapeDtypeStruct(shape, jnp.bfloat16),
        scratch_shapes=[pltpu.SemaphoreType.DMA((len(plan),))],
        input_output_aliases={len(operands) - 1: 0} if placed else {},
        compiler_params=pltpu.CompilerParams(vmem_limit_bytes=VMEM),
    )(*operands)


def exchange_order(ranks):
    near, far = list(range(1, ranks // 2)), list(range(ranks // 2, ranks))
    return near[:-1] + far[::2] + far[1::2] + near[-1:]


def local(
    queries,
    key_weight,
    value_weight,
    prefix_latent,
    fresh_latent,
    span_counts,
    prefix_lengths,
    routes,
):
    ranks, cores = lax.axis_size("dp"), lax.axis_size("ep")
    experts = ranks * cores
    slots = queries.shape[0]
    heads, dim, _ = key_weight.shape
    capacity = slots * routes.shape[1] // experts
    direct = ranks <= DIRECT and capacity % 16 == 0
    me = (lax.axis_index("dp") * cores + lax.axis_index("ep")).astype(jnp.int32).reshape(1)
    nobody = jnp.zeros((1,), jnp.int32)
    shares = [heads * share // sum(CHUNKS) for share in CHUNKS]

    def run(chunk, order, parts, cores, after):
        return attend(
            sum(shares[:chunk]),
            shares[chunk],
            order,
            queries,
            key_weight,
            value_weight,
            prefix_latent,
            fresh_latent,
            span_counts,
            prefix_lengths,
            routes,
            experts,
            parts,
            cores,
            after,
        )

    def to_all(outgoing):
        return lax.all_to_all(
            outgoing.reshape(experts, capacity, -1),
            ("dp", "ep"),
            split_axis=0,
            concat_axis=0,
            tiled=True,
        )

    if not direct:
        outgoing = [run(chunk, nobody, [experts * capacity], 1, [])[0] for chunk in range(len(shares))]
        arrived = jnp.concatenate([to_all(rows) for rows in outgoing], axis=2)
        arrived = arrived.reshape(ranks, cores, capacity, -1).transpose(0, 2, 1, 3)
        return arrived.reshape(1, ranks, capacity, cores * heads * dim)
    opening, mark = run(0, nobody, [experts * capacity], 1, [])
    first = to_all(opening).reshape(experts * capacity, -1)
    parts = [capacity] * ranks + [(cores - 1) * ranks * capacity]
    *kept, message, mark = run(1, me, parts, cores, [mark])
    swapped = lax.ppermute(message, "ep", [(i, i ^ 1) for i in range(cores)])
    order = exchange_order(ranks)
    joined = dict(zip(range(1, ranks), join(kept[1:], swapped)))
    middle = shares[0] * dim
    soon, late = [first, kept[0], swapped], []
    soon_plan = [(0, i * capacity, 0, i, False) for i in range(experts)]
    soon_plan += [(1, 0, middle, 0, True), (2, 0, middle, 1, True)]
    late_plan = []
    for j in order:
        piece = lax.ppermute(joined[j], "dp", [(i, i ^ j) for i in range(ranks)])
        late_plan.append((len(late), 0, middle, j * cores, True))
        late_plan.append((len(late), capacity, middle, j * cores + 1, True))
        late.append(piece)
    shape = (1, ranks, capacity, cores * heads * dim)
    placed = place(me, soon, soon_plan, cores, shape, [])
    return place(me, late, late_plan, cores, shape, [placed])


def solution(mesh):
    in_specs = (
        P(("groups", "dp"), "ep"),
        P("ep", None, None),
        P("ep", None, None),
        P(("groups", "dp"), None),
        P(("groups", "dp"), None),
        P(("groups", "dp")),
        P(("groups", "dp")),
        P(("groups", "dp"), None),
    )
    out_specs = P(("groups", "dp", "ep"), None, None, None)
    return jax.shard_map(local, mesh=mesh, in_specs=in_specs, out_specs=out_specs, check_vma=False)
```

```python
import functools
import math

import jax
import jax.numpy as jnp
from jax import lax
from jax.experimental import pallas as pl
from jax.experimental.pallas import tpu as pltpu
from jax.sharding import PartitionSpec as P

SPAN = 64
STACK = 4
CHUNKS = (15, 17)
DIRECT = 16
ALL_VMEM = 63_400_000
VMEM = 51 * 1024 * 1024
SHORT = pl.CostEstimate(flops=0, bytes_accessed=0, transcendentals=0)
MARK = (8, 128)
MASKED = -1e30
OPEN = 3e38
NT = (((1,), (1,)), ((), ()))


def dot(left, right):
    return jnp.dot(left, right, preferred_element_type=jnp.float32)


def build_table(me, count, routes_ref, table_ref, capacity, cores):
    slots = routes_ref.shape[1]
    rows = table_ref.shape[0]
    place = lax.broadcasted_iota(jnp.int32, (rows, slots), 0)
    token = lax.broadcasted_iota(jnp.int32, (rows, slots), 1)
    block = place // capacity
    chips = rows // (capacity * cores)
    expert = ((block % chips) * cores + block // chips) ^ me
    hit = ((routes_ref[0:1, :] == expert) | (routes_ref[1:2, :] == expert)) & (
        token < count * SPAN
    )
    hit = jnp.where(hit, jnp.float32(1.0), jnp.float32(0.0))
    first = lax.broadcasted_iota(jnp.int32, (slots, slots), 0)
    second = lax.broadcasted_iota(jnp.int32, (slots, slots), 1)
    earlier = jnp.where(first < second, jnp.float32(1.0), jnp.float32(0.0))
    before = dot(hit.astype(jnp.bfloat16), earlier.astype(jnp.bfloat16))
    wanted = (place - block * capacity).astype(jnp.float32)
    table_ref[...] = jnp.where(before == wanted, hit, jnp.float32(0.0)).astype(jnp.bfloat16)


def attend_kernel(
    capacity,
    first,
    cores,
    after,
    me_ref,
    count_ref,
    size_ref,
    routes_ref,
    queries_hbm,
    key_weight_hbm,
    value_weight_hbm,
    prefix_hbm,
    fresh_hbm,
    *rest,
):
    *out_refs, mark_ref, queries_ref, key_weight_ref, value_weight_ref, keys_ref = rest[after:-4]
    mark_ref[...] = jnp.zeros_like(mark_ref)
    cap_ref, table_ref, attended_ref, sem = rest[-4:]
    slots = queries_ref.shape[0]
    past = prefix_hbm.shape[0]
    heads, dim, _ = key_weight_ref.shape
    here = pl.ds(first, heads)
    here = pl.ds(first, heads)
    copies = [
        pltpu.make_async_copy(
            queries_hbm.at[:, pl.ds(first * dim, heads * dim)], queries_ref, sem.at[0]
        ),
        pltpu.make_async_copy(key_weight_hbm.at[here], key_weight_ref, sem.at[1]),
        pltpu.make_async_copy(prefix_hbm, keys_ref.at[pl.ds(0, past)], sem.at[2]),
        pltpu.make_async_copy(fresh_hbm, keys_ref.at[pl.ds(past, slots)], sem.at[3]),
        pltpu.make_async_copy(value_weight_hbm.at[here], value_weight_ref, sem.at[4]),
    ]
    for copy in copies:
        copy.start()
    count, size = count_ref[0], size_ref[0]
    lane = lax.broadcasted_iota(jnp.int32, (slots, past), 1)
    cap_ref[:, :past] = jnp.where(lane < size, jnp.float32(OPEN), jnp.float32(MASKED))
    row = lax.broadcasted_iota(jnp.int32, (slots, slots), 0)
    col = lax.broadcasted_iota(jnp.int32, (slots, slots), 1)
    cap_ref[:, past:] = jnp.where(
        (col <= row) & (col < count * SPAN), jnp.float32(OPEN), jnp.float32(MASKED)
    )
    build_table(me_ref[0], count, routes_ref, table_ref, capacity, cores)
    for copy in copies:
        copy.wait()

    scale = math.log2(math.e) / math.sqrt(dim)
    keys = keys_ref[...]
    stacks = [range(h, min(h + STACK, heads)) for h in range(0, heads, STACK)]
    scores = []
    for stack in stacks:
        lifted = []
        for h in stack:
            one = dot(queries_ref[:, h * dim : (h + 1) * dim], key_weight_ref[h])
            lifted.append(one.astype(jnp.bfloat16))
        lifted = jnp.concatenate(lifted, axis=0)
        scores.append(lax.dot_general(lifted, keys, NT, preferred_element_type=jnp.float32))
    for stack, score in zip(stacks, scores):
        score = score.reshape(len(stack), slots, keys.shape[0])
        score = jnp.minimum(score, cap_ref[...][None])
        highest = jnp.max(score, axis=-1, keepdims=True) * scale
        weights = jnp.exp2(score * scale - highest)
        total = jnp.sum(weights, axis=-1, keepdims=True)
        weights = weights.astype(jnp.bfloat16).reshape(len(stack) * slots, keys.shape[0])
        mixed = dot(weights, keys).astype(jnp.bfloat16)
        for g, h in enumerate(stack):
            projected = dot(mixed[g * slots : (g + 1) * slots], value_weight_ref[h])
            attended_ref[:, h * dim : (h + 1) * dim] = (projected / total[g]).astype(jnp.bfloat16)
    grouped = dot(table_ref[...], attended_ref[...]).astype(jnp.bfloat16)
    row = 0
    for out_ref in out_refs:
        out_ref[...] = grouped[row : row + out_ref.shape[0]]
        row += out_ref.shape[0]


def attend(
    first,
    heads,
    me,
    queries,
    key_weight,
    value_weight,
    prefix,
    fresh,
    count,
    size,
    routes,
    experts,
    parts,
    cores,
    after,
):
    slots = queries.shape[0]
    _, dim, latent = key_weight.shape
    places = slots * routes.shape[1]
    keys = prefix.shape[0] + slots
    smem = pl.BlockSpec(memory_space=pltpu.SMEM)
    vmem = pl.BlockSpec(memory_space=pltpu.VMEM)
    hbm = pl.BlockSpec(memory_space=pltpu.HBM)
    pieces = [jax.ShapeDtypeStruct((rows, heads * dim), jnp.bfloat16) for rows in parts]
    return pl.pallas_call(
        functools.partial(attend_kernel, places // experts, first, cores, len(after)),
        in_specs=[smem, smem, smem, vmem] + [hbm] * (5 + len(after)),
        out_specs=[vmem] * (len(pieces) + 1),
        out_shape=pieces + [jax.ShapeDtypeStruct(MARK, jnp.float32)],
        scratch_shapes=[
            pltpu.VMEM((slots, heads * dim), jnp.bfloat16),
            pltpu.VMEM((heads, dim, latent), jnp.bfloat16),
            pltpu.VMEM((heads, latent, dim), jnp.bfloat16),
            pltpu.VMEM((keys, latent), jnp.bfloat16),
            pltpu.VMEM((slots, keys), jnp.float32),
            pltpu.VMEM((places, slots), jnp.bfloat16),
            pltpu.VMEM((slots, heads * dim), jnp.bfloat16),
            pltpu.SemaphoreType.DMA((5,)),
        ],
        compiler_params=pltpu.CompilerParams(vmem_limit_bytes=VMEM if first else ALL_VMEM),
        cost_estimate=pl.CostEstimate(
            flops=4 * slots * heads * keys * latent,
            bytes_accessed=4 * heads * dim * latent,
            transcendentals=heads * slots * keys,
        ),
    )(me, count, size, routes.T, queries, key_weight, value_weight, prefix, fresh, *after)


def run_copies(copies):
    for copy in copies:
        copy.start()
    for copy in copies:
        copy.wait()


def join_kernel(*refs):
    *refs, sem = refs
    count = (len(refs) - 1) // 2
    copies = []
    for i, (kept_ref, out_ref) in enumerate(zip(refs[:count], refs[count + 1 :])):
        rows = kept_ref.shape[0]
        swapped = refs[count].at[pl.ds((i + 1) * rows, rows)]
        copies += [
            pltpu.make_async_copy(kept_ref, out_ref.at[pl.ds(0, rows)], sem.at[2 * i]),
            pltpu.make_async_copy(swapped, out_ref.at[pl.ds(rows, rows)], sem.at[2 * i + 1]),
        ]
    run_copies(copies)


def join(kept, swapped):
    rows, width = kept[0].shape
    return pl.pallas_call(
        join_kernel,
        in_specs=[pl.BlockSpec(memory_space=pl.ANY)] * (len(kept) + 1),
        out_specs=[pl.BlockSpec(memory_space=pltpu.VMEM)] * len(kept),
        out_shape=[jax.ShapeDtypeStruct((2 * rows, width), jnp.bfloat16)] * len(kept),
        scratch_shapes=[pltpu.SemaphoreType.DMA((2 * len(kept),))],
        compiler_params=pltpu.CompilerParams(vmem_limit_bytes=VMEM),
        cost_estimate=SHORT,
    )(*kept, swapped)


def place_kernel(plan, cores, me_ref, *refs):
    out_ref, sem = refs[-2:]
    _, _, capacity, features = out_ref.shape
    features //= cores
    me = me_ref[0]
    copies = []
    for ref, row, start, bits, apart in plan:
        ref = refs[ref]
        who = me ^ bits if apart else jnp.int32(bits)
        left = pl.multiple_of(who % cores * features + start, math.gcd(features, start))
        target = out_ref.at[0, who // cores, :, pl.ds(left, ref.shape[1])]
        copies.append(
            pltpu.make_async_copy(ref.at[pl.ds(row, capacity)], target, sem.at[len(copies)])
        )
    run_copies(copies)


def place(me, arrays, plan, cores, shape, placed):
    anywhere = pl.BlockSpec(memory_space=pl.ANY)
    operands = [me, *arrays, *placed]
    return pl.pallas_call(
        functools.partial(place_kernel, plan, cores),
        in_specs=[pl.BlockSpec(memory_space=pltpu.SMEM)]
        + [pl.BlockSpec(memory_space=pltpu.VMEM)] * len(arrays)
        + [anywhere] * len(placed),
        out_specs=anywhere,
        out_shape=jax.ShapeDtypeStruct(shape, jnp.bfloat16),
        scratch_shapes=[pltpu.SemaphoreType.DMA((len(plan),))],
        input_output_aliases={len(operands) - 1: 0} if placed else {},
        compiler_params=pltpu.CompilerParams(vmem_limit_bytes=VMEM),
    )(*operands)


def exchange_order(ranks):
    near, far = list(range(1, ranks // 2)), list(range(ranks // 2, ranks))
    return near[:-1] + far[::2] + far[1::2] + near[-1:]


def local(
    queries,
    key_weight,
    value_weight,
    prefix_latent,
    fresh_latent,
    span_counts,
    prefix_lengths,
    routes,
):
    ranks, cores = lax.axis_size("dp"), lax.axis_size("ep")
    experts = ranks * cores
    slots = queries.shape[0]
    heads, dim, _ = key_weight.shape
    capacity = slots * routes.shape[1] // experts
    direct = ranks <= DIRECT and capacity % 16 == 0
    me = (lax.axis_index("dp") * cores + lax.axis_index("ep")).astype(jnp.int32).reshape(1)
    nobody = jnp.zeros((1,), jnp.int32)
    shares = [heads * share // sum(CHUNKS) for share in CHUNKS]

    def run(chunk, order, parts, cores, after):
        return attend(
            sum(shares[:chunk]),
            shares[chunk],
            order,
            queries,
            key_weight,
            value_weight,
            prefix_latent,
            fresh_latent,
            span_counts,
            prefix_lengths,
            routes,
            experts,
            parts,
            cores,
            after,
        )

    def to_all(outgoing):
        return lax.all_to_all(
            outgoing.reshape(experts, capacity, -1),
            ("dp", "ep"),
            split_axis=0,
            concat_axis=0,
            tiled=True,
        )

    if not direct:
        outgoing = [run(chunk, nobody, [experts * capacity], 1, [])[0] for chunk in range(len(shares))]
        arrived = jnp.concatenate([to_all(rows) for rows in outgoing], axis=2)
        arrived = arrived.reshape(ranks, cores, capacity, -1).transpose(0, 2, 1, 3)
        return arrived.reshape(1, ranks, capacity, cores * heads * dim)
    opening, mark = run(0, nobody, [experts * capacity], 1, [])
    first = to_all(opening).reshape(experts * capacity, -1)
    parts = [capacity] * ranks + [(cores - 1) * ranks * capacity]
    *kept, message, mark = run(1, me, parts, cores, [mark])
    swapped = lax.ppermute(message, "ep", [(i, i ^ 1) for i in range(cores)])
    order = exchange_order(ranks)
    joined = dict(zip(range(1, ranks), join(kept[1:], swapped)))
    middle = shares[0] * dim
    soon, late = [first, kept[0], swapped], []
    soon_plan = [(0, i * capacity, 0, i, False) for i in range(experts)]
    soon_plan += [(1, 0, middle, 0, True), (2, 0, middle, 1, True)]
    late_plan = []
    for j in order:
        piece = lax.ppermute(joined[j], "dp", [(i, i ^ j) for i in range(ranks)])
        late_plan.append((len(late), 0, middle, j * cores, True))
        late_plan.append((len(late), capacity, middle, j * cores + 1, True))
        late.append(piece)
    shape = (1, ranks, capacity, cores * heads * dim)
    placed = place(me, soon, soon_plan, cores, shape, [])
    return place(me, late, late_plan, cores, shape, [placed])


def solution(mesh):
    in_specs = (
        P(("groups", "dp"), "ep"),
        P("ep", None, None),
        P("ep", None, None),
        P(("groups", "dp"), None),
        P(("groups", "dp"), None),
        P(("groups", "dp")),
        P(("groups", "dp")),
        P(("groups", "dp"), None),
    )
    out_specs = P(("groups", "dp", "ep"), None, None, None)
    return jax.shard_map(local, mesh=mesh, in_specs=in_specs, out_specs=out_specs, check_vma=False)
```
